32 devices in a mesh: blk: 8 (over z, y), dp: 4 (over x, core).
Axes of the slice: x: 2, y: 2, z: 4, core: 2. Of those that a mesh axis runs over, the one named last changes fastest.
Arguments:
- visual_rows: bfloat16 [4, 256, 4096], P('dp', 'blk'), may hold values from -6 to 6
- value_matrix: bfloat16 [4, 256, 512], P('dp', 'blk'), may hold values from -6 to 6
- key_weight: bfloat16 [4096, 512], replicated, may hold values from -1 to 1
- queries: bfloat16 [4, 1024, 4096], P('dp', 'blk'), may hold values from -1024 to 1024
- output_gradient: bfloat16 [4, 1024, 4096], P('dp', 'blk'), may hold values from -6 to 6
- visual_len: int32 [4], P('dp'), may hold values from 128 to 256, as said below
- frame_end: int32 [4, 8], P('dp'), may hold values from 1 to 2, as said below
Outputs:
- attn_out: bfloat16 [4, 1024, 4096], P('dp', 'blk')
- query_grad: bfloat16 [4, 1024, 4096], P('dp', 'blk')
- value_grad: bfloat16 [4, 256, 512], P('dp', 'blk')
- key_weight_grad: float32 [4096, 512], P(('blk', 'dp'))
The draws below stay inside these ranges and needn't reach their ends.
Inputs may be any that keep to these rules, and one draw needn't show every extreme that they name: `visual_len`: rows 0 to the count minus one of a sample are live; some sample has 256, another 128. `frame_end`: never falling along the text blocks of a sample, 1 for its first block and 2 for its last.
All inputs are finite; a program needn't handle non-finite values.
Results may differ from the reference program's by a relative error of at most 0.02.
Values may be sent and summed in bfloat16 or wider, within the bound.
No kernel may reach another device: no remote copies, remote signals or barrier semaphores. Data moves between devices by JAX's collectives and lax.ppermute only.
A program may use at most 128 MiB of HBM per device.

```python
import math
import jax
import jax.numpy as jnp
from jax import lax

HQ = 32
KEY_HEADS = 4
HEAD_SIZE = 128
VISUAL_FEATURES = 4096
TILE = 128
HEADS_PER_KEY = 8
SAMPLE_COUNT = 4
TEXT_ROWS = 1024
VISUAL_ROWS = 256


def special_rows(key):
    drawn_sample = jax.random.normal(jax.random.fold_in(key, 101), (SAMPLE_COUNT, 2, VISUAL_FEATURES), jnp.float32)
    return jnp.clip(drawn_sample, -6.0, 6.0)


def key_matrix(key):
    drawn_sample = jax.random.normal(jax.random.fold_in(key, 102), (VISUAL_FEATURES, KEY_HEADS * HEAD_SIZE), jnp.float32)
    return jnp.clip(drawn_sample, -6.0, 6.0) / math.sqrt(VISUAL_FEATURES)


def draw_key_weight(key, part):
    return key_matrix(key).astype(jnp.bfloat16)


def draw_visual_rows(key, part):
    bulk = jnp.clip(jax.random.normal(jax.random.fold_in(key, 104), (SAMPLE_COUNT, VISUAL_ROWS, VISUAL_FEATURES), jnp.float32), -6.0, 6.0)
    bulk = bulk.at[:, 0:2, :].set(special_rows(key))
    return bulk.astype(jnp.bfloat16)


def draw_queries(key, part):
    base = 2.5 * jnp.clip(jax.random.normal(jax.random.fold_in(key, 106), (SAMPLE_COUNT, TEXT_ROWS, HQ * HEAD_SIZE), jnp.float32), -6.0, 6.0)
    return base.astype(jnp.bfloat16)


def draw_visual_len(key, part):
    lengths = jax.random.randint(jax.random.fold_in(key, 111), (SAMPLE_COUNT,), TILE, VISUAL_ROWS + 1)
    longest = jax.random.randint(jax.random.fold_in(key, 112), (), 0, SAMPLE_COUNT)
    shortest = (longest + jax.random.randint(jax.random.fold_in(key, 113), (), 1, SAMPLE_COUNT)) % SAMPLE_COUNT
    return lengths.at[longest].set(VISUAL_ROWS).at[shortest].set(TILE).astype(jnp.int32)


def draw_frame_end(key, part):
    steps_up = jax.random.randint(jax.random.fold_in(key, 121), (SAMPLE_COUNT, TEXT_ROWS // TILE), 1, 4)
    climb = jnp.cumsum(steps_up, axis=1)
    climb = climb - climb[:, :1]
    highest = climb[:, -1:]
    return (1 + climb * (VISUAL_ROWS // TILE - 1) // highest).astype(jnp.int32)


def block_levels(key, shape, pieces, smallest, largest):
    def one(axis_at, shards_of):
        steps = jax.random.uniform(jax.random.fold_in(jax.random.fold_in(key, 6), axis_at), (shards_of,), jnp.float32, smallest / len(pieces), largest / len(pieces))
        return jnp.repeat(jnp.exp(steps), shape[axis_at] // shards_of).reshape((-1,) + (1,) * (len(shape) - axis_at - 1))

    level = one(*pieces[0])
    for cut in pieces[1:]:
        level = level * one(*cut)
    return level


def scatter_about(key, shape, spread, bound, pieces=(), held_as=jnp.bfloat16):
    entries = spread * jax.random.normal(key, shape, jnp.float32)
    if pieces:
        entries = entries * block_levels(key, shape, pieces, -0.22, 0.18)
    return jnp.clip(entries, -bound, bound).astype(held_as)


def setup_inputs(seed: int = 0) -> dict:
    key_of = jax.random.split(jax.random.key(seed), 8)
    visual_rows = draw_visual_rows(jax.random.fold_in(key_of[7], 71), 0)
    value_matrix = scatter_about(key_of[1], (SAMPLE_COUNT, VISUAL_ROWS, KEY_HEADS * HEAD_SIZE), 1.0, 6.0, ((0, 4), (1, 8)))
    key_weight = draw_key_weight(jax.random.fold_in(key_of[7], 71), 0)
    queries = draw_queries(jax.random.fold_in(key_of[7], 71), 0)
    output_gradient = scatter_about(key_of[4], (SAMPLE_COUNT, TEXT_ROWS, HQ * HEAD_SIZE), 1.0, 6.0, ((0, 4), (1, 8)))
    visual_len = draw_visual_len(jax.random.fold_in(key_of[7], 71), 0)
    frame_end = draw_frame_end(jax.random.fold_in(key_of[7], 71), 0)
    return dict(visual_rows=visual_rows, value_matrix=value_matrix, key_weight=key_weight, queries=queries, output_gradient=output_gradient, visual_len=visual_len, frame_end=frame_end)


NEGATIVE_FILLER = -1.0e30


def one_sample(visual, value_single, key_weight, query_single, gradient_single, length, frames):
    head_span_width = KEY_HEADS * HEAD_SIZE
    scale = HEAD_SIZE ** -0.5
    key_rows = jnp.dot(visual, key_weight, preferred_element_type=jnp.float32).astype(jnp.bfloat16)
    limits = jnp.minimum(length, TILE * jnp.repeat(frames, TILE, total_repeat_length=TEXT_ROWS))
    live_mask = jnp.arange(VISUAL_ROWS, dtype=jnp.int32)[None, :] < limits[:, None]
    query_matrix = query_single.reshape(TEXT_ROWS, KEY_HEADS, HEADS_PER_KEY, HEAD_SIZE).astype(jnp.float32)
    gradient_rows = gradient_single.reshape(TEXT_ROWS, KEY_HEADS, HEADS_PER_KEY, HEAD_SIZE).astype(jnp.float32)
    key_portion = key_rows.reshape(VISUAL_ROWS, KEY_HEADS, HEAD_SIZE).astype(jnp.float32)
    value_portion = value_single.reshape(VISUAL_ROWS, KEY_HEADS, HEAD_SIZE).astype(jnp.float32)
    scores = jnp.einsum("tkgd,rkd->kgtr", query_matrix, key_portion) * scale
    scores = jnp.where(live_mask, scores, NEGATIVE_FILLER)
    row_peak = jnp.max(scores, axis=3, keepdims=True)
    shifted = jnp.where(live_mask, jnp.exp(scores - row_peak), 0.0)
    probs = shifted / jnp.sum(shifted, axis=3, keepdims=True)
    weights = lax.optimization_barrier(probs.astype(jnp.bfloat16)).astype(jnp.float32)
    attn_out = jnp.einsum("kgtr,rkd->tkgd", weights, value_portion).astype(jnp.bfloat16)
    out_wide = lax.optimization_barrier(attn_out).astype(jnp.float32)
    grad_delta = jnp.einsum("tkgd,tkgd->kgt", gradient_rows, out_wide)
    dprobs = jnp.einsum("tkgd,rkd->kgtr", gradient_rows, value_portion)
    dscores = (probs * (dprobs - grad_delta[..., None]) * scale).astype(jnp.bfloat16)
    dscores = lax.optimization_barrier(dscores).astype(jnp.float32)
    query_grad = jnp.einsum("kgtr,rkd->tkgd", dscores, key_portion).astype(jnp.bfloat16)
    key_grad = jnp.einsum("kgtr,tkgd->rkd", dscores, query_matrix).astype(jnp.bfloat16)
    value_grad = jnp.einsum("kgtr,tkgd->rkd", weights, gradient_rows).astype(jnp.bfloat16)
    weight_term = jnp.dot(visual.T, key_grad.reshape(VISUAL_ROWS, head_span_width), preferred_element_type=jnp.float32)
    return (attn_out.reshape(TEXT_ROWS, HQ * HEAD_SIZE), query_grad.reshape(TEXT_ROWS, HQ * HEAD_SIZE),
            value_grad.reshape(VISUAL_ROWS, head_span_width), weight_term)


def reference(visual_rows, value_matrix, key_weight, queries, output_gradient, visual_len, frame_end):
    def per_sample(total_grad, sample_slices):
        visual, value_single, query_single, gradient_single, length, frames = sample_slices
        attn_out, query_grad, value_grad, weight_term = one_sample(
            visual, value_single, key_weight, query_single, gradient_single, length, frames)
        return total_grad + weight_term, (attn_out, query_grad, value_grad)

    gradient_begin = jnp.zeros((VISUAL_FEATURES, KEY_HEADS * HEAD_SIZE), jnp.float32)
    weight_grad, (attn_out, query_grad, value_grad) = lax.scan(
        per_sample, gradient_begin, (visual_rows, value_matrix, queries, output_gradient, visual_len, frame_end))
    return attn_out, query_grad, value_grad, weight_grad
```

```python
import functools

import jax
import jax.numpy as jnp
from jax import lax
from jax.experimental import pallas as pl
from jax.experimental.pallas import tpu as pltpu
from jax.sharding import PartitionSpec as P

KEY_HEADS = 4
HEAD_SIZE = 128
TILE = 128
HEADS_PER_KEY = 8
LOG2_E = 1.4426950408889634
NEGATIVE_FILLER = -1e30
F32 = jnp.float32
BF16 = jnp.bfloat16


def dot(a, b, contract=((1,), (0,))):
    return lax.dot_general(a, b, (contract, ((), ())), preferred_element_type=F32)


def swap(x, axis, mask):
    size = lax.axis_size(axis)
    return lax.ppermute(x, axis, [(i, i ^ mask) for i in range(size)])


def attention_kernel(pieces, limit_ref, source_ref, q_ref, g_ref, *refs):
    k_refs, v_refs = refs[:pieces], refs[pieces : 2 * pieces]
    o_ref, qg_ref = refs[2 * pieces : 2 * pieces + 2]
    outs = refs[2 * pieces + 2 :]
    kg_refs, vg_refs = outs[:pieces], outs[pieces : 2 * pieces]
    w_all, ds_all, kg_acc, vg_acc = outs[2 * pieces :]
    j, i = pl.program_id(0), pl.program_id(1)
    columns = pl.ds(pl.multiple_of(j * HEAD_SIZE, HEAD_SIZE), HEAD_SIZE)
    keys = jnp.concatenate([r[:, columns] for r in k_refs], axis=0)
    values = jnp.concatenate([r[:, columns] for r in v_refs], axis=0)
    keys_t, values_t = keys.T, values.T
    rows = k_refs[0].shape[0]
    row = lax.broadcasted_iota(jnp.int32, (rows, TILE), 0)
    limit = limit_ref[i]
    bias = jnp.concatenate(
        [
            jnp.where(row + source_ref[p] * rows < limit, 0.0, NEGATIVE_FILLER)
            for p in range(pieces)
        ],
        axis=0,
    )
    scale = HEAD_SIZE**-0.5
    q_stack, g_stack = [], []
    for h in range(HEADS_PER_KEY):
        span = slice(h * HEAD_SIZE, (h + 1) * HEAD_SIZE)
        q, g = q_ref[:, span], g_ref[:, span]
        q_stack.append(q)
        g_stack.append(g)
        raw = dot(keys, q, ((1,), (1,))) + bias
        dprobs = dot(values, g, ((1,), (1,)))
        peak = jnp.max(raw, axis=0, keepdims=True)
        shifted = jnp.exp2((raw - peak) * (scale * LOG2_E))
        probs = shifted * (1.0 / jnp.sum(shifted, axis=0, keepdims=True))
        weights = probs.astype(BF16)
        terms = probs * dprobs
        delta = jnp.sum(terms, axis=0, keepdims=True)
        dscores = ((terms - probs * delta) * scale).astype(BF16)
        w_all[:, span] = weights
        ds_all[:, span] = dscores
        o_ref[:, span] = dot(values_t, weights).T.astype(BF16)
        qg_ref[:, span] = dot(keys_t, dscores).T.astype(BF16)
    kg = dot(ds_all[...], jnp.concatenate(q_stack, axis=0))
    vg = dot(w_all[...], jnp.concatenate(g_stack, axis=0))

    @pl.when(i == 0)
    def _():
        kg_acc[...] = kg
        vg_acc[...] = vg

    @pl.when(i > 0)
    def _():
        kg_acc[...] += kg
        vg_acc[...] += vg

    @pl.when(i == pl.num_programs(1) - 1)
    def _():
        for p in range(pieces):
            kg_refs[p][...] = kg_acc[p * rows : (p + 1) * rows, :].astype(BF16)
            vg_refs[p][...] = vg_acc[p * rows : (p + 1) * rows, :].astype(BF16)


def attention(limits, sources, queries, gradients, keys, values):
    pieces = len(keys)
    rows, width = keys[0].shape
    text = queries.shape[0]
    all_rows = pieces * rows
    span = HEADS_PER_KEY * HEAD_SIZE
    smem = pl.BlockSpec(memory_space=pltpu.SMEM)
    text_block = pl.BlockSpec((TILE, span), lambda j, i: (i, j))
    whole = pl.BlockSpec((rows, width), lambda j, i: (0, 0))
    head = pl.BlockSpec((rows, HEAD_SIZE), lambda j, i: (0, j))
    wide = jax.ShapeDtypeStruct(queries.shape, BF16)
    narrow = jax.ShapeDtypeStruct((rows, width), BF16)
    out = pl.pallas_call(
        functools.partial(attention_kernel, pieces),
        grid=(KEY_HEADS, text // TILE),
        in_specs=[smem, smem, text_block, text_block] + [whole] * (2 * pieces),
        out_specs=[text_block] * 2 + [head] * (2 * pieces),
        out_shape=[wide] * 2 + [narrow] * (2 * pieces),
        scratch_shapes=[
            pltpu.VMEM((all_rows, span), BF16),
            pltpu.VMEM((all_rows, span), BF16),
            pltpu.VMEM((all_rows, HEAD_SIZE), F32),
            pltpu.VMEM((all_rows, HEAD_SIZE), F32),
        ],
        cost_estimate=pl.CostEstimate(
            flops=12 * text * all_rows * KEY_HEADS * span,
            bytes_accessed=8 * text * KEY_HEADS * span,
            transcendentals=0,
        ),
        compiler_params=pltpu.CompilerParams(vmem_limit_bytes=40 * 1024 * 1024),
        name="attention",
    )(limits, sources, queries, gradients, *keys, *values)
    return out[0], out[1], out[2 : 2 + pieces], out[2 + pieces :]


def weight_kernel(pieces, source_ref, core_ref, visual_ref, *refs):
    kg_refs = refs[:pieces]
    own_ref, other_ref, kg_all = refs[pieces:]
    rows = kg_refs[0].shape[0]
    for p in range(pieces):
        start = pl.multiple_of(source_ref[p] * rows, rows)
        kg_all[pl.ds(start, rows), :] = kg_refs[p][...]
    total = dot(visual_ref[...], kg_all[...], ((0,), (0,)))
    half = total.shape[0] // 2
    first = core_ref[0] == 0
    own_ref[...] = jnp.where(first, total[:half], total[half:])
    other_ref[...] = jnp.where(first, total[half:], total[:half])


def weight_terms(sources, core, visual, key_grads):
    pieces = len(key_grads)
    rows, width = key_grads[0].shape
    vmem = pl.BlockSpec(memory_space=pltpu.VMEM)
    smem = pl.BlockSpec(memory_space=pltpu.SMEM)
    half = jax.ShapeDtypeStruct((visual.shape[1] // 2, width), F32)
    return pl.pallas_call(
        functools.partial(weight_kernel, pieces),
        in_specs=[smem, smem] + [vmem] * (1 + pieces),
        out_specs=[vmem] * 2,
        out_shape=[half] * 2,
        scratch_shapes=[pltpu.VMEM((pieces * rows, width), BF16)],
        compiler_params=pltpu.CompilerParams(vmem_limit_bytes=40 * 1024 * 1024),
        name="weight_terms",
    )(sources, core, visual, *key_grads)


def summed(pieces):
    total = pieces[0].astype(F32)
    for piece in pieces[1:]:
        total = total + piece.astype(F32)
    return total.astype(BF16)


def local(visual_rows, value_matrix, key_weight, queries, output_gradient, visual_len, frame_end):
    blocks, samples = lax.axis_size("blk"), lax.axis_size("dp")
    block, sample = lax.axis_index("blk"), lax.axis_index("dp")
    chips = samples // 2
    chip, core = sample // 2, sample % 2
    visual, value = visual_rows[0], value_matrix[0]
    rows, features = visual.shape
    text = queries.shape[1]
    masks = range(1, blocks)
    sources = jnp.stack([block ^ m for m in range(blocks)]).astype(jnp.int32)

    values = [value] + [swap(value, "blk", m) for m in masks]
    key = dot(visual, key_weight).astype(BF16)
    keys = [key] + [swap(key, "blk", m) for m in masks]

    width = features // (blocks * chips)
    spread = visual.reshape(rows, blocks, chips, width)

    def for_chip(m):
        part = lax.dynamic_index_in_dim(spread, chip ^ m, 2, keepdims=False)
        return part.reshape(rows, blocks * width)

    visual_parts = [for_chip(0)] + [swap(for_chip(m), "dp", 2 * m) for m in range(1, chips)]
    visual_columns = lax.all_to_all(
        jnp.concatenate(visual_parts, axis=0), "blk", split_axis=1, concat_axis=0, tiled=True
    )

    tiles = text // TILE
    frames = lax.dynamic_slice_in_dim(frame_end[0], block * tiles, tiles, 0)
    limits = jnp.minimum(visual_len[0], TILE * frames)
    attn_out, query_grad, key_terms, value_terms = attention(
        limits, sources, queries[0], output_gradient[0], keys, values
    )
    key_grad = summed([key_terms[0]] + [swap(key_terms[m], "blk", m) for m in masks])
    value_grad = summed([value_terms[0]] + [swap(value_terms[m], "blk", m) for m in masks])

    chip_grads = jnp.concatenate(
        [key_grad] + [swap(key_grad, "dp", 2 * m) for m in range(1, chips)], axis=0
    )
    key_grads = [chip_grads] + [swap(chip_grads, "blk", m) for m in masks]
    own, other = weight_terms(sources, core[None].astype(jnp.int32), visual_columns, key_grads)
    weight_grad = own + swap(other, "dp", 1)
    return attn_out[None], query_grad[None], value_grad[None], weight_grad


def solution(mesh):
    return jax.shard_map(
        local,
        mesh=mesh,
        in_specs=(
            P("dp", "blk", None),
            P("dp", "blk", None),
            P(),
            P("dp", "blk", None),
            P("dp", "blk", None),
            P("dp"),
            P("dp", None),
        ),
        out_specs=(
            P("dp", "blk", None),
            P("dp", "blk", None),
            P("dp", "blk", None),
            P(("blk", "dp"), None),
        ),
        check_vma=False,
    )
```

```python
import functools

import jax
import jax.numpy as jnp
from jax import lax
from jax.experimental import pallas as pl
from jax.experimental.pallas import tpu as pltpu
from jax.sharding import PartitionSpec as P

KEY_HEADS = 4
HEAD_SIZE = 128
TILE = 128
HEADS_PER_KEY = 8
LOG2_E = 1.4426950408889634
NEGATIVE_FILLER = -1e30
F32 = jnp.float32
BF16 = jnp.bfloat16


def dot(a, b, contract=((1,), (0,))):
    return lax.dot_general(a, b, (contract, ((), ())), preferred_element_type=F32)


def swap(x, axis, mask):
    size = lax.axis_size(axis)
    return lax.ppermute(x, axis, [(i, i ^ mask) for i in range(size)])


def project_kernel(blocks, chips, chip_ref, visual_ref, slab_ref, weight_ref, value_ref, *refs):
    copies_ref, spread_refs, acc_ref = refs[0], refs[1:-1], refs[-1]
    step = pl.program_id(0)
    part = dot(slab_ref[...], weight_ref[...])

    @pl.when(step == 0)
    def _():
        acc_ref[...] = part
        width = spread_refs[0].shape[2]
        for m in range(chips):
            chip = chip_ref[0] ^ m
            for b in range(blocks):
                if width % HEAD_SIZE == 0:
                    start = pl.multiple_of((b * chips + chip) * width, HEAD_SIZE)
                    spread_refs[m][b] = visual_ref[:, pl.ds(start, width)]
                else:
                    for c in range(chips):

                        @pl.when(chip == c)
                        def _(m=m, b=b, c=c):
                            start = (b * chips + c) * width
                            spread_refs[m][b] = visual_ref[:, start : start + width]

    @pl.when(step > 0)
    def _():
        acc_ref[...] += part

    @pl.when(step == pl.num_programs(0) - 1)
    def _():
        both = jnp.concatenate([acc_ref[...].astype(BF16), value_ref[...]], axis=1)
        for b in range(blocks):
            copies_ref[b] = both


def project(blocks, chips, chip, visual, key_weight, value):
    rows, features = visual.shape
    columns = key_weight.shape[1]
    width = features // (blocks * chips)
    steps = 8
    slab = features // steps
    smem = pl.BlockSpec(memory_space=pltpu.SMEM)

    def whole(shape):
        return pl.BlockSpec(shape, lambda k: (0,) * len(shape))

    copies = (blocks, rows, columns + value.shape[1])
    spread = (blocks, rows, width)
    out = pl.pallas_call(
        functools.partial(project_kernel, blocks, chips),
        grid=(steps,),
        in_specs=[
            smem,
            whole(visual.shape),
            pl.BlockSpec((rows, slab), lambda k: (0, k)),
            pl.BlockSpec((slab, columns), lambda k: (k, 0)),
            whole(value.shape),
        ],
        out_specs=[whole(copies)] + [whole(spread)] * chips,
        out_shape=[jax.ShapeDtypeStruct(copies, BF16)]
        + [jax.ShapeDtypeStruct(spread, BF16)] * chips,
        scratch_shapes=[pltpu.VMEM((rows, columns), F32)],
        cost_estimate=pl.CostEstimate(
            flops=2 * rows * features * columns,
            bytes_accessed=2 * features * columns,
            transcendentals=0,
        ),
        compiler_params=pltpu.CompilerParams(vmem_limit_bytes=32 * 1024 * 1024),
        name="project",
    )(chip, visual, visual, key_weight, value)
    return out[0], out[1:]


def attention_kernel(limit_ref, q_ref, g_ref, k_ref, v_ref, *refs):
    o_ref, qg_ref, kg_ref, vg_ref, w_all, ds_all, kg_acc, vg_acc = refs
    i = pl.program_id(1)
    keys, values = k_ref[...], v_ref[...]
    keys_t, values_t = keys.T, values.T
    pair = 2 * TILE
    row = lax.broadcasted_iota(jnp.int32, (keys.shape[0], pair), 0)
    bias = jnp.where(row < limit_ref[i], 0.0, NEGATIVE_FILLER)
    scale = HEAD_SIZE**-0.5
    q_stack, g_stack = [], []
    for h in range(0, HEADS_PER_KEY, 2):
        first = slice(h * HEAD_SIZE, (h + 1) * HEAD_SIZE)
        second = slice((h + 1) * HEAD_SIZE, (h + 2) * HEAD_SIZE)
        both = slice(h * HEAD_SIZE, (h + 2) * HEAD_SIZE)
        q = jnp.concatenate([q_ref[:, first], q_ref[:, second]], axis=0)
        g = jnp.concatenate([g_ref[:, first], g_ref[:, second]], axis=0)
        q_stack.append(q)
        g_stack.append(g)
        raw = dot(keys, q, ((1,), (1,))) + bias
        dprobs = dot(values, g, ((1,), (1,)))
        peak = jnp.max(raw, axis=0, keepdims=True)
        shifted = jnp.exp2((raw - peak) * (scale * LOG2_E))
        probs = shifted * (1.0 / jnp.sum(shifted, axis=0, keepdims=True))
        weights = probs.astype(BF16)
        terms = probs * dprobs
        delta = jnp.sum(terms, axis=0, keepdims=True)
        dscores = ((terms - probs * delta) * scale).astype(BF16)
        w_all[:, both] = weights
        ds_all[:, both] = dscores
        out = dot(values_t, weights).T.astype(BF16)
        o_ref[:, first] = out[:TILE]
        o_ref[:, second] = out[TILE:]
        grad = dot(keys_t, dscores).T.astype(BF16)
        qg_ref[:, first] = grad[:TILE]
        qg_ref[:, second] = grad[TILE:]
    kg = dot(ds_all[...], jnp.concatenate(q_stack, axis=0))
    vg = dot(w_all[...], jnp.concatenate(g_stack, axis=0))

    @pl.when(i == 0)
    def _():
        kg_acc[...] = kg
        vg_acc[...] = vg

    @pl.when(i > 0)
    def _():
        kg_acc[...] += kg
        vg_acc[...] += vg

    @pl.when(i == pl.num_programs(1) - 1)
    def _():
        kg_ref[...] = kg_acc[...].astype(BF16)
        vg_ref[...] = vg_acc[...].astype(BF16)


def attention(limits, queries, gradients, keys_values):
    all_rows = keys_values.shape[0]
    text = queries.shape[0]
    span = HEADS_PER_KEY * HEAD_SIZE
    smem = pl.BlockSpec(memory_space=pltpu.SMEM)
    text_block = pl.BlockSpec((TILE, span), lambda j, i: (i, j))
    key_block = pl.BlockSpec((all_rows, HEAD_SIZE), lambda j, i: (0, j))
    value_block = pl.BlockSpec((all_rows, HEAD_SIZE), lambda j, i: (0, KEY_HEADS + j))
    wide = jax.ShapeDtypeStruct(queries.shape, BF16)
    narrow = jax.ShapeDtypeStruct((all_rows, KEY_HEADS * HEAD_SIZE), BF16)
    return pl.pallas_call(
        attention_kernel,
        grid=(KEY_HEADS, text // TILE),
        in_specs=[smem, text_block, text_block, key_block, value_block],
        out_specs=[text_block, text_block, key_block, key_block],
        out_shape=[wide, wide, narrow, narrow],
        scratch_shapes=[
            pltpu.VMEM((all_rows, span), BF16),
            pltpu.VMEM((all_rows, span), BF16),
            pltpu.VMEM((all_rows, HEAD_SIZE), F32),
            pltpu.VMEM((all_rows, HEAD_SIZE), F32),
        ],
        cost_estimate=pl.CostEstimate(
            flops=12 * text * all_rows * KEY_HEADS * span,
            bytes_accessed=8 * text * KEY_HEADS * span,
            transcendentals=0,
        ),
        compiler_params=pltpu.CompilerParams(vmem_limit_bytes=40 * 1024 * 1024),
        name="attention",
    )(limits, queries, gradients, keys_values, keys_values)


def weight_kernel(core_ref, visual_ref, kg_ref, own_ref, other_ref):
    total = dot(visual_ref[...], kg_ref[...], ((0,), (0,)))
    half = total.shape[0] // 2
    first = core_ref[0] == 0
    own_ref[...] = jnp.where(first, total[:half], total[half:])
    other_ref[...] = jnp.where(first, total[half:], total[:half])


def weight_terms(core, visual, key_grads):
    vmem = pl.BlockSpec(memory_space=pltpu.VMEM)
    smem = pl.BlockSpec(memory_space=pltpu.SMEM)
    half = jax.ShapeDtypeStruct((visual.shape[1] // 2, key_grads.shape[1]), F32)
    return pl.pallas_call(
        weight_kernel,
        in_specs=[smem, vmem, vmem],
        out_specs=[vmem] * 2,
        out_shape=[half] * 2,
        compiler_params=pltpu.CompilerParams(vmem_limit_bytes=32 * 1024 * 1024),
        name="weight_terms",
    )(core, visual, key_grads)


def exchange(pieces):
    return lax.all_to_all(pieces, "blk", split_axis=0, concat_axis=0, tiled=True)


def reduced(terms, blocks):
    parts = exchange(terms.reshape(blocks, -1, terms.shape[1]))
    return jnp.sum(parts.astype(F32), axis=0).astype(BF16)


def local(visual_rows, value_matrix, key_weight, queries, output_gradient, visual_len, frame_end):
    blocks, samples = lax.axis_size("blk"), lax.axis_size("dp")
    block, sample = lax.axis_index("blk"), lax.axis_index("dp")
    chips = samples // 2
    chip = (sample // 2)[None].astype(jnp.int32)
    core = (sample % 2)[None].astype(jnp.int32)
    text = queries.shape[1]

    copies, spread = project(blocks, chips, chip, visual_rows[0], key_weight, value_matrix[0])
    keys_values = exchange(copies).reshape(-1, copies.shape[2])

    visual_parts = [spread[0]] + [swap(spread[m], "dp", 2 * m) for m in range(1, chips)]
    visual_columns = exchange(jnp.concatenate(visual_parts, axis=1))
    visual_columns = visual_columns.reshape(-1, visual_columns.shape[2])

    tiles = text // TILE
    frames = lax.dynamic_slice_in_dim(frame_end[0], block * tiles, tiles, 0)
    limits = jnp.minimum(visual_len[0], TILE * frames)
    attn_out, query_grad, key_terms, value_terms = attention(
        limits, queries[0], output_gradient[0], keys_values
    )
    key_grad = reduced(key_terms, blocks)
    value_grad = reduced(value_terms, blocks)

    chip_grads = jnp.concatenate(
        [key_grad] + [swap(key_grad, "dp", 2 * m) for m in range(1, chips)], axis=0
    )
    key_grads = exchange(jnp.broadcast_to(chip_grads[None], (blocks, *chip_grads.shape)))
    own, other = weight_terms(core, visual_columns, key_grads.reshape(-1, key_grad.shape[1]))
    weight_grad = own + swap(other, "dp", 1)
    return attn_out[None], query_grad[None], value_grad[None], weight_grad


def solution(mesh):
    return jax.shard_map(
        local,
        mesh=mesh,
        in_specs=(
            P("dp", "blk", None),
            P("dp", "blk", None),
            P(),
            P("dp", "blk", None),
            P("dp", "blk", None),
            P("dp"),
            P("dp", None),
        ),
        out_specs=(
            P("dp", "blk", None),
            P("dp", "blk", None),
            P("dp", "blk", None),
            P(("blk", "dp"), None),
        ),
        check_vma=False,
    )
```

```python
import functools

import jax
import jax.numpy as jnp
from jax import lax
from jax.experimental import pallas as pl
from jax.experimental.pallas import tpu as pltpu
from jax.sharding import PartitionSpec as P

KEY_HEADS = 4
HEAD_SIZE = 128
TILE = 128
HEADS_PER_KEY = 8
LOG2_E = 1.4426950408889634
NEGATIVE_FILLER = -1e30
F32 = jnp.float32
BF16 = jnp.bfloat16


def dot(a, b, contract=((1,), (0,))):
    return lax.dot_general(a, b, (contract, ((), ())), preferred_element_type=F32)


def spread_kernel(visual_ref, value_ref, out_ref):
    blocks = out_ref.shape[0]
    values = value_ref[...]
    start = values.shape[1]
    width = out_ref.shape[2] - start
    for b in range(blocks):
        out_ref[b, :, :start] = values
        out_ref[b, :, start:] = visual_ref[:, b * width : (b + 1) * width]


def spread(blocks, visual, value):
    rows, features = visual.shape
    vmem = pl.BlockSpec(memory_space=pltpu.VMEM)
    return pl.pallas_call(
        spread_kernel,
        in_specs=[vmem, vmem],
        out_specs=vmem,
        out_shape=jax.ShapeDtypeStruct(
            (blocks, rows, value.shape[1] + features // blocks), BF16
        ),
        name="spread",
    )(visual, value)


def project_kernel(visual_ref, weight_ref, copies_ref, acc_ref):
    step = pl.program_id(0)
    part = dot(visual_ref[...], weight_ref[...])

    @pl.when(step == 0)
    def _():
        acc_ref[...] = part

    @pl.when(step > 0)
    def _():
        acc_ref[...] += part

    @pl.when(step == pl.num_programs(0) - 1)
    def _():
        keys = acc_ref[...].astype(BF16)
        for b in range(copies_ref.shape[0]):
            copies_ref[b] = keys


def project(blocks, visual, key_weight):
    rows, features = visual.shape
    columns = key_weight.shape[1]
    steps = 8
    slab = features // steps
    return pl.pallas_call(
        project_kernel,
        grid=(steps,),
        in_specs=[
            pl.BlockSpec((rows, slab), lambda k: (0, k)),
            pl.BlockSpec((slab, columns), lambda k: (k, 0)),
        ],
        out_specs=pl.BlockSpec((blocks, rows, columns), lambda k: (0, 0, 0)),
        out_shape=jax.ShapeDtypeStruct((blocks, rows, columns), BF16),
        scratch_shapes=[pltpu.VMEM((rows, columns), F32)],
        cost_estimate=pl.CostEstimate(
            flops=2 * rows * features * columns,
            bytes_accessed=2 * features * columns,
            transcendentals=0,
        ),
        name="project",
    )(visual, key_weight)


def attention_kernel(length_ref, frame_ref, q_ref, g_ref, k_ref, v_ref, *refs):
    o_ref, qg_ref, kg_ref, vg_ref, w_all, ds_all, kg_acc, vg_acc = refs
    i = pl.program_id(1)
    tile = lax.axis_index("blk") * pl.num_programs(1) + i
    limit = jnp.minimum(length_ref[0], TILE * frame_ref[0, tile])
    keys, values = k_ref[...], v_ref[...]
    keys_t, values_t = keys.T, values.T
    pair = 2 * TILE
    row = lax.broadcasted_iota(jnp.int32, (keys.shape[0], pair), 0)
    bias = jnp.where(row < limit, 0.0, NEGATIVE_FILLER)
    scale = HEAD_SIZE**-0.5
    q_stack, g_stack = [], []
    for h in range(0, HEADS_PER_KEY, 2):
        first = slice(h * HEAD_SIZE, (h + 1) * HEAD_SIZE)
        second = slice((h + 1) * HEAD_SIZE, (h + 2) * HEAD_SIZE)
        both = slice(h * HEAD_SIZE, (h + 2) * HEAD_SIZE)
        q = jnp.concatenate([q_ref[:, first], q_ref[:, second]], axis=0)
        g = jnp.concatenate([g_ref[:, first], g_ref[:, second]], axis=0)
        q_stack.append(q)
        g_stack.append(g)
        raw = dot(keys, q, ((1,), (1,))) + bias
        dprobs = dot(values, g, ((1,), (1,)))
        peak = jnp.max(raw, axis=0, keepdims=True)
        shifted = jnp.exp2((raw - peak) * (scale * LOG2_E))
        probs = shifted * (1.0 / jnp.sum(shifted, axis=0, keepdims=True))
        weights = probs.astype(BF16)
        terms = probs * dprobs
        delta = jnp.sum(terms, axis=0, keepdims=True)
        dscores = ((terms - probs * delta) * scale).astype(BF16)
        w_all[:, both] = weights
        ds_all[:, both] = dscores
        out = dot(values_t, weights).T.astype(BF16)
        o_ref[:, first] = out[:TILE]
        o_ref[:, second] = out[TILE:]
        grad = dot(keys_t, dscores).T.astype(BF16)
        qg_ref[:, first] = grad[:TILE]
        qg_ref[:, second] = grad[TILE:]
    kg = dot(ds_all[...], jnp.concatenate(q_stack, axis=0))
    vg = dot(w_all[...], jnp.concatenate(g_stack, axis=0))

    @pl.when(i == 0)
    def _():
        kg_acc[...] = kg
        vg_acc[...] = vg

    @pl.when(i > 0)
    def _():
        kg_acc[...] += kg
        vg_acc[...] += vg

    @pl.when(i == pl.num_programs(1) - 1)
    def _():
        kg_ref[...] = kg_acc[...].astype(BF16)
        vg_ref[...] = vg_acc[...].astype(BF16)


def attention(length, frames, queries, gradients, keys, values):
    all_rows = keys.shape[0]
    text = queries.shape[0]
    span = HEADS_PER_KEY * HEAD_SIZE
    smem = pl.BlockSpec(memory_space=pltpu.SMEM)
    text_block = pl.BlockSpec((TILE, span), lambda j, i: (i, j))
    key_block = pl.BlockSpec((all_rows, HEAD_SIZE), lambda j, i: (0, j))
    wide = jax.ShapeDtypeStruct(queries.shape, BF16)
    narrow = jax.ShapeDtypeStruct((all_rows, KEY_HEADS * HEAD_SIZE), BF16)
    return pl.pallas_call(
        attention_kernel,
        grid=(KEY_HEADS, text // TILE),
        in_specs=[smem, smem, text_block, text_block, key_block, key_block],
        out_specs=[text_block, text_block, key_block, key_block],
        out_shape=[wide, wide, narrow, narrow],
        scratch_shapes=[
            pltpu.VMEM((all_rows, span), BF16),
            pltpu.VMEM((all_rows, span), BF16),
            pltpu.VMEM((all_rows, HEAD_SIZE), F32),
            pltpu.VMEM((all_rows, HEAD_SIZE), F32),
        ],
        cost_estimate=pl.CostEstimate(
            flops=12 * text * all_rows * KEY_HEADS * span,
            bytes_accessed=8 * text * KEY_HEADS * span,
            transcendentals=0,
        ),
        compiler_params=pltpu.CompilerParams(vmem_limit_bytes=40 * 1024 * 1024),
        name="attention",
    )(length, frames, queries, gradients, keys, values)


def weight_kernel(visual_ref, kg_ref, out_ref):
    total = dot(visual_ref[...], kg_ref[...], ((0,), (0,)))
    out_ref[...] = total.astype(BF16).reshape(out_ref.shape)


def weight_terms(samples, width, gathered, key_grads):
    rows, columns = key_grads.shape
    skipped = (gathered.shape[1] - width) // width
    return pl.pallas_call(
        weight_kernel,
        grid=(1,),
        in_specs=[
            pl.BlockSpec((rows, width), lambda k: (0, skipped)),
            pl.BlockSpec((rows, columns), lambda k: (0, 0)),
        ],
        out_specs=pl.BlockSpec((samples, width // samples, columns), lambda k: (0, 0, 0)),
        out_shape=jax.ShapeDtypeStruct((samples, width // samples, columns), BF16),
        compiler_params=pltpu.CompilerParams(vmem_limit_bytes=32 * 1024 * 1024),
        name="weight_terms",
    )(gathered, key_grads)


def sum_kernel(parts_ref, copies_ref):
    total = jnp.sum(parts_ref[...].astype(F32), axis=0).astype(BF16)
    for b in range(copies_ref.shape[0]):
        copies_ref[b] = total


def sum_copies(parts):
    vmem = pl.BlockSpec(memory_space=pltpu.VMEM)
    return pl.pallas_call(
        sum_kernel,
        in_specs=[vmem],
        out_specs=vmem,
        out_shape=jax.ShapeDtypeStruct(parts.shape, BF16),
        compiler_params=pltpu.CompilerParams(vmem_limit_bytes=32 * 1024 * 1024),
        name="sum_copies",
    )(parts)


def exchange(pieces, axis="blk"):
    return lax.all_to_all(pieces, axis, split_axis=0, concat_axis=0, tiled=True)


def flat(pieces):
    return pieces.reshape(-1, pieces.shape[-1])


def local(visual_rows, value_matrix, key_weight, queries, output_gradient, visual_len, frame_end):
    blocks, samples = lax.axis_size("blk"), lax.axis_size("dp")
    visual, value = visual_rows[0], value_matrix[0]
    rows, features = visual.shape
    columns = key_weight.shape[1]

    first = spread(blocks, visual, value)
    first, visual = lax.optimization_barrier((first, visual))
    gathered = flat(exchange(first))
    keys = flat(exchange(project(blocks, visual, key_weight)))
    attn_out, query_grad, key_terms, value_terms = attention(
        visual_len, frame_end, queries[0], output_gradient[0], keys, gathered
    )
    key_parts = exchange(key_terms.reshape(blocks, rows, columns))
    key_grads = flat(exchange(sum_copies(key_parts)))
    weight_parts = weight_terms(samples, features // blocks, gathered, key_grads)
    weight_parts, value_terms = lax.optimization_barrier((weight_parts, value_terms))
    weight_grad = jnp.sum(exchange(weight_parts, "dp").astype(F32), axis=0)
    value_parts = exchange(value_terms.reshape(blocks, rows, columns))
    value_grad = jnp.sum(value_parts.astype(F32), axis=0).astype(BF16)
    return attn_out[None], query_grad[None], value_grad[None], weight_grad


def solution(mesh):
    return jax.shard_map(
        local,
        mesh=mesh,
        in_specs=(
            P("dp", "blk", None),
            P("dp", "blk", None),
            P(),
            P("dp", "blk", None),
            P("dp", "blk", None),
            P("dp"),
            P("dp", None),
        ),
        out_specs=(
            P("dp", "blk", None),
            P("dp", "blk", None),
            P("dp", "blk", None),
            P(("blk", "dp"), None),
        ),
        check_vma=False,
    )
```

```python
import functools

import jax
import jax.numpy as jnp
from jax import lax
from jax.experimental import pallas as pl
from jax.experimental.pallas import tpu as pltpu
from jax.sharding import PartitionSpec as P

KEY_HEADS = 4
HEAD_SIZE = 128
TILE = 128
HEADS_PER_KEY = 8
LOG2_E = 1.4426950408889634
NEGATIVE_FILLER = -1e30
F32 = jnp.float32
BF16 = jnp.bfloat16
MIB = 1024 * 1024
VMEM = pl.BlockSpec(memory_space=pltpu.VMEM)


def dot(a, b, contract=((1,), (0,))):
    return lax.dot_general(a, b, (contract, ((), ())), preferred_element_type=F32)


def swap(x, axis, mask):
    size = lax.axis_size(axis)
    return lax.ppermute(x, axis, [(i, i ^ mask) for i in range(size)])


def project_kernel(streams, visual_ref, *refs):
    weight_refs, value_ref, out_ref, acc_ref = refs[:streams], *refs[streams:]
    step = pl.program_id(0)
    slab = weight_refs[0].shape[0]
    part = dot(visual_ref[:, :slab], weight_refs[0][...])
    for p in range(1, streams):
        part += dot(visual_ref[:, p * slab : (p + 1) * slab], weight_refs[p][...])

    @pl.when(step == 0)
    def _():
        acc_ref[...] = part

    @pl.when(step > 0)
    def _():
        acc_ref[...] += part

    @pl.when(step == pl.num_programs(0) - 1)
    def _():
        columns = acc_ref.shape[1]
        out_ref[:, :columns] = acc_ref[...].astype(BF16)
        out_ref[:, columns:] = value_ref[...]


def project(visual, key_weight, value):
    rows, features = visual.shape
    columns = key_weight.shape[1]
    steps, streams = 2, 4
    slab = features // (steps * streams)
    out = (rows, columns + value.shape[1])
    return pl.pallas_call(
        functools.partial(project_kernel, streams),
        grid=(steps,),
        in_specs=[pl.BlockSpec((rows, streams * slab), lambda k: (0, k))]
        + [
            pl.BlockSpec((slab, columns), lambda k, p=p: (k * streams + p, 0))
            for p in range(streams)
        ]
        + [pl.BlockSpec(value.shape, lambda k: (0, 0))],
        out_specs=pl.BlockSpec(out, lambda k: (0, 0)),
        out_shape=jax.ShapeDtypeStruct(out, BF16),
        scratch_shapes=[pltpu.VMEM((rows, columns), F32)],
        cost_estimate=pl.CostEstimate(
            flops=2 * rows * features * columns,
            bytes_accessed=2 * features * columns,
            transcendentals=0,
        ),
        name="project",
    )(visual, *[key_weight] * streams, value)


def attention_kernel(pieces, length_ref, frame_ref, q_ref, g_ref, visual_ref, *refs):
    kv_refs, (o_ref, qg_ref) = refs[:pieces], refs[pieces : pieces + 2]
    key_refs, value_refs = refs[pieces + 2 : 2 * pieces + 2], refs[2 * pieces + 2 : 3 * pieces + 2]
    w_all, ds_all, kg_acc, vg_acc = refs[3 * pieces + 2 :]
    j, i = pl.program_id(0), pl.program_id(1)
    block = lax.axis_index("blk")
    limit = jnp.minimum(length_ref[0], TILE * frame_ref[0, block * pl.num_programs(1) + i])
    width = KEY_HEADS * HEAD_SIZE
    head = pl.ds(pl.multiple_of(j * HEAD_SIZE, HEAD_SIZE), HEAD_SIZE)
    value_head = pl.ds(pl.multiple_of(width + j * HEAD_SIZE, HEAD_SIZE), HEAD_SIZE)
    keys = jnp.concatenate([r[:, head] for r in kv_refs], axis=0)
    values = jnp.concatenate([r[:, value_head] for r in kv_refs], axis=0)
    keys_t, values_t = keys.T, values.T
    pair = 2 * TILE
    rows = kv_refs[0].shape[0]
    row = lax.broadcasted_iota(jnp.int32, (rows, pair), 0)
    bias = jnp.concatenate(
        [
            jnp.where(row + (block ^ m) * rows < limit, 0.0, NEGATIVE_FILLER)
            for m in range(pieces)
        ],
        axis=0,
    )
    scale = HEAD_SIZE**-0.5
    q_stack, g_stack = [], []
    for h in range(0, HEADS_PER_KEY, 2):
        first = slice(h * HEAD_SIZE, (h + 1) * HEAD_SIZE)
        second = slice((h + 1) * HEAD_SIZE, (h + 2) * HEAD_SIZE)
        both = slice(h * HEAD_SIZE, (h + 2) * HEAD_SIZE)
        q = jnp.concatenate([q_ref[:, first], q_ref[:, second]], axis=0)
        g = jnp.concatenate([g_ref[:, first], g_ref[:, second]], axis=0)
        q_stack.append(q)
        g_stack.append(g)
        raw = dot(keys, q, ((1,), (1,))) + bias
        dprobs = dot(values, g, ((1,), (1,)))
        peak = jnp.max(raw, axis=0, keepdims=True)
        shifted = jnp.exp2((raw - peak) * (scale * LOG2_E))
        probs = shifted * (1.0 / jnp.sum(shifted, axis=0, keepdims=True))
        weights = probs.astype(BF16)
        terms = probs * dprobs
        delta = jnp.sum(terms, axis=0, keepdims=True)
        dscores = ((terms - probs * delta) * scale).astype(BF16)
        w_all[:, both] = weights
        ds_all[:, both] = dscores
        out = dot(values_t, weights).T.astype(BF16)
        o_ref[:, first] = out[:TILE]
        o_ref[:, second] = out[TILE:]
        grad = dot(keys_t, dscores).T.astype(BF16)
        qg_ref[:, first] = grad[:TILE]
        qg_ref[:, second] = grad[TILE:]
    kg = dot(ds_all[...], jnp.concatenate(q_stack, axis=0))
    vg = dot(w_all[...], jnp.concatenate(g_stack, axis=0))

    @pl.when(i == 0)
    def _():
        kg_acc[...] = kg
        vg_acc[...] = vg

    @pl.when(i > 0)
    def _():
        kg_acc[...] += kg
        vg_acc[...] += vg

    @pl.when(i == pl.num_programs(1) - 1)
    def _():
        for m in range(pieces):
            part = slice(m * rows, (m + 1) * rows)
            key_refs[m][:, head] = kg_acc[part, :].astype(BF16)
            value_refs[m][:, head] = vg_acc[part, :].astype(BF16)

    @pl.when(jnp.logical_and(j == 0, i == 0))
    def _():
        share = visual_ref.shape[1] // pieces
        for m in range(pieces):
            start = pl.multiple_of((block ^ m) * share, HEAD_SIZE)
            key_refs[m][:, width:] = visual_ref[:, pl.ds(start, share)]


def attention(length, frames, queries, gradients, visual, keys_values):
    pieces = len(keys_values)
    rows, both = keys_values[0].shape
    width = both // 2
    text = queries.shape[0]
    all_rows = pieces * rows
    span = HEADS_PER_KEY * HEAD_SIZE
    smem = pl.BlockSpec(memory_space=pltpu.SMEM)
    text_block = pl.BlockSpec((TILE, span), lambda j, i: (i, j))

    def whole(shape):
        return pl.BlockSpec(shape, lambda j, i: (0, 0))

    key_shape, value_shape = (rows, width + visual.shape[1] // pieces), (rows, width)
    wide = jax.ShapeDtypeStruct(queries.shape, BF16)
    out = pl.pallas_call(
        functools.partial(attention_kernel, pieces),
        grid=(KEY_HEADS, text // TILE),
        in_specs=[smem, smem, text_block, text_block, whole(visual.shape)]
        + [whole((rows, both))] * pieces,
        out_specs=[text_block] * 2 + [whole(key_shape)] * pieces + [whole(value_shape)] * pieces,
        out_shape=[wide] * 2
        + [jax.ShapeDtypeStruct(key_shape, BF16)] * pieces
        + [jax.ShapeDtypeStruct(value_shape, BF16)] * pieces,
        scratch_shapes=[
            pltpu.VMEM((all_rows, span), BF16),
            pltpu.VMEM((all_rows, span), BF16),
            pltpu.VMEM((all_rows, HEAD_SIZE), F32),
            pltpu.VMEM((all_rows, HEAD_SIZE), F32),
        ],
        cost_estimate=pl.CostEstimate(
            flops=12 * text * all_rows * KEY_HEADS * span,
            bytes_accessed=8 * text * KEY_HEADS * span,
            transcendentals=0,
        ),
        compiler_params=pltpu.CompilerParams(vmem_limit_bytes=40 * MIB),
        name="attention",
    )(length, frames, queries, gradients, visual, *keys_values)
    return out[0], out[1], out[2 : 2 + pieces], out[2 + pieces :]


def sum_kernel(pieces, *refs):
    part_refs, value_refs, out_refs = (refs[k * pieces : (k + 1) * pieces] for k in range(3))
    width = value_refs[0].shape[1]
    total = part_refs[0][:, :width].astype(F32)
    for ref in part_refs[1:]:
        total += ref[:, :width].astype(F32)
    own = total.astype(BF16)
    for m in range(pieces):
        out_refs[m][:, :width] = own
        out_refs[m][:, width:] = value_refs[m][...]


def sum_terms(parts, value_terms):
    pieces = len(parts)
    rows, width = value_terms[0].shape
    return pl.pallas_call(
        functools.partial(sum_kernel, pieces),
        in_specs=[VMEM] * (2 * pieces),
        out_specs=[VMEM] * pieces,
        out_shape=[jax.ShapeDtypeStruct((rows, 2 * width), BF16)] * pieces,
        compiler_params=pltpu.CompilerParams(vmem_limit_bytes=32 * MIB),
        name="sum_terms",
    )(*parts, *value_terms)


def weight_kernel(pieces, core_ref, *refs):
    part_refs, sum_refs = refs[:pieces], refs[pieces : 2 * pieces]
    value_ref, keep_ref, send_ref = refs[2 * pieces :]
    width = value_ref.shape[1]
    total = sum_refs[0][:, width:].astype(F32)
    for ref in sum_refs[1:]:
        total += ref[:, width:].astype(F32)
    value_ref[...] = total.astype(BF16)
    visual = jnp.concatenate([r[:, width:] for r in part_refs], axis=0)
    key_grad = jnp.concatenate([r[:, :width] for r in sum_refs], axis=0)
    product = dot(visual, key_grad, ((0,), (0,)))
    count, rows, _ = keep_ref.shape
    core = core_ref[0] == 0
    for n in range(count):
        even = product[2 * n * rows : (2 * n + 1) * rows]
        odd = product[(2 * n + 1) * rows : (2 * n + 2) * rows]
        keep_ref[n] = jnp.where(core, even, odd)
        send_ref[n] = jnp.where(core, odd, even).astype(BF16)


def weight_terms(samples, core, parts, sums):
    pieces = len(parts)
    rows, both = sums[0].shape
    width = both // 2
    features = parts[0].shape[1] - width
    half = (samples // 2, features // samples, width)
    return pl.pallas_call(
        functools.partial(weight_kernel, pieces),
        in_specs=[pl.BlockSpec(memory_space=pltpu.SMEM)] + [VMEM] * (2 * pieces),
        out_specs=[VMEM] * 3,
        out_shape=[
            jax.ShapeDtypeStruct((rows, width), BF16),
            jax.ShapeDtypeStruct(half, F32),
            jax.ShapeDtypeStruct(half, BF16),
        ],
        compiler_params=pltpu.CompilerParams(vmem_limit_bytes=32 * MIB),
        name="weight_terms",
    )(core, *parts, *sums)


def halve_kernel(bit_ref, kept_ref, came_ref, keep_ref, send_ref):
    low = bit_ref[0] == 0
    for n in range(keep_ref.shape[0]):
        even = kept_ref[2 * n] + came_ref[2 * n].astype(F32)
        odd = kept_ref[2 * n + 1] + came_ref[2 * n + 1].astype(F32)
        keep_ref[n] = jnp.where(low, even, odd)
        send_ref[n] = jnp.where(low, odd, even).astype(BF16)


def halve(bit, kept, came):
    half = (kept.shape[0] // 2, *kept.shape[1:])
    return pl.pallas_call(
        halve_kernel,
        in_specs=[pl.BlockSpec(memory_space=pltpu.SMEM), VMEM, VMEM],
        out_specs=[VMEM] * 2,
        out_shape=[jax.ShapeDtypeStruct(half, F32), jax.ShapeDtypeStruct(half, BF16)],
        compiler_params=pltpu.CompilerParams(vmem_limit_bytes=32 * MIB),
        name="halve",
    )(bit, kept, came)


def local(visual_rows, value_matrix, key_weight, queries, output_gradient, visual_len, frame_end):
    blocks, samples = lax.axis_size("blk"), lax.axis_size("dp")
    sample = lax.axis_index("dp").astype(jnp.int32)
    visual = visual_rows[0]
    masks = range(1, blocks)

    own = project(visual, key_weight, value_matrix[0])
    keys_values = [own] + [swap(own, "blk", m) for m in masks]
    attn_out, query_grad, key_terms, value_terms = attention(
        visual_len, frame_end, queries[0], output_gradient[0], visual, keys_values
    )
    parts = [key_terms[0]] + [swap(key_terms[m], "blk", m) for m in masks]
    sums = sum_terms(parts, value_terms)
    sums = [sums[0]] + [swap(sums[m], "blk", m) for m in masks]
    value_grad, kept, sent = weight_terms(samples, (sample % 2)[None], parts, sums)
    came, bit = swap(sent, "dp", 1), 1
    while kept.shape[0] > 1:
        kept, sent = halve(((sample >> bit) % 2)[None], kept, came)
        came, bit = swap(sent, "dp", 1 << bit), bit + 1
    weight_grad = kept[0] + came[0].astype(F32)
    return attn_out[None], query_grad[None], value_grad[None], weight_grad


def solution(mesh):
    return jax.shard_map(
        local,
        mesh=mesh,
        in_specs=(
            P("dp", "blk", None),
            P("dp", "blk", None),
            P(),
            P("dp", "blk", None),
            P("dp", "blk", None),
            P("dp"),
            P("dp", None),
        ),
        out_specs=(
            P("dp", "blk", None),
            P("dp", "blk", None),
            P("dp", "blk", None),
            P(("blk", "dp"), None),
        ),
        check_vma=False,
    )
```

```python
import functools

import jax
import jax.numpy as jnp
from jax import lax
from jax.experimental import pallas as pl
from jax.experimental.pallas import tpu as pltpu
from jax.sharding import PartitionSpec as P

KEY_HEADS = 4
HEAD_SIZE = 128
TILE = 128
HEADS_PER_KEY = 8
LOG2_E = 1.4426950408889634
NEGATIVE_FILLER = -1e30
F32 = jnp.float32
BF16 = jnp.bfloat16
MIB = 1024 * 1024
VMEM = pl.BlockSpec(memory_space=pltpu.VMEM)


def dot(a, b, contract=((1,), (0,))):
    return lax.dot_general(a, b, (contract, ((), ())), preferred_element_type=F32)


def swap(x, axis, mask):
    size = lax.axis_size(axis)
    return lax.ppermute(x, axis, [(i, i ^ mask) for i in range(size)])


def partner(piece, pieces):
    return (pieces - piece) % pieces


def project_kernel(chunks, weight_hbm, visual_ref, value_ref, out_ref, weight, sems):
    slab = weight.shape[0] // chunks
    copies = []
    for c in range(chunks):
        part = pl.ds(c * slab, slab)
        copies.append(pltpu.make_async_copy(weight_hbm.at[part], weight.at[part], sems.at[c]))
        copies[c].start()
    keys = jnp.zeros((visual_ref.shape[0], weight.shape[1]), F32)
    for c in range(chunks):
        copies[c].wait()
        part = slice(c * slab, (c + 1) * slab)
        keys += dot(visual_ref[:, part], weight[part, :])
    columns = weight.shape[1]
    out_ref[:, :columns] = keys.astype(BF16)
    out_ref[:, columns:] = value_ref[...]


def project(visual, key_weight, value):
    rows, features = visual.shape
    columns = key_weight.shape[1]
    chunks = 16
    return pl.pallas_call(
        functools.partial(project_kernel, chunks),
        in_specs=[pl.BlockSpec(memory_space=pltpu.HBM), VMEM, VMEM],
        out_specs=VMEM,
        out_shape=jax.ShapeDtypeStruct((rows, columns + value.shape[1]), BF16),
        scratch_shapes=[
            pltpu.VMEM(key_weight.shape, BF16),
            pltpu.SemaphoreType.DMA((chunks,)),
        ],
        cost_estimate=pl.CostEstimate(
            flops=2 * rows * features * columns,
            bytes_accessed=2 * features * columns,
            transcendentals=0,
        ),
        name="project",
    )(key_weight, visual, value)


def scores_kernel(pieces, length_ref, frame_ref, q_ref, g_ref, visual_hbm, *refs):
    kv_refs, (w_ref, ds_ref) = refs[:pieces], refs[pieces : pieces + 2]
    key_refs = refs[pieces + 2 : 2 * pieces + 2]
    kg_acc, visual, sem = refs[2 * pieces + 2 :]
    j, i = pl.program_id(0), pl.program_id(1)
    last = jnp.logical_and(j == pl.num_programs(0) - 1, i == pl.num_programs(1) - 1)
    copy = pltpu.make_async_copy(visual_hbm, visual, sem)

    @pl.when(jnp.logical_and(j == 0, i == 0))
    def _():
        copy.start()

    block = lax.axis_index("blk")
    limit = jnp.minimum(length_ref[0], TILE * frame_ref[0, block * pl.num_programs(1) + i])
    width = KEY_HEADS * HEAD_SIZE
    head = pl.ds(pl.multiple_of(j * HEAD_SIZE, HEAD_SIZE), HEAD_SIZE)
    value_head = pl.ds(pl.multiple_of(width + j * HEAD_SIZE, HEAD_SIZE), HEAD_SIZE)
    keys = jnp.concatenate([r[:, head] for r in kv_refs], axis=0)
    values = jnp.concatenate([r[:, value_head] for r in kv_refs], axis=0)
    pair = 2 * TILE
    rows = kv_refs[0].shape[0]
    row = lax.broadcasted_iota(jnp.int32, (rows, pair), 0)
    bias = jnp.concatenate(
        [
            jnp.where(row + (block ^ partner(m, pieces)) * rows < limit, 0.0, NEGATIVE_FILLER)
            for m in range(pieces)
        ],
        axis=0,
    )
    scale = HEAD_SIZE**-0.5
    pairs = HEADS_PER_KEY // 2
    q_stack, raw, dprobs = [], {}, {}

    def stacked(ref, p):
        first = slice(p * pair, p * pair + HEAD_SIZE)
        second = slice(p * pair + HEAD_SIZE, (p + 1) * pair)
        return jnp.concatenate([ref[:, first], ref[:, second]], axis=0)

    def products(p):
        q_stack.append(stacked(q_ref, p))
        raw[p] = dot(keys, q_stack[p], ((1,), (1,)))
        dprobs[p] = dot(values, stacked(g_ref, p), ((1,), (1,)))

    products(0)
    for p in range(pairs):
        if p + 1 < pairs:
            products(p + 1)
        scores = raw.pop(p) + bias
        peak = jnp.max(scores, axis=0, keepdims=True)
        shifted = jnp.exp2((scores - peak) * (scale * LOG2_E))
        probs = shifted * (1.0 / jnp.sum(shifted, axis=0, keepdims=True))
        terms = probs * dprobs.pop(p)
        delta = jnp.sum(terms, axis=0, keepdims=True)
        both = slice(p * pair, (p + 1) * pair)
        w_ref[:, both] = probs.astype(BF16)
        ds_ref[:, both] = ((terms - probs * delta) * scale).astype(BF16)
    kg = dot(ds_ref[...], jnp.concatenate(q_stack, axis=0))

    @pl.when(i == 0)
    def _():
        kg_acc[...] = kg

    @pl.when(i > 0)
    def _():
        kg_acc[...] += kg

    @pl.when(i == pl.num_programs(1) - 1)
    def _():
        for m in range(pieces):
            key_refs[m][:, head] = kg_acc[m * rows : (m + 1) * rows, :].astype(BF16)

    @pl.when(last)
    def _():
        copy.wait()
        share = visual.shape[1] // pieces
        for m in range(pieces):
            start = pl.multiple_of((block ^ partner(m, pieces)) * share, HEAD_SIZE)
            key_refs[m][:, width:] = visual[:, pl.ds(start, share)]


def values_kernel(pieces, g_ref, w_ref, *refs):
    value_refs, vg_acc = refs[:pieces], refs[pieces]
    j, i = pl.program_id(0), pl.program_id(1)
    head = pl.ds(pl.multiple_of(j * HEAD_SIZE, HEAD_SIZE), HEAD_SIZE)
    rows = value_refs[0].shape[0]
    stack = [g_ref[:, h * HEAD_SIZE : (h + 1) * HEAD_SIZE] for h in range(HEADS_PER_KEY)]
    vg = dot(w_ref[...], jnp.concatenate(stack, axis=0))

    @pl.when(i == 0)
    def _():
        vg_acc[...] = vg

    @pl.when(i > 0)
    def _():
        vg_acc[...] += vg

    @pl.when(i == pl.num_programs(1) - 1)
    def _():
        for m in range(pieces):
            value_refs[m][:, head] = vg_acc[m * rows : (m + 1) * rows, :].astype(BF16)


def outputs_kernel(pieces, w_ref, ds_ref, *refs):
    kv_refs, (o_ref, qg_ref) = refs[:pieces], refs[pieces:]
    j = pl.program_id(0)
    width = KEY_HEADS * HEAD_SIZE
    head = pl.ds(pl.multiple_of(j * HEAD_SIZE, HEAD_SIZE), HEAD_SIZE)
    value_head = pl.ds(pl.multiple_of(width + j * HEAD_SIZE, HEAD_SIZE), HEAD_SIZE)
    keys_t = jnp.concatenate([r[:, head] for r in kv_refs], axis=0).T
    values_t = jnp.concatenate([r[:, value_head] for r in kv_refs], axis=0).T
    pair = 2 * TILE
    for p in range(HEADS_PER_KEY // 2):
        first = slice(p * pair, p * pair + HEAD_SIZE)
        second = slice(p * pair + HEAD_SIZE, (p + 1) * pair)
        both = slice(p * pair, (p + 1) * pair)
        out = dot(values_t, w_ref[:, both]).T.astype(BF16)
        grad = dot(keys_t, ds_ref[:, both]).T.astype(BF16)
        o_ref[:, first] = out[:TILE]
        o_ref[:, second] = out[TILE:]
        qg_ref[:, first] = grad[:TILE]
        qg_ref[:, second] = grad[TILE:]


class Attention:
    def __init__(self, queries, pieces, rows):
        self.pieces, self.rows = pieces, rows
        self.text, self.wide = queries.shape
        self.tiles = self.text // TILE
        self.all_rows = pieces * rows
        self.width = KEY_HEADS * HEAD_SIZE
        span = HEADS_PER_KEY * HEAD_SIZE
        tiles = self.tiles
        self.text_block = pl.BlockSpec((TILE, span), lambda j, i: (i, j))
        self.inner_block = pl.BlockSpec((self.all_rows, span), lambda j, i: (0, j * tiles + i))
        self.inner = jax.ShapeDtypeStruct((self.all_rows, tiles * self.wide), BF16)

    def whole(self, columns):
        return pl.BlockSpec((self.rows, columns), lambda j, i: (0, 0))

    def call(self, kernel, products, moved, name, **specs):
        return pl.pallas_call(
            functools.partial(kernel, self.pieces),
            grid=(KEY_HEADS, self.tiles),
            cost_estimate=pl.CostEstimate(
                flops=2 * products * self.text * self.all_rows * self.wide,
                bytes_accessed=2 * moved * self.text * self.wide,
                transcendentals=0,
            ),
            compiler_params=pltpu.CompilerParams(vmem_limit_bytes=32 * MIB),
            name=name,
            **specs,
        )

    def scores(self, length, frames, queries, gradients, visual, keys_values):
        smem = pl.BlockSpec(memory_space=pltpu.SMEM)
        hbm = pl.BlockSpec(memory_space=pltpu.HBM)
        columns = self.width + visual.shape[1] // self.pieces
        piece = jax.ShapeDtypeStruct((self.rows, columns), BF16)
        out = self.call(
            scores_kernel,
            6,
            4,
            "scores",
            in_specs=[smem, smem, self.text_block, self.text_block, hbm]
            + [self.whole(2 * self.width)] * self.pieces,
            out_specs=[self.inner_block] * 2 + [self.whole(columns)] * self.pieces,
            out_shape=[self.inner] * 2 + [piece] * self.pieces,
            scratch_shapes=[
                pltpu.VMEM((self.all_rows, HEAD_SIZE), F32),
                pltpu.VMEM(visual.shape, BF16),
                pltpu.SemaphoreType.DMA,
            ],
        )(length, frames, queries, gradients, visual, *keys_values)
        return out[0], out[1], out[2:]

    def values(self, gradients, weights):
        piece = jax.ShapeDtypeStruct((self.rows, self.width), BF16)
        return self.call(
            values_kernel,
            1,
            2,
            "values",
            in_specs=[self.text_block, self.inner_block],
            out_specs=[self.whole(self.width)] * self.pieces,
            out_shape=[piece] * self.pieces,
            scratch_shapes=[pltpu.VMEM((self.all_rows, HEAD_SIZE), F32)],
        )(gradients, weights)

    def outputs(self, weights, dscores, keys_values):
        return self.call(
            outputs_kernel,
            2,
            4,
            "outputs",
            in_specs=[self.inner_block] * 2 + [self.whole(2 * self.width)] * self.pieces,
            out_specs=[self.text_block] * 2,
            out_shape=[jax.ShapeDtypeStruct((self.text, self.wide), BF16)] * 2,
        )(weights, dscores, *keys_values)


def sum_kernel(pieces, *refs):
    part_refs, value_refs, out_refs = (refs[k * pieces : (k + 1) * pieces] for k in range(3))
    width = value_refs[0].shape[1]
    total = part_refs[0][:, :width].astype(F32)
    for ref in part_refs[1:]:
        total += ref[:, :width].astype(F32)
    own = total.astype(BF16)
    for m in range(pieces):
        out_refs[m][:, :width] = own
        out_refs[m][:, width:] = value_refs[m][...]


def sum_terms(parts, value_terms):
    pieces = len(parts)
    rows, width = value_terms[0].shape
    return pl.pallas_call(
        functools.partial(sum_kernel, pieces),
        in_specs=[VMEM] * (2 * pieces),
        out_specs=[VMEM] * pieces,
        out_shape=[jax.ShapeDtypeStruct((rows, 2 * width), BF16)] * pieces,
        compiler_params=pltpu.CompilerParams(vmem_limit_bytes=32 * MIB),
        name="sum_terms",
    )(*parts, *value_terms)


def weight_kernel(pieces, core_ref, *refs):
    part_refs, sum_refs = refs[:pieces], refs[pieces : 2 * pieces]
    value_ref, keep_ref, send_ref = refs[2 * pieces :]
    width = value_ref.shape[1]
    total = sum_refs[0][:, width:].astype(F32)
    for ref in sum_refs[1:]:
        total += ref[:, width:].astype(F32)
    value_ref[...] = total.astype(BF16)
    visual = jnp.concatenate([r[:, width:] for r in part_refs], axis=0)
    key_grad = jnp.concatenate([r[:, :width] for r in sum_refs], axis=0)
    product = dot(visual, key_grad, ((0,), (0,)))
    count, rows, _ = keep_ref.shape
    core = core_ref[0] == 0
    for n in range(count):
        even = product[2 * n * rows : (2 * n + 1) * rows]
        odd = product[(2 * n + 1) * rows : (2 * n + 2) * rows]
        keep_ref[n] = jnp.where(core, even, odd)
        send_ref[n] = jnp.where(core, odd, even).astype(BF16)


def weight_terms(samples, core, parts, sums):
    pieces = len(parts)
    rows, both = sums[0].shape
    width = both // 2
    features = parts[0].shape[1] - width
    half = (samples // 2, features // samples, width)
    return pl.pallas_call(
        functools.partial(weight_kernel, pieces),
        in_specs=[pl.BlockSpec(memory_space=pltpu.SMEM)] + [VMEM] * (2 * pieces),
        out_specs=[VMEM] * 3,
        out_shape=[
            jax.ShapeDtypeStruct((rows, width), BF16),
            jax.ShapeDtypeStruct(half, F32),
            jax.ShapeDtypeStruct(half, BF16),
        ],
        compiler_params=pltpu.CompilerParams(vmem_limit_bytes=32 * MIB),
        name="weight_terms",
    )(core, *parts, *sums)


def halve_kernel(bit_ref, kept_ref, came_ref, keep_ref, send_ref):
    low = bit_ref[0] == 0
    for n in range(keep_ref.shape[0]):
        even = kept_ref[2 * n] + came_ref[2 * n].astype(F32)
        odd = kept_ref[2 * n + 1] + came_ref[2 * n + 1].astype(F32)
        keep_ref[n] = jnp.where(low, even, odd)
        send_ref[n] = jnp.where(low, odd, even).astype(BF16)


def halve(bit, kept, came):
    half = (kept.shape[0] // 2, *kept.shape[1:])
    return pl.pallas_call(
        halve_kernel,
        in_specs=[pl.BlockSpec(memory_space=pltpu.SMEM), VMEM, VMEM],
        out_specs=[VMEM] * 2,
        out_shape=[jax.ShapeDtypeStruct(half, F32), jax.ShapeDtypeStruct(half, BF16)],
        compiler_params=pltpu.CompilerParams(vmem_limit_bytes=32 * MIB),
        name="halve",
    )(bit, kept, came)


def local(visual_rows, value_matrix, key_weight, queries, output_gradient, visual_len, frame_end):
    blocks, samples = lax.axis_size("blk"), lax.axis_size("dp")
    sample = lax.axis_index("dp").astype(jnp.int32)
    visual = visual_rows[0]

    def from_partners(pieces):
        came = {m: swap(pieces[m], "blk", partner(m, blocks)) for m in reversed(range(1, blocks))}
        return [pieces[0]] + [came[m] for m in range(1, blocks)]

    keys_values = from_partners([project(visual, key_weight, value_matrix[0])] * blocks)
    attention = Attention(queries[0], blocks, visual.shape[0])
    weights, dscores, key_terms = attention.scores(
        visual_len, frame_end, queries[0], output_gradient[0], visual, keys_values
    )
    parts = from_partners(key_terms)
    parts[1], weights = lax.optimization_barrier((parts[1], weights))
    value_terms = attention.values(output_gradient[0], weights)
    sums = from_partners(sum_terms(parts, value_terms))
    sums[1], weights = lax.optimization_barrier((sums[1], weights))
    attn_out, query_grad = attention.outputs(weights, dscores, keys_values)
    value_grad, kept, sent = weight_terms(samples, (sample % 2)[None], parts, sums)
    came, bit = swap(sent, "dp", 1), 1
    while kept.shape[0] > 1:
        kept, sent = halve(((sample >> bit) % 2)[None], kept, came)
        came, bit = swap(sent, "dp", 1 << bit), bit + 1
    came, attn_out, query_grad = lax.optimization_barrier((came, attn_out, query_grad))
    weight_grad = kept[0] + came[0].astype(F32)
    return attn_out[None], query_grad[None], value_grad[None], weight_grad


def solution(mesh):
    return jax.shard_map(
        local,
        mesh=mesh,
        in_specs=(
            P("dp", "blk", None),
            P("dp", "blk", None),
            P(),
            P("dp", "blk", None),
            P("dp", "blk", None),
            P("dp"),
            P("dp", None),
        ),
        out_specs=(
            P("dp", "blk", None),
            P("dp", "blk", None),
            P("dp", "blk", None),
            P(("blk", "dp"), None),
        ),
        check_vma=False,
    )
```

```python
import functools

import jax
import jax.numpy as jnp
from jax import lax
from jax.experimental import pallas as pl
from jax.experimental.pallas import tpu as pltpu
from jax.sharding import PartitionSpec as P

KEY_HEADS = 4
HEAD_SIZE = 128
TILE = 128
HEADS_PER_KEY = 8
LOG2_E = 1.4426950408889634
NEGATIVE_FILLER = -1e30
F32 = jnp.float32
BF16 = jnp.bfloat16
MIB = 1024 * 1024
VMEM = pl.BlockSpec(memory_space=pltpu.VMEM)


def dot(a, b, contract=((1,), (0,))):
    return lax.dot_general(a, b, (contract, ((), ())), preferred_element_type=F32)


def swap(x, axis, mask):
    size = lax.axis_size(axis)
    return lax.ppermute(x, axis, [(i, i ^ mask) for i in range(size)])


def in_hbm(x):
    return pltpu.with_memory_space_constraint(x, pltpu.HBM)


def partner(piece, pieces):
    return (pieces - piece) % pieces


def project_kernel(streams, visual_ref, *refs):
    weight_refs, value_ref, out_ref, acc_ref = refs[:streams], *refs[streams:]
    step = pl.program_id(0)
    slab = weight_refs[0].shape[0]
    part = dot(visual_ref[:, :slab], weight_refs[0][...])
    for p in range(1, streams):
        part += dot(visual_ref[:, p * slab : (p + 1) * slab], weight_refs[p][...])

    @pl.when(step == 0)
    def _():
        acc_ref[...] = part

    @pl.when(step > 0)
    def _():
        acc_ref[...] += part

    @pl.when(step == pl.num_programs(0) - 1)
    def _():
        columns = acc_ref.shape[1]
        out_ref[:, :columns] = acc_ref[...].astype(BF16)
        out_ref[:, columns:] = value_ref[...]


def project(visual, key_weight, value):
    rows, features = visual.shape
    columns = key_weight.shape[1]
    steps, streams = 2, 4
    slab = features // (steps * streams)
    out = (rows, columns + value.shape[1])
    return pl.pallas_call(
        functools.partial(project_kernel, streams),
        grid=(steps,),
        in_specs=[pl.BlockSpec((rows, streams * slab), lambda k: (0, k))]
        + [
            pl.BlockSpec((slab, columns), lambda k, p=p: (k * streams + p, 0))
            for p in range(streams)
        ]
        + [pl.BlockSpec(value.shape, lambda k: (0, 0))],
        out_specs=pl.BlockSpec(out, lambda k: (0, 0)),
        out_shape=jax.ShapeDtypeStruct(out, BF16),
        scratch_shapes=[pltpu.VMEM((rows, columns), F32)],
        cost_estimate=pl.CostEstimate(
            flops=2 * rows * features * columns,
            bytes_accessed=2 * features * columns,
            transcendentals=0,
        ),
        compiler_params=pltpu.CompilerParams(vmem_limit_bytes=32 * MIB),
        name="project",
    )(in_hbm(visual), *[in_hbm(key_weight)] * streams, in_hbm(value))


def scores_kernel(pieces, length_ref, frame_ref, q_ref, g_ref, visual_hbm, *refs):
    kv_refs, (w_ref, ds_ref, kv_ref) = refs[:pieces], refs[pieces : pieces + 3]
    key_refs = refs[pieces + 3 : 2 * pieces + 3]
    kg_acc, visual, sem = refs[2 * pieces + 3 :]
    j, i = pl.program_id(0), pl.program_id(1)
    last = jnp.logical_and(j == pl.num_programs(0) - 1, i == pl.num_programs(1) - 1)
    copy = pltpu.make_async_copy(visual_hbm, visual, sem)

    @pl.when(jnp.logical_and(j == 0, i == 0))
    def _():
        copy.start()

    block = lax.axis_index("blk")
    limit = jnp.minimum(length_ref[0], TILE * frame_ref[0, block * pl.num_programs(1) + i])
    width = KEY_HEADS * HEAD_SIZE
    head = pl.ds(pl.multiple_of(j * HEAD_SIZE, HEAD_SIZE), HEAD_SIZE)
    value_head = pl.ds(pl.multiple_of(width + j * HEAD_SIZE, HEAD_SIZE), HEAD_SIZE)
    keys = jnp.concatenate([r[:, head] for r in kv_refs], axis=0)
    values = jnp.concatenate([r[:, value_head] for r in kv_refs], axis=0)
    kv_ref[:, :HEAD_SIZE] = keys
    kv_ref[:, HEAD_SIZE:] = values
    pair = 2 * TILE
    rows = kv_refs[0].shape[0]
    row = lax.broadcasted_iota(jnp.int32, (rows, pair), 0)
    bias = jnp.concatenate(
        [
            jnp.where(row + (block ^ partner(m, pieces)) * rows < limit, 0.0, NEGATIVE_FILLER)
            for m in range(pieces)
        ],
        axis=0,
    )
    scale = HEAD_SIZE**-0.5
    pairs = HEADS_PER_KEY // 2
    q_stack, raw, dprobs = [], {}, {}

    def stacked(ref, p):
        first = slice(p * pair, p * pair + HEAD_SIZE)
        second = slice(p * pair + HEAD_SIZE, (p + 1) * pair)
        return jnp.concatenate([ref[:, first], ref[:, second]], axis=0)

    def products(p):
        q_stack.append(stacked(q_ref, p))
        raw[p] = dot(keys, q_stack[p], ((1,), (1,)))
        dprobs[p] = dot(values, stacked(g_ref, p), ((1,), (1,)))

    products(0)
    for p in range(pairs):
        if p + 1 < pairs:
            products(p + 1)
        scores = raw.pop(p) + bias
        peak = jnp.max(scores, axis=0, keepdims=True)
        shifted = jnp.exp2((scores - peak) * (scale * LOG2_E))
        probs = shifted * (1.0 / jnp.sum(shifted, axis=0, keepdims=True))
        terms = probs * dprobs.pop(p)
        delta = jnp.sum(terms, axis=0, keepdims=True)
        both = slice(p * pair, (p + 1) * pair)
        w_ref[:, both] = probs.astype(BF16)
        ds_ref[:, both] = ((terms - probs * delta) * scale).astype(BF16)
    kg = dot(ds_ref[...], jnp.concatenate(q_stack, axis=0))

    @pl.when(i == 0)
    def _():
        kg_acc[...] = kg

    @pl.when(i > 0)
    def _():
        kg_acc[...] += kg

    @pl.when(i == pl.num_programs(1) - 1)
    def _():
        for m in range(pieces):
            key_refs[m][:, head] = kg_acc[m * rows : (m + 1) * rows, :].astype(BF16)

    @pl.when(last)
    def _():
        copy.wait()
        share = visual.shape[1] // pieces
        for m in range(pieces):
            start = pl.multiple_of((block ^ partner(m, pieces)) * share, HEAD_SIZE)
            key_refs[m][:, width:] = visual[:, pl.ds(start, share)]


def values_kernel(pieces, g_ref, w_ref, *refs):
    value_refs, vg_acc = refs[:pieces], refs[pieces]
    j, i = pl.program_id(0), pl.program_id(1)
    head = pl.ds(pl.multiple_of(j * HEAD_SIZE, HEAD_SIZE), HEAD_SIZE)
    rows = value_refs[0].shape[0]
    stack = [g_ref[:, h * HEAD_SIZE : (h + 1) * HEAD_SIZE] for h in range(HEADS_PER_KEY)]
    vg = dot(w_ref[...], jnp.concatenate(stack, axis=0))

    @pl.when(i == 0)
    def _():
        vg_acc[...] = vg

    @pl.when(i > 0)
    def _():
        vg_acc[...] += vg

    @pl.when(i == pl.num_programs(1) - 1)
    def _():
        for m in range(pieces):
            value_refs[m][:, head] = vg_acc[m * rows : (m + 1) * rows, :].astype(BF16)


def outputs_kernel(pieces, w_ref, ds_ref, kv_ref, o_ref, qg_ref):
    keys_t, values_t = kv_ref[:, :HEAD_SIZE].T, kv_ref[:, HEAD_SIZE:].T
    pair = 2 * TILE
    for p in range(HEADS_PER_KEY // 2):
        first = slice(p * pair, p * pair + HEAD_SIZE)
        second = slice(p * pair + HEAD_SIZE, (p + 1) * pair)
        both = slice(p * pair, (p + 1) * pair)
        out = dot(values_t, w_ref[:, both]).T.astype(BF16)
        grad = dot(keys_t, ds_ref[:, both]).T.astype(BF16)
        o_ref[:, first] = out[:TILE]
        o_ref[:, second] = out[TILE:]
        qg_ref[:, first] = grad[:TILE]
        qg_ref[:, second] = grad[TILE:]


class Attention:
    def __init__(self, queries, pieces, rows):
        self.pieces, self.rows = pieces, rows
        self.text, self.wide = queries.shape
        self.tiles = self.text // TILE
        self.all_rows = pieces * rows
        self.width = KEY_HEADS * HEAD_SIZE
        span = HEADS_PER_KEY * HEAD_SIZE
        tiles = self.tiles
        self.text_block = pl.BlockSpec((TILE, span), lambda j, i: (i, j))
        self.inner_block = pl.BlockSpec((self.all_rows, span), lambda j, i: (0, j * tiles + i))
        self.inner = pltpu.HBM((self.all_rows, tiles * self.wide), BF16)
        self.head_block = pl.BlockSpec((self.all_rows, 2 * HEAD_SIZE), lambda j, i: (0, j))

    def whole(self, columns):
        return pl.BlockSpec((self.rows, columns), lambda j, i: (0, 0))

    def call(self, kernel, products, moved, name, **specs):
        return pl.pallas_call(
            functools.partial(kernel, self.pieces),
            grid=(KEY_HEADS, self.tiles),
            cost_estimate=pl.CostEstimate(
                flops=2 * products * self.text * self.all_rows * self.wide,
                bytes_accessed=2 * moved * self.text * self.wide,
                transcendentals=0,
            ),
            compiler_params=pltpu.CompilerParams(vmem_limit_bytes=32 * MIB),
            name=name,
            **specs,
        )

    def scores(self, length, frames, queries, gradients, visual, keys_values):
        smem = pl.BlockSpec(memory_space=pltpu.SMEM)
        hbm = pl.BlockSpec(memory_space=pltpu.HBM)
        columns = self.width + visual.shape[1] // self.pieces
        piece = jax.ShapeDtypeStruct((self.rows, columns), BF16)
        out = self.call(
            scores_kernel,
            6,
            4,
            "scores",
            in_specs=[smem, smem, self.text_block, self.text_block, hbm]
            + [self.whole(2 * self.width)] * self.pieces,
            out_specs=[self.inner_block] * 2
            + [self.head_block]
            + [self.whole(columns)] * self.pieces,
            out_shape=[self.inner] * 2
            + [pltpu.HBM((self.all_rows, 2 * self.width), BF16)]
            + [piece] * self.pieces,
            scratch_shapes=[
                pltpu.VMEM((self.all_rows, HEAD_SIZE), F32),
                pltpu.VMEM(visual.shape, BF16),
                pltpu.SemaphoreType.DMA,
            ],
        )(length, frames, queries, gradients, in_hbm(visual), *keys_values)
        return out[0], out[1], out[2], out[3:]

    def values(self, gradients, weights):
        piece = jax.ShapeDtypeStruct((self.rows, self.width), BF16)
        return self.call(
            values_kernel,
            1,
            2,
            "values",
            in_specs=[self.text_block, self.inner_block],
            out_specs=[self.whole(self.width)] * self.pieces,
            out_shape=[piece] * self.pieces,
            scratch_shapes=[pltpu.VMEM((self.all_rows, HEAD_SIZE), F32)],
        )(in_hbm(gradients), in_hbm(weights))

    def outputs(self, weights, dscores, keys_values):
        return self.call(
            outputs_kernel,
            2,
            4,
            "outputs",
            in_specs=[self.inner_block] * 2 + [self.head_block],
            out_specs=[self.text_block] * 2,
            out_shape=[jax.ShapeDtypeStruct((self.text, self.wide), BF16)] * 2,
        )(in_hbm(weights), in_hbm(dscores), in_hbm(keys_values))


def sum_kernel(pieces, *refs):
    part_refs, value_refs, out_refs = (refs[k * pieces : (k + 1) * pieces] for k in range(3))
    width = value_refs[0].shape[1]
    total = part_refs[0][:, :width].astype(F32)
    for ref in part_refs[1:]:
        total += ref[:, :width].astype(F32)
    own = total.astype(BF16)
    for m in range(pieces):
        out_refs[m][:, :width] = own
        out_refs[m][:, width:] = value_refs[m][...]


def sum_terms(parts, value_terms):
    pieces = len(parts)
    rows, width = value_terms[0].shape
    return pl.pallas_call(
        functools.partial(sum_kernel, pieces),
        in_specs=[VMEM] * (2 * pieces),
        out_specs=[VMEM] * pieces,
        out_shape=[jax.ShapeDtypeStruct((rows, 2 * width), BF16)] * pieces,
        compiler_params=pltpu.CompilerParams(vmem_limit_bytes=32 * MIB),
        name="sum_terms",
    )(*parts, *value_terms)


def weight_kernel(pieces, core_ref, *refs):
    part_refs, sum_refs = refs[:pieces], refs[pieces : 2 * pieces]
    value_ref, keep_ref, send_ref = refs[2 * pieces :]
    width = value_ref.shape[1]
    total = sum_refs[0][:, width:].astype(F32)
    for ref in sum_refs[1:]:
        total += ref[:, width:].astype(F32)
    value_ref[...] = total.astype(BF16)
    visual = jnp.concatenate([r[:, width:] for r in part_refs], axis=0)
    key_grad = jnp.concatenate([r[:, :width] for r in sum_refs], axis=0)
    product = dot(visual, key_grad, ((0,), (0,)))
    count, rows, _ = keep_ref.shape
    core = core_ref[0] == 0
    for n in range(count):
        even = product[2 * n * rows : (2 * n + 1) * rows]
        odd = product[(2 * n + 1) * rows : (2 * n + 2) * rows]
        keep_ref[n] = jnp.where(core, even, odd)
        send_ref[n] = jnp.where(core, odd, even).astype(BF16)


def weight_terms(samples, core, parts, sums):
    pieces = len(parts)
    rows, both = sums[0].shape
    width = both // 2
    features = parts[0].shape[1] - width
    half = (samples // 2, features // samples, width)
    return pl.pallas_call(
        functools.partial(weight_kernel, pieces),
        in_specs=[pl.BlockSpec(memory_space=pltpu.SMEM)] + [VMEM] * (2 * pieces),
        out_specs=[VMEM] * 3,
        out_shape=[
            jax.ShapeDtypeStruct((rows, width), BF16),
            jax.ShapeDtypeStruct(half, F32),
            jax.ShapeDtypeStruct(half, BF16),
        ],
        compiler_params=pltpu.CompilerParams(vmem_limit_bytes=32 * MIB),
        name="weight_terms",
    )(core, *parts, *sums)


def halve_kernel(bit_ref, kept_ref, came_ref, keep_ref, send_ref):
    low = bit_ref[0] == 0
    for n in range(keep_ref.shape[0]):
        even = kept_ref[2 * n] + came_ref[2 * n].astype(F32)
        odd = kept_ref[2 * n + 1] + came_ref[2 * n + 1].astype(F32)
        keep_ref[n] = jnp.where(low, even, odd)
        send_ref[n] = jnp.where(low, odd, even).astype(BF16)


def halve(bit, kept, came):
    half = (kept.shape[0] // 2, *kept.shape[1:])
    return pl.pallas_call(
        halve_kernel,
        in_specs=[pl.BlockSpec(memory_space=pltpu.SMEM), VMEM, VMEM],
        out_specs=[VMEM] * 2,
        out_shape=[jax.ShapeDtypeStruct(half, F32), jax.ShapeDtypeStruct(half, BF16)],
        compiler_params=pltpu.CompilerParams(vmem_limit_bytes=32 * MIB),
        name="halve",
    )(bit, kept, came)


def local(visual_rows, value_matrix, key_weight, queries, output_gradient, visual_len, frame_end):
    blocks, samples = lax.axis_size("blk"), lax.axis_size("dp")
    sample = lax.axis_index("dp").astype(jnp.int32)
    visual = visual_rows[0]

    def from_partners(pieces):
        came = {m: swap(pieces[m], "blk", partner(m, blocks)) for m in reversed(range(1, blocks))}
        return [pieces[0]] + [came[m] for m in range(1, blocks)]

    keys_values = from_partners([project(visual, key_weight, value_matrix[0])] * blocks)
    attention = Attention(queries[0], blocks, visual.shape[0])
    weights, dscores, all_keys_values, key_terms = attention.scores(
        visual_len, frame_end, queries[0], output_gradient[0], visual, keys_values
    )
    parts = from_partners(key_terms)
    parts[1], weights = lax.optimization_barrier((parts[1], weights))
    value_terms = attention.values(output_gradient[0], weights)
    sums = from_partners(sum_terms(parts, value_terms))
    sums[1], weights = lax.optimization_barrier((sums[1], weights))
    attn_out, query_grad = attention.outputs(weights, dscores, all_keys_values)
    value_grad, kept, sent = weight_terms(samples, (sample % 2)[None], parts, sums)
    came, bit = swap(sent, "dp", 1), 1
    while kept.shape[0] > 1:
        kept, sent = halve(((sample >> bit) % 2)[None], kept, came)
        came, bit = swap(sent, "dp", 1 << bit), bit + 1
    came, attn_out, query_grad = lax.optimization_barrier((came, attn_out, query_grad))
    weight_grad = kept[0] + came[0].astype(F32)
    return attn_out[None], query_grad[None], value_grad[None], weight_grad


def solution(mesh):
    return jax.shard_map(
        local,
        mesh=mesh,
        in_specs=(
            P("dp", "blk", None),
            P("dp", "blk", None),
            P(),
            P("dp", "blk", None),
            P("dp", "blk", None),
            P("dp"),
            P("dp", None),
        ),
        out_specs=(
            P("dp", "blk", None),
            P("dp", "blk", None),
            P("dp", "blk", None),
            P(("blk", "dp"), None),
        ),
        check_vma=False,
    )
```

```python
import functools

import jax
import jax.numpy as jnp
from jax import lax
from jax.experimental import pallas as pl
from jax.experimental.pallas import tpu as pltpu
from jax.sharding import PartitionSpec as P

KEY_HEADS = 4
HEAD_SIZE = 128
TILE = 128
HEADS_PER_KEY = 8
LOG2_E = 1.4426950408889634
NEGATIVE_FILLER = -1e30
F32 = jnp.float32
BF16 = jnp.bfloat16
MIB = 1024 * 1024
VMEM = pl.BlockSpec(memory_space=pltpu.VMEM)


def dot(a, b, contract=((1,), (0,))):
    return lax.dot_general(a, b, (contract, ((), ())), preferred_element_type=F32)


def swap(x, axis, mask):
    size = lax.axis_size(axis)
    return lax.ppermute(x, axis, [(i, i ^ mask) for i in range(size)])


def in_hbm(x):
    return pltpu.with_memory_space_constraint(x, pltpu.HBM)


def partner(piece, pieces):
    return (pieces - piece) % pieces


def project_kernel(streams, visual_ref, *refs):
    weight_refs, value_ref, out_ref, acc_ref = refs[:streams], *refs[streams:]
    step = pl.program_id(0)
    slab = weight_refs[0].shape[0]
    part = dot(visual_ref[:, :slab], weight_refs[0][...])
    for p in range(1, streams):
        part += dot(visual_ref[:, p * slab : (p + 1) * slab], weight_refs[p][...])

    @pl.when(step == 0)
    def _():
        acc_ref[...] = part

    @pl.when(step > 0)
    def _():
        acc_ref[...] += part

    @pl.when(step == pl.num_programs(0) - 1)
    def _():
        columns = acc_ref.shape[1]
        out_ref[:, :columns] = acc_ref[...].astype(BF16)
        out_ref[:, columns:] = value_ref[...]


def project(visual, key_weight, value):
    rows, features = visual.shape
    columns = key_weight.shape[1]
    steps, streams = 2, 4
    slab = features // (steps * streams)
    out = (rows, columns + value.shape[1])
    return pl.pallas_call(
        functools.partial(project_kernel, streams),
        grid=(steps,),
        in_specs=[pl.BlockSpec((rows, streams * slab), lambda k: (0, k))]
        + [
            pl.BlockSpec((slab, columns), lambda k, p=p: (k * streams + p, 0))
            for p in range(streams)
        ]
        + [pl.BlockSpec(value.shape, lambda k: (0, 0))],
        out_specs=pl.BlockSpec(out, lambda k: (0, 0)),
        out_shape=jax.ShapeDtypeStruct(out, BF16),
        scratch_shapes=[pltpu.VMEM((rows, columns), F32)],
        cost_estimate=pl.CostEstimate(
            flops=2 * rows * features * columns,
            bytes_accessed=2 * features * columns,
            transcendentals=0,
        ),
        compiler_params=pltpu.CompilerParams(vmem_limit_bytes=32 * MIB),
        name="project",
    )(in_hbm(visual), *[in_hbm(key_weight)] * streams, in_hbm(value))


def head_pair(ref, rows, start):
    first = pl.ds(pl.multiple_of(start, HEAD_SIZE), HEAD_SIZE)
    second = pl.ds(pl.multiple_of(start + HEAD_SIZE, HEAD_SIZE), HEAD_SIZE)
    return jnp.concatenate([ref[rows, first], ref[rows, second]], axis=0)


def scores_kernel(pieces, length_ref, frame_ref, q_ref, g_ref, visual_hbm, *refs):
    kv_refs, (w_ref, ds_ref, k_ref, v_ref) = refs[:pieces], refs[pieces : pieces + 4]
    key_refs = refs[pieces + 4 : 2 * pieces + 4]
    kg_acc, bias_ref, visual, sem = refs[2 * pieces + 4 :]
    copy = pltpu.make_async_copy(visual_hbm, visual, sem)
    copy.start()
    block = lax.axis_index("blk")
    tiles = q_ref.shape[0] // TILE
    rows = kv_refs[0].shape[0]
    width = KEY_HEADS * HEAD_SIZE
    pair = 2 * TILE
    pairs = HEADS_PER_KEY // 2
    span = HEADS_PER_KEY * HEAD_SIZE
    scale = HEAD_SIZE**-0.5
    for m in range(pieces):
        part = slice(m * rows, (m + 1) * rows)
        k_ref[part, :] = kv_refs[m][:, :width]
        v_ref[part, :] = kv_refs[m][:, width:]
    row = lax.broadcasted_iota(jnp.int32, (rows, pair), 0)
    for i in range(tiles):
        text = slice(i * TILE, (i + 1) * TILE)
        limit = jnp.minimum(length_ref[0], TILE * frame_ref[0, block * tiles + i])
        for m in range(pieces):
            live = row + (block ^ partner(m, pieces)) * rows < limit
            bias_ref[m * rows : (m + 1) * rows, :] = jnp.where(live, 0.0, NEGATIVE_FILLER)

        @pl.loop(0, KEY_HEADS)
        def _(j, i=i, text=text):
            head = pl.ds(pl.multiple_of(j * HEAD_SIZE, HEAD_SIZE), HEAD_SIZE)
            keys, values = k_ref[:, head], v_ref[:, head]
            q_stack, raw, dprobs = [], {}, {}

            def products(p):
                start = j * span + p * pair
                q_stack.append(head_pair(q_ref, text, start))
                raw[p] = dot(keys, q_stack[p], ((1,), (1,)))
                dprobs[p] = dot(values, head_pair(g_ref, text, start), ((1,), (1,)))

            products(0)
            ds_stack = []
            for p in range(pairs):
                if p + 1 < pairs:
                    products(p + 1)
                scores = raw.pop(p) + bias_ref[...]
                peak = jnp.max(scores, axis=0, keepdims=True)
                shifted = jnp.exp2((scores - peak) * (scale * LOG2_E))
                terms = shifted * dprobs.pop(p)
                inverse = 1.0 / jnp.sum(shifted, axis=0, keepdims=True)
                slope = inverse * scale
                offset = jnp.sum(terms, axis=0, keepdims=True) * inverse * slope
                start = (i * KEY_HEADS + j) * span + p * pair
                both = pl.ds(pl.multiple_of(start, HEAD_SIZE), pair)
                w_ref[:, both] = (shifted * inverse).astype(BF16)
                ds_stack.append((terms * slope - shifted * offset).astype(BF16))
                ds_ref[:, both] = ds_stack[p]
            kg = dot(jnp.concatenate(ds_stack, axis=1), jnp.concatenate(q_stack, axis=0))
            if i == 0:
                kg_acc[:, head] = kg
            else:
                kg_acc[:, head] += kg

    copy.wait()
    share = visual.shape[1] // pieces
    for m in range(pieces):
        start = pl.multiple_of((block ^ partner(m, pieces)) * share, HEAD_SIZE)
        key_refs[m][:, :width] = kg_acc[m * rows : (m + 1) * rows, :].astype(BF16)
        key_refs[m][:, width:] = visual[:, pl.ds(start, share)]


def values_kernel(pieces, g_ref, w_ref, v_ref, *refs):
    o_ref, value_refs, vg_acc = refs[0], refs[1 : 1 + pieces], refs[1 + pieces]
    j, i = pl.program_id(0), pl.program_id(1)
    head = pl.ds(pl.multiple_of(j * HEAD_SIZE, HEAD_SIZE), HEAD_SIZE)
    rows = value_refs[0].shape[0]
    stack = [g_ref[:, h * HEAD_SIZE : (h + 1) * HEAD_SIZE] for h in range(HEADS_PER_KEY)]
    vg = dot(w_ref[...], jnp.concatenate(stack, axis=0))
    store_rows(o_ref, v_ref[...].T, w_ref)

    @pl.when(i == 0)
    def _():
        vg_acc[...] = vg

    @pl.when(i > 0)
    def _():
        vg_acc[...] += vg

    @pl.when(i == pl.num_programs(1) - 1)
    def _():
        for m in range(pieces):
            value_refs[m][:, head] = vg_acc[m * rows : (m + 1) * rows, :].astype(BF16)


def store_rows(out_ref, left, inner_ref):
    pair = 2 * TILE
    for p in range(HEADS_PER_KEY // 2):
        out = dot(left, inner_ref[:, p * pair : (p + 1) * pair]).T.astype(BF16)
        out_ref[:, p * pair : p * pair + HEAD_SIZE] = out[:TILE]
        out_ref[:, p * pair + HEAD_SIZE : (p + 1) * pair] = out[TILE:]


def queries_kernel(pieces, ds_ref, k_ref, qg_ref):
    store_rows(qg_ref, k_ref[...].T, ds_ref)


class Attention:
    def __init__(self, queries, pieces, rows):
        self.pieces, self.rows = pieces, rows
        self.text, self.wide = queries.shape
        self.tiles = self.text // TILE
        self.all_rows = pieces * rows
        self.width = KEY_HEADS * HEAD_SIZE
        span = HEADS_PER_KEY * HEAD_SIZE
        self.text_block = pl.BlockSpec((TILE, span), lambda j, i: (i, j))
        self.inner_block = pl.BlockSpec((self.all_rows, span), lambda j, i: (0, i * KEY_HEADS + j))
        self.head_block = pl.BlockSpec((self.all_rows, HEAD_SIZE), lambda j, i: (0, j))
        self.inner = jax.ShapeDtypeStruct((self.all_rows, self.tiles * self.wide), BF16)

    def call(self, kernel, products, moved, name, **specs):
        return pl.pallas_call(
            functools.partial(kernel, self.pieces),
            cost_estimate=pl.CostEstimate(
                flops=2 * products * self.text * self.all_rows * self.wide,
                bytes_accessed=2 * moved * self.text * self.wide,
                transcendentals=0,
            ),
            compiler_params=pltpu.CompilerParams(vmem_limit_bytes=32 * MIB),
            name=name,
            **specs,
        )

    def scores(self, length, frames, queries, gradients, visual, keys_values):
        smem = pl.BlockSpec(memory_space=pltpu.SMEM)
        hbm = pl.BlockSpec(memory_space=pltpu.HBM)
        columns = self.width + visual.shape[1] // self.pieces
        piece = jax.ShapeDtypeStruct((self.rows, columns), BF16)
        heads = jax.ShapeDtypeStruct((self.all_rows, self.width), BF16)
        out = self.call(
            scores_kernel,
            6,
            4,
            "scores",
            in_specs=[smem, smem, VMEM, VMEM, hbm] + [VMEM] * self.pieces,
            out_specs=[VMEM] * (4 + self.pieces),
            out_shape=[self.inner] * 2 + [heads] * 2 + [piece] * self.pieces,
            scratch_shapes=[
                pltpu.VMEM((self.all_rows, self.width), F32),
                pltpu.VMEM((self.all_rows, 2 * TILE), F32),
                pltpu.VMEM(visual.shape, BF16),
                pltpu.SemaphoreType.DMA,
            ],
        )(length, frames, queries, gradients, in_hbm(visual), *keys_values)
        return out[:4], out[4:]

    def values(self, gradients, weights, values):
        piece = jax.ShapeDtypeStruct((self.rows, self.width), BF16)
        out = self.call(
            values_kernel,
            1,
            2,
            "values",
            grid=(KEY_HEADS, self.tiles),
            in_specs=[self.text_block, self.inner_block, self.head_block],
            out_specs=[self.text_block]
            + [pl.BlockSpec((self.rows, self.width), lambda j, i: (0, 0))] * self.pieces,
            out_shape=[jax.ShapeDtypeStruct((self.text, self.wide), BF16)] + [piece] * self.pieces,
            scratch_shapes=[pltpu.VMEM((self.all_rows, HEAD_SIZE), F32)],
        )(in_hbm(gradients), weights, values)
        return out[0], out[1:]

    def queries(self, dscores, keys):
        return self.call(
            queries_kernel,
            1,
            3,
            "queries",
            grid=(KEY_HEADS, self.tiles),
            in_specs=[self.inner_block, self.head_block],
            out_specs=self.text_block,
            out_shape=jax.ShapeDtypeStruct((self.text, self.wide), BF16),
        )(dscores, keys)


def sum_kernel(pieces, *refs):
    part_refs, value_refs, out_refs = (refs[k * pieces : (k + 1) * pieces] for k in range(3))
    width = value_refs[0].shape[1]
    total = part_refs[0][:, :width].astype(F32)
    for ref in part_refs[1:]:
        total += ref[:, :width].astype(F32)
    own = total.astype(BF16)
    for m in range(pieces):
        out_refs[m][:, :width] = own
        out_refs[m][:, width:] = value_refs[m][...]


def sum_terms(parts, value_terms):
    pieces = len(parts)
    rows, width = value_terms[0].shape
    return pl.pallas_call(
        functools.partial(sum_kernel, pieces),
        in_specs=[VMEM] * (2 * pieces),
        out_specs=[VMEM] * pieces,
        out_shape=[jax.ShapeDtypeStruct((rows, 2 * width), BF16)] * pieces,
        compiler_params=pltpu.CompilerParams(vmem_limit_bytes=32 * MIB),
        name="sum_terms",
    )(*parts, *value_terms)


def weight_kernel(pieces, core_ref, *refs):
    part_refs, sum_refs = refs[:pieces], refs[pieces : 2 * pieces]
    value_ref, keep_ref, send_ref = refs[2 * pieces :]
    width = value_ref.shape[1]
    total = sum_refs[0][:, width:].astype(F32)
    for ref in sum_refs[1:]:
        total += ref[:, width:].astype(F32)
    value_ref[...] = total.astype(BF16)
    visual = jnp.concatenate([r[:, width:] for r in part_refs], axis=0)
    key_grad = jnp.concatenate([r[:, :width] for r in sum_refs], axis=0)
    product = dot(visual, key_grad, ((0,), (0,)))
    count, rows, _ = keep_ref.shape
    core = core_ref[0] == 0
    for n in range(count):
        even = product[2 * n * rows : (2 * n + 1) * rows]
        odd = product[(2 * n + 1) * rows : (2 * n + 2) * rows]
        keep_ref[n] = jnp.where(core, even, odd)
        send_ref[n] = jnp.where(core, odd, even).astype(BF16)


def weight_terms(samples, core, parts, sums):
    pieces = len(parts)
    rows, both = sums[0].shape
    width = both // 2
    features = parts[0].shape[1] - width
    half = (samples // 2, features // samples, width)
    return pl.pallas_call(
        functools.partial(weight_kernel, pieces),
        in_specs=[pl.BlockSpec(memory_space=pltpu.SMEM)] + [VMEM] * (2 * pieces),
        out_specs=[VMEM] * 3,
        out_shape=[
            jax.ShapeDtypeStruct((rows, width), BF16),
            jax.ShapeDtypeStruct(half, F32),
            jax.ShapeDtypeStruct(half, BF16),
        ],
        compiler_params=pltpu.CompilerParams(vmem_limit_bytes=32 * MIB),
        name="weight_terms",
    )(core, *parts, *sums)


def halve_kernel(bit_ref, kept_ref, came_ref, keep_ref, send_ref):
    low = bit_ref[0] == 0
    for n in range(keep_ref.shape[0]):
        even = kept_ref[2 * n] + came_ref[2 * n].astype(F32)
        odd = kept_ref[2 * n + 1] + came_ref[2 * n + 1].astype(F32)
        keep_ref[n] = jnp.where(low, even, odd)
        send_ref[n] = jnp.where(low, odd, even).astype(BF16)


def halve(bit, kept, came):
    half = (kept.shape[0] // 2, *kept.shape[1:])
    return pl.pallas_call(
        halve_kernel,
        in_specs=[pl.BlockSpec(memory_space=pltpu.SMEM), VMEM, VMEM],
        out_specs=[VMEM] * 2,
        out_shape=[jax.ShapeDtypeStruct(half, F32), jax.ShapeDtypeStruct(half, BF16)],
        compiler_params=pltpu.CompilerParams(vmem_limit_bytes=32 * MIB),
        name="halve",
    )(bit, kept, came)


def local(visual_rows, value_matrix, key_weight, queries, output_gradient, visual_len, frame_end):
    blocks, samples = lax.axis_size("blk"), lax.axis_size("dp")
    sample = lax.axis_index("dp").astype(jnp.int32)
    visual = visual_rows[0]

    def from_partners(pieces):
        came = {m: swap(pieces[m], "blk", partner(m, blocks)) for m in reversed(range(1, blocks))}
        return [pieces[0]] + [came[m] for m in range(1, blocks)]

    keys_values = from_partners([project(visual, key_weight, value_matrix[0])] * blocks)
    attention = Attention(queries[0], blocks, visual.shape[0])
    inner, key_terms = attention.scores(
        visual_len, frame_end, queries[0], output_gradient[0], visual, keys_values
    )
    weights, dscores, keys, values = inner
    parts = from_partners(key_terms)
    parts[1], weights = lax.optimization_barrier((parts[1], weights))
    attn_out, value_terms = attention.values(output_gradient[0], weights, values)
    sums = from_partners(sum_terms(parts, value_terms))
    sums[1], dscores = lax.optimization_barrier((sums[1], dscores))
    query_grad = attention.queries(dscores, keys)
    value_grad, kept, sent = weight_terms(samples, (sample % 2)[None], parts, sums)
    came, bit = swap(sent, "dp", 1), 1
    while kept.shape[0] > 1:
        kept, sent = halve(((sample >> bit) % 2)[None], kept, came)
        came, bit = swap(sent, "dp", 1 << bit), bit + 1
    came, query_grad = lax.optimization_barrier((came, query_grad))
    weight_grad = kept[0] + came[0].astype(F32)
    return attn_out[None], query_grad[None], value_grad[None], weight_grad


def solution(mesh):
    return jax.shard_map(
        local,
        mesh=mesh,
        in_specs=(
            P("dp", "blk", None),
            P("dp", "blk", None),
            P(),
            P("dp", "blk", None),
            P("dp", "blk", None),
            P("dp"),
            P("dp", None),
        ),
        out_specs=(
            P("dp", "blk", None),
            P("dp", "blk", None),
            P("dp", "blk", None),
            P(("blk", "dp"), None),
        ),
        check_vma=False,
    )
```

```python
import functools

import jax
import jax.numpy as jnp
from jax import lax
from jax.experimental import pallas as pl
from jax.experimental.pallas import tpu as pltpu
from jax.sharding import PartitionSpec as P

KEY_HEADS = 4
HEAD_SIZE = 128
TILE = 128
HEADS_PER_KEY = 8
LOG2_E = 1.4426950408889634
NEGATIVE_FILLER = -1e30
F32 = jnp.float32
BF16 = jnp.bfloat16
MIB = 1024 * 1024
VMEM = pl.BlockSpec(memory_space=pltpu.VMEM)


def dot(a, b, contract=((1,), (0,))):
    return lax.dot_general(a, b, (contract, ((), ())), preferred_element_type=F32)


def swap(x, axis, mask):
    size = lax.axis_size(axis)
    return lax.ppermute(x, axis, [(i, i ^ mask) for i in range(size)])


def in_hbm(x):
    return pltpu.with_memory_space_constraint(x, pltpu.HBM)


def partner(piece, pieces):
    return (pieces - piece) % pieces


def term_order(pieces):
    order = [partner(p, pieces) for p in range(pieces)]
    return order[:2] + order[-2:] + order[2:-2] if pieces > 4 else order


def project_kernel(streams, visual_ref, *refs):
    weight_refs, value_ref, out_ref, acc_ref = refs[:streams], *refs[streams:]
    step = pl.program_id(0)
    slab = weight_refs[0].shape[0]
    part = dot(visual_ref[:, :slab], weight_refs[0][...])
    for p in range(1, streams):
        part += dot(visual_ref[:, p * slab : (p + 1) * slab], weight_refs[p][...])

    @pl.when(step == 0)
    def _():
        acc_ref[...] = part

    @pl.when(step > 0)
    def _():
        acc_ref[...] += part

    @pl.when(step == pl.num_programs(0) - 1)
    def _():
        columns = acc_ref.shape[1]
        out_ref[:, :columns] = acc_ref[...].astype(BF16)
        out_ref[:, columns:] = value_ref[...]


def project(visual, key_weight, value):
    rows, features = visual.shape
    columns = key_weight.shape[1]
    steps, streams = 2, 4
    slab = features // (steps * streams)
    out = (rows, columns + value.shape[1])
    return pl.pallas_call(
        functools.partial(project_kernel, streams),
        grid=(steps,),
        in_specs=[pl.BlockSpec((rows, streams * slab), lambda k: (0, k))]
        + [
            pl.BlockSpec((slab, columns), lambda k, p=p: (k * streams + p, 0))
            for p in range(streams)
        ]
        + [pl.BlockSpec(value.shape, lambda k: (0, 0))],
        out_specs=pl.BlockSpec(out, lambda k: (0, 0)),
        out_shape=jax.ShapeDtypeStruct(out, BF16),
        scratch_shapes=[pltpu.VMEM((rows, columns), F32)],
        cost_estimate=pl.CostEstimate(
            flops=2 * rows * features * columns,
            bytes_accessed=2 * features * columns,
            transcendentals=0,
        ),
        compiler_params=pltpu.CompilerParams(vmem_limit_bytes=32 * MIB),
        name="project",
    )(in_hbm(visual), *[in_hbm(key_weight)] * streams, in_hbm(value))


def head_pair(ref, rows, start):
    first = pl.ds(pl.multiple_of(start, HEAD_SIZE), HEAD_SIZE)
    second = pl.ds(pl.multiple_of(start + HEAD_SIZE, HEAD_SIZE), HEAD_SIZE)
    return jnp.concatenate([ref[rows, first], ref[rows, second]], axis=0)


def scores_kernel(pieces, length_ref, frame_ref, q_ref, g_ref, visual_hbm, *refs):
    kv_refs, (w_ref, again_ref, ds_ref, k_ref, v_ref) = refs[:pieces], refs[pieces : pieces + 5]
    key_refs = refs[pieces + 5 : 2 * pieces + 5]
    kg_acc, bias_ref, visual, sem = refs[2 * pieces + 5 :]
    copy = pltpu.make_async_copy(visual_hbm, visual, sem)
    copy.start()
    block = lax.axis_index("blk")
    tiles = q_ref.shape[0] // TILE
    rows = kv_refs[0].shape[0]
    width = KEY_HEADS * HEAD_SIZE
    pair = 2 * TILE
    pairs = HEADS_PER_KEY // 2
    span = HEADS_PER_KEY * HEAD_SIZE
    scale = HEAD_SIZE**-0.5
    for m in range(pieces):
        part = slice(m * rows, (m + 1) * rows)
        k_ref[part, :] = kv_refs[m][:, :width]
        v_ref[part, :] = kv_refs[m][:, width:]
    row = lax.broadcasted_iota(jnp.int32, (rows, pair), 0)
    for i in range(tiles):
        text = slice(i * TILE, (i + 1) * TILE)
        limit = jnp.minimum(length_ref[0], TILE * frame_ref[0, block * tiles + i])
        for m in range(pieces):
            live = row + (block ^ partner(m, pieces)) * rows < limit
            bias_ref[m * rows : (m + 1) * rows, :] = jnp.where(live, 0.0, NEGATIVE_FILLER)

        @pl.loop(0, KEY_HEADS)
        def _(j, i=i, text=text):
            head = pl.ds(pl.multiple_of(j * HEAD_SIZE, HEAD_SIZE), HEAD_SIZE)
            keys, values = k_ref[:, head], v_ref[:, head]
            q_stack, raw, dprobs = [], {}, {}

            def products(p):
                start = j * span + p * pair
                q_stack.append(head_pair(q_ref, text, start))
                raw[p] = dot(keys, q_stack[p], ((1,), (1,)))
                dprobs[p] = dot(values, head_pair(g_ref, text, start), ((1,), (1,)))

            products(0)
            ds_stack = []
            for p in range(pairs):
                if p + 1 < pairs:
                    products(p + 1)
                scores = raw.pop(p) + bias_ref[...]
                peak = jnp.max(scores, axis=0, keepdims=True)
                shifted = jnp.exp2((scores - peak) * (scale * LOG2_E))
                terms = shifted * dprobs.pop(p)
                inverse = 1.0 / jnp.sum(shifted, axis=0, keepdims=True)
                slope = inverse * scale
                offset = jnp.sum(terms, axis=0, keepdims=True) * inverse * slope
                start = (i * KEY_HEADS + j) * span + p * pair
                both = pl.ds(pl.multiple_of(start, HEAD_SIZE), pair)
                weights = (shifted * inverse).astype(BF16)
                w_ref[:, both] = weights
                again_ref[:, both] = weights
                ds_stack.append((terms * slope - shifted * offset).astype(BF16))
                ds_ref[:, both] = ds_stack[p]
            kg = dot(jnp.concatenate(ds_stack, axis=1), jnp.concatenate(q_stack, axis=0))
            if i == 0:
                kg_acc[:, head] = kg
            else:
                kg_acc[:, head] += kg

    copy.wait()
    share = visual.shape[1] // pieces
    for ref, other in zip(key_refs, term_order(pieces)):
        start = pl.multiple_of((block ^ other) * share, HEAD_SIZE)
        first = partner(other, pieces) * rows
        ref[:, :width] = kg_acc[first : first + rows, :].astype(BF16)
        ref[:, width:] = visual[:, pl.ds(start, share)]


def values_kernel(pieces, g_ref, w_ref, *refs):
    value_refs, vg_acc = refs[:pieces], refs[pieces]
    j, i = pl.program_id(0), pl.program_id(1)
    head = pl.ds(pl.multiple_of(j * HEAD_SIZE, HEAD_SIZE), HEAD_SIZE)
    rows = value_refs[0].shape[0]
    stack = [g_ref[:, h * HEAD_SIZE : (h + 1) * HEAD_SIZE] for h in range(HEADS_PER_KEY)]
    vg = dot(w_ref[...], jnp.concatenate(stack, axis=0))

    @pl.when(i == 0)
    def _():
        vg_acc[...] = vg

    @pl.when(i > 0)
    def _():
        vg_acc[...] += vg

    @pl.when(i == pl.num_programs(1) - 1)
    def _():
        for m in range(pieces):
            value_refs[m][:, head] = vg_acc[m * rows : (m + 1) * rows, :].astype(BF16)


def store_rows(out_ref, left, inner_ref):
    pair = 2 * TILE
    for p in range(HEADS_PER_KEY // 2):
        out = dot(left, inner_ref[:, p * pair : (p + 1) * pair]).T.astype(BF16)
        out_ref[:, p * pair : p * pair + HEAD_SIZE] = out[:TILE]
        out_ref[:, p * pair + HEAD_SIZE : (p + 1) * pair] = out[TILE:]


def rows_kernel(pieces, inner_ref, head_ref, out_ref):
    store_rows(out_ref, head_ref[...].T, inner_ref)


class Attention:
    def __init__(self, queries, pieces, rows):
        self.pieces, self.rows = pieces, rows
        self.text, self.wide = queries.shape
        self.tiles = self.text // TILE
        self.all_rows = pieces * rows
        self.width = KEY_HEADS * HEAD_SIZE
        span = HEADS_PER_KEY * HEAD_SIZE
        self.text_block = pl.BlockSpec((TILE, span), lambda j, i: (i, j))
        self.inner_block = pl.BlockSpec((self.all_rows, span), lambda j, i: (0, i * KEY_HEADS + j))
        self.head_block = pl.BlockSpec((self.all_rows, HEAD_SIZE), lambda j, i: (0, j))
        self.inner = jax.ShapeDtypeStruct((self.all_rows, self.tiles * self.wide), BF16)

    def call(self, kernel, products, moved, name, **specs):
        return pl.pallas_call(
            functools.partial(kernel, self.pieces),
            cost_estimate=pl.CostEstimate(
                flops=2 * products * self.text * self.all_rows * self.wide,
                bytes_accessed=2 * moved * self.text * self.wide,
                transcendentals=0,
            ),
            compiler_params=pltpu.CompilerParams(vmem_limit_bytes=32 * MIB),
            name=name,
            **specs,
        )

    def scores(self, length, frames, queries, gradients, visual, keys_values):
        smem = pl.BlockSpec(memory_space=pltpu.SMEM)
        hbm = pl.BlockSpec(memory_space=pltpu.HBM)
        columns = self.width + visual.shape[1] // self.pieces
        piece = jax.ShapeDtypeStruct((self.rows, columns), BF16)
        heads = jax.ShapeDtypeStruct((self.all_rows, self.width), BF16)
        out = self.call(
            scores_kernel,
            6,
            4,
            "scores",
            in_specs=[smem, smem, VMEM, VMEM, hbm] + [VMEM] * self.pieces,
            out_specs=[VMEM] * (5 + self.pieces),
            out_shape=[self.inner] * 3 + [heads] * 2 + [piece] * self.pieces,
            scratch_shapes=[
                pltpu.VMEM((self.all_rows, self.width), F32),
                pltpu.VMEM((self.all_rows, 2 * TILE), F32),
                pltpu.VMEM(visual.shape, BF16),
                pltpu.SemaphoreType.DMA,
            ],
        )(length, frames, queries, gradients, in_hbm(visual), *keys_values)
        return out[:5], out[5:]

    def values(self, gradients, weights):
        piece = jax.ShapeDtypeStruct((self.rows, self.width), BF16)
        return self.call(
            values_kernel,
            1,
            2,
            "values",
            grid=(KEY_HEADS, self.tiles),
            in_specs=[self.text_block, self.inner_block],
            out_specs=[pl.BlockSpec((self.rows, self.width), lambda j, i: (0, 0))] * self.pieces,
            out_shape=[piece] * self.pieces,
            scratch_shapes=[pltpu.VMEM((self.all_rows, HEAD_SIZE), F32)],
        )(in_hbm(gradients), weights)

    def over_rows(self, inner, heads, name):
        return self.call(
            rows_kernel,
            1,
            3,
            name,
            grid=(KEY_HEADS, self.tiles),
            in_specs=[self.inner_block, self.head_block],
            out_specs=self.text_block,
            out_shape=jax.ShapeDtypeStruct((self.text, self.wide), BF16),
        )(inner, heads)


def sum_kernel(pieces, *refs):
    part_refs, value_refs = refs[:pieces], refs[pieces : 2 * pieces]
    visual_ref, out_refs = refs[2 * pieces], refs[2 * pieces + 1 :]
    rows, width = value_refs[0].shape
    total = part_refs[0][:, :width].astype(F32)
    for ref in part_refs[1:]:
        total += ref[:, :width].astype(F32)
    own = total.astype(BF16)
    for ref, other in zip(part_refs, term_order(pieces)):
        first = partner(other, pieces) * rows
        visual_ref[first : first + rows, :] = ref[:, width:]
    for m in range(pieces):
        out_refs[m][:, :width] = own
        out_refs[m][:, width:] = value_refs[m][...]


def sum_terms(parts, value_terms):
    pieces = len(parts)
    rows, width = value_terms[0].shape
    visual = (pieces * rows, parts[0].shape[1] - width)
    out = pl.pallas_call(
        functools.partial(sum_kernel, pieces),
        in_specs=[VMEM] * (2 * pieces),
        out_specs=[VMEM] * (1 + pieces),
        out_shape=[jax.ShapeDtypeStruct(visual, BF16)]
        + [jax.ShapeDtypeStruct((rows, 2 * width), BF16)] * pieces,
        compiler_params=pltpu.CompilerParams(vmem_limit_bytes=32 * MIB),
        name="sum_terms",
    )(*parts, *value_terms)
    return out[0], out[1:]


def turn_kernel(in_ref, out_ref):
    out_ref[...] = in_ref[...].T


def turn(x):
    return pl.pallas_call(
        turn_kernel,
        in_specs=[VMEM],
        out_specs=VMEM,
        out_shape=jax.ShapeDtypeStruct(x.shape[::-1], x.dtype),
        compiler_params=pltpu.CompilerParams(vmem_limit_bytes=32 * MIB),
        name="turn",
    )(x)


def weight_kernel(pieces, core_ref, visual_ref, *refs):
    sum_refs, (value_ref, keep_ref, send_ref) = refs[:pieces], refs[pieces:]
    width = value_ref.shape[1]
    total = sum_refs[0][:, width:].astype(F32)
    for ref in sum_refs[1:]:
        total += ref[:, width:].astype(F32)
    value_ref[...] = total.astype(BF16)
    product = dot(visual_ref[...], jnp.concatenate([r[:, :width] for r in sum_refs], axis=0))
    count, rows, _ = keep_ref.shape
    core = core_ref[0] == 0
    for n in range(count):
        even = product[2 * n * rows : (2 * n + 1) * rows]
        odd = product[(2 * n + 1) * rows : (2 * n + 2) * rows]
        keep_ref[n] = jnp.where(core, even, odd)
        send_ref[n] = jnp.where(core, odd, even).astype(BF16)


def weight_terms(samples, core, visual, sums):
    pieces = len(sums)
    rows, both = sums[0].shape
    width = both // 2
    half = (samples // 2, visual.shape[0] // samples, width)
    return pl.pallas_call(
        functools.partial(weight_kernel, pieces),
        in_specs=[pl.BlockSpec(memory_space=pltpu.SMEM)] + [VMEM] * (1 + pieces),
        out_specs=[VMEM] * 3,
        out_shape=[
            jax.ShapeDtypeStruct((rows, width), BF16),
            jax.ShapeDtypeStruct(half, F32),
            jax.ShapeDtypeStruct(half, BF16),
        ],
        compiler_params=pltpu.CompilerParams(vmem_limit_bytes=32 * MIB),
        name="weight_terms",
    )(core, visual, *sums)


def halve_kernel(bit_ref, kept_ref, came_ref, keep_ref, send_ref):
    low = bit_ref[0] == 0
    for n in range(keep_ref.shape[0]):
        even = kept_ref[2 * n] + came_ref[2 * n].astype(F32)
        odd = kept_ref[2 * n + 1] + came_ref[2 * n + 1].astype(F32)
        keep_ref[n] = jnp.where(low, even, odd)
        send_ref[n] = jnp.where(low, odd, even).astype(BF16)


def halve(bit, kept, came):
    half = (kept.shape[0] // 2, *kept.shape[1:])
    return pl.pallas_call(
        halve_kernel,
        in_specs=[pl.BlockSpec(memory_space=pltpu.SMEM), VMEM, VMEM],
        out_specs=[VMEM] * 2,
        out_shape=[jax.ShapeDtypeStruct(half, F32), jax.ShapeDtypeStruct(half, BF16)],
        compiler_params=pltpu.CompilerParams(vmem_limit_bytes=32 * MIB),
        name="halve",
    )(bit, kept, came)


def local(visual_rows, value_matrix, key_weight, queries, output_gradient, visual_len, frame_end):
    blocks, samples = lax.axis_size("blk"), lax.axis_size("dp")
    sample = lax.axis_index("dp").astype(jnp.int32)
    visual = visual_rows[0]

    order = [partner(p, blocks) for p in range(blocks)]

    def from_partners(pieces, order=order):
        came = {p: swap(pieces[p], "blk", order[p]) for p in reversed(range(1, blocks))}
        return [pieces[0]] + [came[p] for p in range(1, blocks)]

    keys_values = from_partners([project(visual, key_weight, value_matrix[0])] * blocks)
    attention = Attention(queries[0], blocks, visual.shape[0])
    inner, key_terms = attention.scores(
        visual_len, frame_end, queries[0], output_gradient[0], visual, keys_values
    )
    weights, again, dscores, keys, values = inner
    parts = from_partners(key_terms, term_order(blocks))
    parts[1], weights = lax.optimization_barrier((parts[1], weights))
    value_terms = attention.values(output_gradient[0], weights)
    visual_columns, sums = sum_terms(parts, value_terms)
    sums = from_partners(sums)
    sums[1], again, dscores, visual_columns = lax.optimization_barrier(
        (sums[1], again, dscores, visual_columns)
    )
    visual_columns = turn(visual_columns)
    attn_out = attention.over_rows(again, values, "output")
    visual_columns, attn_out = lax.optimization_barrier((visual_columns, attn_out))
    query_grad = attention.over_rows(dscores, keys, "query_grad")
    value_grad, kept, sent = weight_terms(samples, (sample % 2)[None], visual_columns, sums)
    came, bit = swap(sent, "dp", 1), 1
    while kept.shape[0] > 1:
        kept, sent = halve(((sample >> bit) % 2)[None], kept, came)
        came, bit = swap(sent, "dp", 1 << bit), bit + 1
    came, query_grad = lax.optimization_barrier((came, query_grad))
    weight_grad = kept[0] + came[0].astype(F32)
    return attn_out[None], query_grad[None], value_grad[None], weight_grad


def solution(mesh):
    return jax.shard_map(
        local,
        mesh=mesh,
        in_specs=(
            P("dp", "blk", None),
            P("dp", "blk", None),
            P(),
            P("dp", "blk", None),
            P("dp", "blk", None),
            P("dp"),
            P("dp", None),
        ),
        out_specs=(
            P("dp", "blk", None),
            P("dp", "blk", None),
            P("dp", "blk", None),
            P(("blk", "dp"), None),
        ),
        check_vma=False,
    )
```

```python
import functools

import jax
import jax.numpy as jnp
from jax import lax
from jax.experimental import pallas as pl
from jax.experimental.pallas import tpu as pltpu
from jax.sharding import PartitionSpec as P

KEY_HEADS = 4
HEAD_SIZE = 128
TILE = 128
HEADS_PER_KEY = 8
LOG2_E = 1.4426950408889634
NEGATIVE_FILLER = -1e30
F32 = jnp.float32
BF16 = jnp.bfloat16
MIB = 1024 * 1024
VMEM = pl.BlockSpec(memory_space=pltpu.VMEM)


def dot(a, b, contract=((1,), (0,))):
    return lax.dot_general(a, b, (contract, ((), ())), preferred_element_type=F32)


def swap(x, axis, mask):
    size = lax.axis_size(axis)
    return lax.ppermute(x, axis, [(i, i ^ mask) for i in range(size)])


def in_hbm(x):
    return pltpu.with_memory_space_constraint(x, pltpu.HBM)


def gather(own, near=None):
    blocks = lax.axis_size("blk")
    half = blocks // 2
    masks = range(half - 1, 0, -1)
    pieces = {half: swap(own, "blk", half)}
    pieces.update({m: swap(near[m - 1] if near else own, "blk", m) for m in masks})
    pieces.update({m + half: swap(pieces[half], "blk", m) for m in masks})
    pieces[0] = own
    return [pieces[m] for m in range(blocks)]


def near_exchange(pieces):
    return [swap(piece, "blk", m) for m, piece in enumerate(pieces, 1)]


def project_kernel(streams, visual_ref, *refs):
    weight_refs, value_ref = refs[:streams], refs[streams]
    out_ref, own_ref, near_refs = refs[streams + 1], refs[streams + 2], refs[streams + 3 : -1]
    acc_ref = refs[-1]
    step = pl.program_id(0)
    slab = weight_refs[0].shape[0]
    part = 0.0
    for p in range(streams):
        start = pl.multiple_of((step * streams + p) * slab, HEAD_SIZE)
        part += dot(visual_ref[:, pl.ds(start, slab)], weight_refs[p][...])

    @pl.when(step == 0)
    def _():
        acc_ref[...] = part
        block = lax.axis_index("blk")
        half = len(near_refs) + 1
        rows, width = visual_ref.shape[0], own_ref.shape[1]
        for m, ref in enumerate((own_ref, *near_refs)):
            for side in range(2):
                start = pl.multiple_of((block ^ (m + side * half)) * width, HEAD_SIZE)
                ref[side * rows : (side + 1) * rows, :] = visual_ref[:, pl.ds(start, width)]

    @pl.when(step > 0)
    def _():
        acc_ref[...] += part

    @pl.when(step == pl.num_programs(0) - 1)
    def _():
        columns = acc_ref.shape[1]
        out_ref[:, :columns] = acc_ref[...].astype(BF16)
        out_ref[:, columns:] = value_ref[...]


def project(blocks, visual, key_weight, value):
    rows, features = visual.shape
    columns = key_weight.shape[1]
    steps, streams = 2, 4
    slab = features // (steps * streams)
    out = (rows, columns + value.shape[1])
    both = (2 * rows, features // blocks)
    half = blocks // 2

    def whole(shape):
        return pl.BlockSpec(shape, lambda k: (0, 0))

    out = pl.pallas_call(
        functools.partial(project_kernel, streams),
        grid=(steps,),
        in_specs=[whole(visual.shape)]
        + [
            pl.BlockSpec((slab, columns), lambda k, p=p: (k * streams + p, 0))
            for p in range(streams)
        ]
        + [whole(value.shape)],
        out_specs=[whole(out)] + [whole(both)] * half,
        out_shape=[jax.ShapeDtypeStruct(out, BF16)] + [jax.ShapeDtypeStruct(both, BF16)] * half,
        scratch_shapes=[pltpu.VMEM((rows, columns), F32)],
        cost_estimate=pl.CostEstimate(
            flops=2 * rows * features * columns,
            bytes_accessed=2 * features * columns,
            transcendentals=0,
        ),
        compiler_params=pltpu.CompilerParams(vmem_limit_bytes=32 * MIB),
        name="project",
    )(in_hbm(visual), *[in_hbm(key_weight)] * streams, in_hbm(value))
    return out[0], out[1], out[2:]


def head_pair(ref, rows, start):
    first = pl.ds(pl.multiple_of(start, HEAD_SIZE), HEAD_SIZE)
    second = pl.ds(pl.multiple_of(start + HEAD_SIZE, HEAD_SIZE), HEAD_SIZE)
    return jnp.concatenate([ref[rows, first], ref[rows, second]], axis=0)


def store_sides(own_ref, near_refs, terms, columns):
    half = len(near_refs) + 1
    rows = own_ref.shape[0] // 2
    for m, ref in enumerate((own_ref, *near_refs)):
        for side in range(2):
            first = (m + side * half) * rows
            part = terms[first : first + rows, :].astype(ref.dtype)
            ref[side * rows : (side + 1) * rows, columns] = part


def scores_kernel(pieces, length_ref, frame_ref, q_ref, g_ref, *refs):
    kv_refs, (w_ref, again_ref, ds_ref, k_ref, v_ref) = refs[:pieces], refs[pieces : pieces + 5]
    own_ref, near_refs, (kg_acc, bias_ref) = refs[pieces + 5], refs[pieces + 6 : -2], refs[-2:]
    block = lax.axis_index("blk")
    tiles = q_ref.shape[0] // TILE
    rows = kv_refs[0].shape[0]
    width = KEY_HEADS * HEAD_SIZE
    pair = 2 * TILE
    pairs = HEADS_PER_KEY // 2
    span = HEADS_PER_KEY * HEAD_SIZE
    scale = HEAD_SIZE**-0.5
    for m in range(pieces):
        part = slice(m * rows, (m + 1) * rows)
        k_ref[part, :] = kv_refs[m][:, :width]
        v_ref[part, :] = kv_refs[m][:, width:]
    row = lax.broadcasted_iota(jnp.int32, (rows, pair), 0)
    for i in range(tiles):
        text = slice(i * TILE, (i + 1) * TILE)
        limit = jnp.minimum(length_ref[0], TILE * frame_ref[0, block * tiles + i])
        for m in range(pieces):
            live = row + (block ^ m) * rows < limit
            bias_ref[m * rows : (m + 1) * rows, :] = jnp.where(live, 0.0, NEGATIVE_FILLER)

        @pl.loop(0, KEY_HEADS)
        def _(j, i=i, text=text):
            head = pl.ds(pl.multiple_of(j * HEAD_SIZE, HEAD_SIZE), HEAD_SIZE)
            keys, values = k_ref[:, head], v_ref[:, head]
            q_stack, raw, dprobs = [], {}, {}

            def products(p):
                start = j * span + p * pair
                q_stack.append(head_pair(q_ref, text, start))
                raw[p] = dot(keys, q_stack[p], ((1,), (1,)))
                dprobs[p] = dot(values, head_pair(g_ref, text, start), ((1,), (1,)))

            products(0)
            ds_stack = []
            for p in range(pairs):
                if p + 1 < pairs:
                    products(p + 1)
                scores = raw.pop(p) + bias_ref[...]
                peak = jnp.max(scores, axis=0, keepdims=True)
                shifted = jnp.exp2((scores - peak) * (scale * LOG2_E))
                terms = shifted * dprobs.pop(p)
                inverse = 1.0 / jnp.sum(shifted, axis=0, keepdims=True)
                slope = inverse * scale
                offset = jnp.sum(terms, axis=0, keepdims=True) * inverse * slope
                start = (i * KEY_HEADS + j) * span + p * pair
                both = pl.ds(pl.multiple_of(start, HEAD_SIZE), pair)
                weights = (shifted * inverse).astype(BF16)
                w_ref[:, both] = weights
                again_ref[:, both] = weights
                ds_stack.append((terms * slope - shifted * offset).astype(BF16))
                ds_ref[:, both] = ds_stack[p]
            kg = dot(jnp.concatenate(ds_stack, axis=1), jnp.concatenate(q_stack, axis=0))
            if i == 0:
                kg_acc[:, head] = kg
            else:
                kg_acc[:, head] += kg

    store_sides(own_ref, near_refs, kg_acc, slice(None))


def values_kernel(pieces, g_ref, w_ref, own_ref, *refs):
    near_refs, vg_acc = refs[:-1], refs[-1]
    j, i = pl.program_id(0), pl.program_id(1)
    head = pl.ds(pl.multiple_of(j * HEAD_SIZE, HEAD_SIZE), HEAD_SIZE)
    stack = [g_ref[:, h * HEAD_SIZE : (h + 1) * HEAD_SIZE] for h in range(HEADS_PER_KEY)]
    vg = dot(w_ref[...], jnp.concatenate(stack, axis=0))

    @pl.when(i == 0)
    def _():
        vg_acc[...] = vg

    @pl.when(i > 0)
    def _():
        vg_acc[...] += vg

    @pl.when(i == pl.num_programs(1) - 1)
    def _():
        store_sides(own_ref, near_refs, vg_acc, head)


def store_rows(out_ref, left, inner_ref):
    pair = 2 * TILE
    for p in range(HEADS_PER_KEY // 2):
        out = dot(left, inner_ref[:, p * pair : (p + 1) * pair]).T.astype(BF16)
        out_ref[:, p * pair : p * pair + HEAD_SIZE] = out[:TILE]
        out_ref[:, p * pair + HEAD_SIZE : (p + 1) * pair] = out[TILE:]


def rows_kernel(pieces, inner_ref, head_ref, out_ref):
    store_rows(out_ref, head_ref[...].T, inner_ref)


class Attention:
    def __init__(self, queries, pieces, rows):
        self.pieces, self.rows = pieces, rows
        self.text, self.wide = queries.shape
        self.tiles = self.text // TILE
        self.all_rows = pieces * rows
        self.width = KEY_HEADS * HEAD_SIZE
        span = HEADS_PER_KEY * HEAD_SIZE
        self.text_block = pl.BlockSpec((TILE, span), lambda j, i: (i, j))
        self.inner_block = pl.BlockSpec((self.all_rows, span), lambda j, i: (0, i * KEY_HEADS + j))
        self.head_block = pl.BlockSpec((self.all_rows, HEAD_SIZE), lambda j, i: (0, j))
        self.inner = jax.ShapeDtypeStruct((self.all_rows, self.tiles * self.wide), BF16)
        self.sides = (2 * rows, self.width)
        self.terms = [jax.ShapeDtypeStruct(self.sides, F32)]
        self.terms += [jax.ShapeDtypeStruct(self.sides, BF16)] * (pieces // 2 - 1)

    def call(self, kernel, products, moved, name, **specs):
        return pl.pallas_call(
            functools.partial(kernel, self.pieces),
            cost_estimate=pl.CostEstimate(
                flops=2 * products * self.text * self.all_rows * self.wide,
                bytes_accessed=2 * moved * self.text * self.wide,
                transcendentals=0,
            ),
            compiler_params=pltpu.CompilerParams(vmem_limit_bytes=32 * MIB),
            name=name,
            **specs,
        )

    def scores(self, length, frames, queries, gradients, keys_values):
        smem = pl.BlockSpec(memory_space=pltpu.SMEM)
        heads = jax.ShapeDtypeStruct((self.all_rows, self.width), BF16)
        out = self.call(
            scores_kernel,
            6,
            4,
            "scores",
            in_specs=[smem, smem, VMEM, VMEM] + [VMEM] * self.pieces,
            out_specs=[VMEM] * (5 + len(self.terms)),
            out_shape=[self.inner] * 3 + [heads] * 2 + self.terms,
            scratch_shapes=[
                pltpu.VMEM((self.all_rows, self.width), F32),
                pltpu.VMEM((self.all_rows, 2 * TILE), F32),
            ],
        )(length, frames, queries, gradients, *keys_values)
        return out[:5], out[5], out[6:]

    def values(self, gradients, weights):
        out = self.call(
            values_kernel,
            1,
            2,
            "values",
            grid=(KEY_HEADS, self.tiles),
            in_specs=[self.text_block, self.inner_block],
            out_specs=[pl.BlockSpec(self.sides, lambda j, i: (0, 0))] * len(self.terms),
            out_shape=self.terms,
            scratch_shapes=[pltpu.VMEM((self.all_rows, HEAD_SIZE), F32)],
        )(in_hbm(gradients), weights)
        return out[0], out[1:]

    def over_rows(self, inner, heads, name):
        return self.call(
            rows_kernel,
            1,
            3,
            name,
            grid=(KEY_HEADS, self.tiles),
            in_specs=[self.inner_block, self.head_block],
            out_specs=self.text_block,
            out_shape=jax.ShapeDtypeStruct((self.text, self.wide), BF16),
        )(inner, heads)


def in_vmem(kernel, name, out_shape, *arrays):
    return pl.pallas_call(
        kernel,
        in_specs=[VMEM] * len(arrays),
        out_specs=[VMEM] * len(out_shape),
        out_shape=[jax.ShapeDtypeStruct(*shape) for shape in out_shape],
        compiler_params=pltpu.CompilerParams(vmem_limit_bytes=32 * MIB),
        name=name,
    )(*arrays)


def sum_kernel(own_ref, *refs):
    came_refs, (near_ref, far_ref) = refs[:-2], refs[-2:]
    rows = near_ref.shape[0]
    for ref, part in ((near_ref, slice(0, rows)), (far_ref, slice(rows, 2 * rows))):
        total = own_ref[part, :]
        for came_ref in came_refs:
            total += came_ref[part, :].astype(F32)
        ref[...] = total.astype(ref.dtype)


def near_sums(own, came, name):
    half = (own.shape[0] // 2, own.shape[1])
    return in_vmem(sum_kernel, name, [(half, F32), (half, BF16)], own, *came)


def add_kernel(near_ref, far_ref, *refs):
    value_refs, (own_ref, again_ref), near_refs = (
        refs[: len(refs) // 2 - 1],
        refs[len(refs) // 2 - 1 : len(refs) // 2 + 1],
        refs[len(refs) // 2 + 1 :],
    )
    rows = own_ref.shape[0]
    total = (near_ref[...] + far_ref[...].astype(F32)).astype(BF16)
    own_ref[...] = total
    again_ref[...] = total
    for ref, value_ref in zip(near_refs, value_refs):
        ref[:rows, :] = total
        ref[rows:, :] = value_ref[...]


def add_far(near, far, values):
    rows, width = far.shape
    more = [((rows + v.shape[0], width), BF16) for v in values]
    out = in_vmem(add_kernel, "key_grad", [(far.shape, BF16)] * 2 + more, near, far, *values)
    return out[0], out[1], out[2:]


def add_value_kernel(near_ref, far_ref, out_ref):
    out_ref[...] = (near_ref[...] + far_ref[...].astype(F32)).astype(BF16)


def pack_kernel(*refs):
    in_refs, (near_ref, far_ref) = refs[:-2], refs[-2:]
    rows = in_refs[0].shape[0] // 2
    for m, ref in enumerate(in_refs):
        near_ref[m * rows : (m + 1) * rows, :] = ref[:rows, :]
        far_ref[m * rows : (m + 1) * rows, :] = ref[rows:, :]


def pack(own, came):
    half = ((1 + len(came)) * own.shape[0] // 2, own.shape[1])
    return in_vmem(pack_kernel, "pack_visual", [(half, BF16)] * 2, own, *came)


def turn_kernel(near_ref, far_ref, out_ref):
    out_ref[...] = jnp.concatenate([near_ref[...], far_ref[...]], axis=0).T


def turn(near, far):
    shape = (near.shape[1], 2 * near.shape[0])
    return in_vmem(turn_kernel, "turn_visual", [(shape, BF16)], near, far)[0]


def weight_kernel(order, core_ref, visual_ref, value_ref, *refs):
    pieces = len(order)
    kg_refs = [refs[order.index(m)] for m in range(pieces)]
    keep_ref, send_ref, near_ref, far_ref = refs[pieces:]
    rows = near_ref.shape[0]
    product = dot(visual_ref[...], jnp.concatenate([r[:rows, :] for r in kg_refs], axis=0))
    count, share, _ = keep_ref.shape
    core = core_ref[0] == 0
    for n in range(count):
        even = product[2 * n * share : (2 * n + 1) * share]
        odd = product[(2 * n + 1) * share : (2 * n + 2) * share]
        keep_ref[n] = jnp.where(core, even, odd)
        send_ref[n] = jnp.where(core, odd, even).astype(BF16)
    for side, ref in enumerate((near_ref, far_ref)):
        total = value_ref[side * rows : (side + 1) * rows, :]
        for kg_ref in kg_refs[1 : pieces // 2]:
            total += kg_ref[(1 + side) * rows : (2 + side) * rows, :].astype(F32)
        ref[...] = total.astype(ref.dtype)


def weight_terms(samples, core, visual, value_own, key_grads):
    rows, width = key_grads[0].shape
    half = (samples // 2, visual.shape[0] // samples, width)
    middle = len(key_grads) // 2
    order = [0, *range(middle - 1, 0, -1), *range(middle + 1, 2 * middle), middle]
    return pl.pallas_call(
        functools.partial(weight_kernel, order),
        in_specs=[pl.BlockSpec(memory_space=pltpu.SMEM)] + [VMEM] * (2 + len(key_grads)),
        out_specs=[VMEM] * 4,
        out_shape=[
            jax.ShapeDtypeStruct(half, F32),
            jax.ShapeDtypeStruct(half, BF16),
            jax.ShapeDtypeStruct((rows, width), F32),
            jax.ShapeDtypeStruct((rows, width), BF16),
        ],
        compiler_params=pltpu.CompilerParams(vmem_limit_bytes=32 * MIB),
        name="weight_terms",
    )(core, visual, value_own, *[key_grads[m] for m in order])


def halve_kernel(bit_ref, kept_ref, came_ref, keep_ref, send_ref):
    low = bit_ref[0] == 0
    for n in range(keep_ref.shape[0]):
        even = kept_ref[2 * n] + came_ref[2 * n].astype(F32)
        odd = kept_ref[2 * n + 1] + came_ref[2 * n + 1].astype(F32)
        keep_ref[n] = jnp.where(low, even, odd)
        send_ref[n] = jnp.where(low, odd, even).astype(BF16)


def halve(bit, kept, came):
    half = (kept.shape[0] // 2, *kept.shape[1:])
    return pl.pallas_call(
        halve_kernel,
        in_specs=[pl.BlockSpec(memory_space=pltpu.SMEM), VMEM, VMEM],
        out_specs=[VMEM] * 2,
        out_shape=[jax.ShapeDtypeStruct(half, F32), jax.ShapeDtypeStruct(half, BF16)],
        compiler_params=pltpu.CompilerParams(vmem_limit_bytes=32 * MIB),
        name="halve",
    )(bit, kept, came)


def local(visual_rows, value_matrix, key_weight, queries, output_gradient, visual_len, frame_end):
    tie = lax.optimization_barrier
    blocks, samples = lax.axis_size("blk"), lax.axis_size("dp")
    sample = lax.axis_index("dp").astype(jnp.int32)
    visual, half = visual_rows[0], blocks // 2

    own, visual_own, visual_near = project(blocks, visual, key_weight, value_matrix[0])
    keys_values = gather(own)
    keys_values[1], *visual_near = tie((keys_values[1], *visual_near))
    visual_near = near_exchange(visual_near)
    attention = Attention(queries[0], blocks, visual.shape[0])
    inner, key_own, key_near = attention.scores(
        visual_len, frame_end, queries[0], output_gradient[0], keys_values
    )
    weights, again, dscores, keys, values = inner
    key_near, visual_near = tie((key_near, visual_near))

    key_near = near_exchange(key_near)
    value_own, value_near = attention.values(output_gradient[0], weights)
    value_own, visual_own, visual_near = tie((value_own, visual_own, visual_near))
    visual_near, visual_far = pack(visual_own, visual_near)
    visual_far = swap(visual_far, "blk", half)
    key_own, value_own = tie((key_own, value_own))
    key_sum, key_far = near_sums(key_own, key_near, "key_sums")
    key_far = swap(key_far, "blk", half)
    key_grad, key_again, near = add_far(key_sum, key_far, value_near)
    key_grads = gather(key_grad, near)
    key_grads[0] = key_again
    visual_columns = turn(visual_near, visual_far)
    attn_out = attention.over_rows(in_hbm(again), values, "output")
    visual_columns, attn_out, dscores = tie((visual_columns, attn_out, dscores))
    kept, sent, value_sum, value_far = weight_terms(
        samples, (sample % 2)[None], visual_columns, value_own, key_grads
    )
    value_far = swap(value_far, "blk", half)
    query_grad = attention.over_rows(dscores, keys, "query_grad")
    came, bit = swap(sent, "dp", 1), 1
    while kept.shape[0] > 1:
        kept, sent = halve(((sample >> bit) % 2)[None], kept, came)
        came, bit = swap(sent, "dp", 1 << bit), bit + 1
    value_far, query_grad = tie((value_far, query_grad))
    shape = [(value_far.shape, BF16)]
    value_grad = in_vmem(add_value_kernel, "value_grad", shape, value_sum, value_far)[0]
    came, query_grad, value_grad = tie((came, query_grad, value_grad))
    weight_grad = kept[0] + came[0].astype(F32)
    return attn_out[None], query_grad[None], value_grad[None], weight_grad


def solution(mesh):
    return jax.shard_map(
        local,
        mesh=mesh,
        in_specs=(
            P("dp", "blk", None),
            P("dp", "blk", None),
            P(),
            P("dp", "blk", None),
            P("dp", "blk", None),
            P("dp"),
            P("dp", None),
        ),
        out_specs=(
            P("dp", "blk", None),
            P("dp", "blk", None),
            P("dp", "blk", None),
            P(("blk", "dp"), None),
        ),
        check_vma=False,
    )
```

```python
import functools

import jax
import jax.numpy as jnp
from jax import lax
from jax.experimental import pallas as pl
from jax.experimental.pallas import tpu as pltpu
from jax.sharding import PartitionSpec as P

KEY_HEADS = 4
HEAD_SIZE = 128
TILE = 128
HEADS_PER_KEY = 8
LOG2_E = 1.4426950408889634
NEGATIVE_FILLER = -1e30
F32 = jnp.float32
BF16 = jnp.bfloat16
MIB = 1024 * 1024
VMEM = pl.BlockSpec(memory_space=pltpu.VMEM)


def dot(a, b, contract=((1,), (0,))):
    return lax.dot_general(a, b, (contract, ((), ())), preferred_element_type=F32)


def swap(x, axis, mask):
    size = lax.axis_size(axis)
    return lax.ppermute(x, axis, [(i, i ^ mask) for i in range(size)])


def in_hbm(x):
    return pltpu.with_memory_space_constraint(x, pltpu.HBM)


def gather(own, near=None):
    blocks = lax.axis_size("blk")
    half = blocks // 2
    masks = range(half - 1, 0, -1)
    pieces = {half: swap(own, "blk", half)}
    pieces.update({m: swap(near[m - 1] if near else own, "blk", m) for m in masks})
    pieces.update({m + half: swap(pieces[half], "blk", m) for m in masks})
    pieces[0] = own
    return [pieces[m] for m in range(blocks)]


def near_exchange(pieces):
    return [swap(piece, "blk", m) for m, piece in enumerate(pieces, 1)]


def project_kernel(streams, visual_ref, *refs):
    weight_refs, value_ref = refs[:streams], refs[streams]
    out_ref, own_ref, near_refs = refs[streams + 1], refs[streams + 2], refs[streams + 3 : -1]
    acc_ref = refs[-1]
    step = pl.program_id(0)
    slab = weight_refs[0].shape[0]
    part = 0.0
    for p in range(streams):
        start = pl.multiple_of((step * streams + p) * slab, HEAD_SIZE)
        part += dot(visual_ref[:, pl.ds(start, slab)], weight_refs[p][...])

    @pl.when(step == 0)
    def _():
        acc_ref[...] = part
        block = lax.axis_index("blk")
        half = len(near_refs) + 1
        rows, width = visual_ref.shape[0], own_ref.shape[1]
        for m in range(half):
            for side in range(2):
                start = pl.multiple_of((block ^ (m + side * half)) * width, HEAD_SIZE)
                columns = visual_ref[:, pl.ds(start, width)]
                if m == 0:
                    own_ref[side * rows : (side + 1) * rows, :] = columns
                else:
                    first = out_ref.shape[1] + side * width
                    near_refs[m - 1][:, first : first + width] = columns

    @pl.when(step > 0)
    def _():
        acc_ref[...] += part

    @pl.when(step == pl.num_programs(0) - 1)
    def _():
        columns = acc_ref.shape[1]
        keys = acc_ref[...].astype(BF16)
        for ref in (out_ref, *near_refs):
            ref[:, :columns] = keys
            ref[:, columns : out_ref.shape[1]] = value_ref[...]


def project(blocks, visual, key_weight, value):
    rows, features = visual.shape
    columns = key_weight.shape[1]
    steps, streams = 2, 4
    slab = features // (steps * streams)
    width = features // blocks
    out = (rows, columns + value.shape[1])
    shapes = [out, (2 * rows, width)] + [(rows, out[1] + 2 * width)] * (blocks // 2 - 1)

    def whole(shape):
        return pl.BlockSpec(shape, lambda k: (0, 0))

    out = pl.pallas_call(
        functools.partial(project_kernel, streams),
        grid=(steps,),
        in_specs=[whole(visual.shape)]
        + [
            pl.BlockSpec((slab, columns), lambda k, p=p: (k * streams + p, 0))
            for p in range(streams)
        ]
        + [whole(value.shape)],
        out_specs=[whole(shape) for shape in shapes],
        out_shape=[jax.ShapeDtypeStruct(shape, BF16) for shape in shapes],
        scratch_shapes=[pltpu.VMEM((rows, columns), F32)],
        cost_estimate=pl.CostEstimate(
            flops=2 * rows * features * columns,
            bytes_accessed=2 * features * columns,
            transcendentals=0,
        ),
        compiler_params=pltpu.CompilerParams(vmem_limit_bytes=32 * MIB),
        name="project",
    )(in_hbm(visual), *[in_hbm(key_weight)] * streams, in_hbm(value))
    return out[0], out[1], out[2:]


def head_pair(ref, rows, start):
    first = pl.ds(pl.multiple_of(start, HEAD_SIZE), HEAD_SIZE)
    second = pl.ds(pl.multiple_of(start + HEAD_SIZE, HEAD_SIZE), HEAD_SIZE)
    return jnp.concatenate([ref[rows, first], ref[rows, second]], axis=0)


def store_sides(own_ref, near_refs, terms, columns):
    half = len(near_refs) + 1
    rows = own_ref.shape[0] // 2
    for m, ref in enumerate((own_ref, *near_refs)):
        for side in range(2):
            first = (m + side * half) * rows
            part = terms[first : first + rows, :].astype(ref.dtype)
            ref[side * rows : (side + 1) * rows, columns] = part


def scores_kernel(pieces, length_ref, frame_ref, q_ref, g_ref, *refs):
    kv_refs, (w_ref, again_ref, ds_ref, k_ref, v_ref) = refs[:pieces], refs[pieces : pieces + 5]
    own_ref, near_refs, (kg_acc, bias_ref) = refs[pieces + 5], refs[pieces + 6 : -2], refs[-2:]
    block = lax.axis_index("blk")
    tiles = q_ref.shape[0] // TILE
    rows = kv_refs[0].shape[0]
    width = KEY_HEADS * HEAD_SIZE
    pair = 2 * TILE
    pairs = HEADS_PER_KEY // 2
    span = HEADS_PER_KEY * HEAD_SIZE
    scale = HEAD_SIZE**-0.5
    for m in range(pieces):
        part = slice(m * rows, (m + 1) * rows)
        k_ref[part, :] = kv_refs[m][:, :width]
        v_ref[part, :] = kv_refs[m][:, width : 2 * width]
    row = lax.broadcasted_iota(jnp.int32, (rows, pair), 0)
    for i in range(tiles):
        text = slice(i * TILE, (i + 1) * TILE)
        limit = jnp.minimum(length_ref[0], TILE * frame_ref[0, block * tiles + i])
        for m in range(pieces):
            live = row + (block ^ m) * rows < limit
            bias_ref[m * rows : (m + 1) * rows, :] = jnp.where(live, 0.0, NEGATIVE_FILLER)

        @pl.loop(0, KEY_HEADS)
        def _(j, i=i, text=text):
            head = pl.ds(pl.multiple_of(j * HEAD_SIZE, HEAD_SIZE), HEAD_SIZE)
            keys, values = k_ref[:, head], v_ref[:, head]
            q_stack, raw, dprobs = [], {}, {}

            def products(p):
                start = j * span + p * pair
                q_stack.append(head_pair(q_ref, text, start))
                raw[p] = dot(keys, q_stack[p], ((1,), (1,)))
                dprobs[p] = dot(values, head_pair(g_ref, text, start), ((1,), (1,)))

            products(0)
            ds_stack = []
            for p in range(pairs):
                if p + 1 < pairs:
                    products(p + 1)
                scores = raw.pop(p) + bias_ref[...]
                peak = jnp.max(scores, axis=0, keepdims=True)
                shifted = jnp.exp2((scores - peak) * (scale * LOG2_E))
                terms = shifted * dprobs.pop(p)
                inverse = 1.0 / jnp.sum(shifted, axis=0, keepdims=True)
                slope = inverse * scale
                offset = jnp.sum(terms, axis=0, keepdims=True) * inverse * slope
                start = (i * KEY_HEADS + j) * span + p * pair
                both = pl.ds(pl.multiple_of(start, HEAD_SIZE), pair)
                weights = (shifted * inverse).astype(BF16)
                w_ref[:, both] = weights
                again_ref[:, both] = weights
                ds_stack.append((terms * slope - shifted * offset).astype(BF16))
                ds_ref[:, both] = ds_stack[p]
            kg = dot(jnp.concatenate(ds_stack, axis=1), jnp.concatenate(q_stack, axis=0))
            if i == 0:
                kg_acc[:, head] = kg
            else:
                kg_acc[:, head] += kg

    store_sides(own_ref, near_refs, kg_acc, slice(None))


def values_kernel(pieces, g_ref, w_ref, own_ref, *refs):
    near_refs, vg_acc = refs[:-1], refs[-1]
    j, i = pl.program_id(0), pl.program_id(1)
    head = pl.ds(pl.multiple_of(j * HEAD_SIZE, HEAD_SIZE), HEAD_SIZE)
    stack = [g_ref[:, h * HEAD_SIZE : (h + 1) * HEAD_SIZE] for h in range(HEADS_PER_KEY)]
    vg = dot(w_ref[...], jnp.concatenate(stack, axis=0))

    @pl.when(i == 0)
    def _():
        vg_acc[...] = vg

    @pl.when(i > 0)
    def _():
        vg_acc[...] += vg

    @pl.when(i == pl.num_programs(1) - 1)
    def _():
        store_sides(own_ref, near_refs, vg_acc, head)


def store_rows(out_ref, left, inner_ref):
    pair = 2 * TILE
    for p in range(HEADS_PER_KEY // 2):
        out = dot(left, inner_ref[:, p * pair : (p + 1) * pair]).T.astype(BF16)
        out_ref[:, p * pair : p * pair + HEAD_SIZE] = out[:TILE]
        out_ref[:, p * pair + HEAD_SIZE : (p + 1) * pair] = out[TILE:]


def rows_kernel(pieces, inner_ref, head_ref, out_ref):
    store_rows(out_ref, head_ref[...].T, inner_ref)


class Attention:
    def __init__(self, queries, pieces, rows):
        self.pieces, self.rows = pieces, rows
        self.text, self.wide = queries.shape
        self.tiles = self.text // TILE
        self.all_rows = pieces * rows
        self.width = KEY_HEADS * HEAD_SIZE
        span = HEADS_PER_KEY * HEAD_SIZE
        self.text_block = pl.BlockSpec((TILE, span), lambda j, i: (i, j))
        self.inner_block = pl.BlockSpec((self.all_rows, span), lambda j, i: (0, i * KEY_HEADS + j))
        self.head_block = pl.BlockSpec((self.all_rows, HEAD_SIZE), lambda j, i: (0, j))
        self.inner = jax.ShapeDtypeStruct((self.all_rows, self.tiles * self.wide), BF16)
        self.sides = (2 * rows, self.width)
        self.terms = [jax.ShapeDtypeStruct(self.sides, F32)]
        self.terms += [jax.ShapeDtypeStruct(self.sides, BF16)] * (pieces // 2 - 1)

    def call(self, kernel, share, name, **specs):
        return pl.pallas_call(
            functools.partial(kernel, self.pieces),
            cost_estimate=pl.CostEstimate(
                flops=int(share * 12 * self.text * self.all_rows * self.wide),
                bytes_accessed=int(share * 8 * self.text * self.wide),
                transcendentals=0,
            ),
            compiler_params=pltpu.CompilerParams(vmem_limit_bytes=32 * MIB),
            name=name,
            **specs,
        )

    def scores(self, length, frames, queries, gradients, keys_values):
        smem = pl.BlockSpec(memory_space=pltpu.SMEM)
        heads = jax.ShapeDtypeStruct((self.all_rows, self.width), BF16)
        out = self.call(
            scores_kernel,
            1.0,
            "scores",
            in_specs=[smem, smem, VMEM, VMEM] + [VMEM] * self.pieces,
            out_specs=[VMEM] * (5 + len(self.terms)),
            out_shape=[self.inner] * 3 + [heads] * 2 + self.terms,
            scratch_shapes=[
                pltpu.VMEM((self.all_rows, self.width), F32),
                pltpu.VMEM((self.all_rows, 2 * TILE), F32),
            ],
        )(length, frames, queries, gradients, *keys_values)
        return out[:5], out[5], out[6:]

    def values(self, gradients, weights):
        out = self.call(
            values_kernel,
            0.03,
            "values",
            grid=(KEY_HEADS, self.tiles),
            in_specs=[self.text_block, self.inner_block],
            out_specs=[pl.BlockSpec(self.sides, lambda j, i: (0, 0))] * len(self.terms),
            out_shape=self.terms,
            scratch_shapes=[pltpu.VMEM((self.all_rows, HEAD_SIZE), F32)],
        )(in_hbm(gradients), weights)
        return out[0], out[1:]

    def over_rows(self, inner, heads, name):
        return self.call(
            rows_kernel,
            0.03,
            name,
            grid=(KEY_HEADS, self.tiles),
            in_specs=[self.inner_block, self.head_block],
            out_specs=self.text_block,
            out_shape=jax.ShapeDtypeStruct((self.text, self.wide), BF16),
        )(inner, heads)


def in_vmem(kernel, name, out_shape, *arrays):
    return pl.pallas_call(
        kernel,
        in_specs=[VMEM] * len(arrays),
        out_specs=[VMEM] * len(out_shape),
        out_shape=[jax.ShapeDtypeStruct(*shape) for shape in out_shape],
        compiler_params=pltpu.CompilerParams(vmem_limit_bytes=32 * MIB),
        name=name,
    )(*arrays)


def sum_kernel(own_ref, *refs):
    came_refs, (near_ref, far_ref) = refs[:-2], refs[-2:]
    rows = near_ref.shape[0]
    for ref, part in ((near_ref, slice(0, rows)), (far_ref, slice(rows, 2 * rows))):
        total = own_ref[part, :]
        for came_ref in came_refs:
            total += came_ref[part, :].astype(F32)
        ref[...] = total.astype(ref.dtype)


def near_sums(own, came, name):
    half = (own.shape[0] // 2, own.shape[1])
    return in_vmem(sum_kernel, name, [(half, F32), (half, BF16)], own, *came)


def add_kernel(near_ref, far_ref, *refs):
    value_refs, (own_ref, again_ref), near_refs = (
        refs[: len(refs) // 2 - 1],
        refs[len(refs) // 2 - 1 : len(refs) // 2 + 1],
        refs[len(refs) // 2 + 1 :],
    )
    rows = own_ref.shape[0]
    total = (near_ref[...] + far_ref[...].astype(F32)).astype(BF16)
    own_ref[...] = total
    again_ref[...] = total
    for ref, value_ref in zip(near_refs, value_refs):
        ref[:rows, :] = total
        ref[rows:, :] = value_ref[...]


def add_far(near, far, values):
    rows, width = far.shape
    more = [((rows + v.shape[0], width), BF16) for v in values]
    out = in_vmem(add_kernel, "key_grad", [(far.shape, BF16)] * 2 + more, near, far, *values)
    return out[0], out[1], out[2:]


def add_value_kernel(near_ref, far_ref, out_ref):
    out_ref[...] = (near_ref[...] + far_ref[...].astype(F32)).astype(BF16)


def pack_kernel(own_ref, *refs):
    came_refs, out_refs = refs[:-2], refs[-2:]
    rows, width = own_ref.shape[0] // 2, own_ref.shape[1]
    for side, ref in enumerate(out_refs):
        ref[:rows, :] = own_ref[side * rows : (side + 1) * rows, :]
        for m, came_ref in enumerate(came_refs, 1):
            first = came_ref.shape[1] - (2 - side) * width
            ref[m * rows : (m + 1) * rows, :] = came_ref[:, first : first + width]


def pack(own, came):
    half = ((1 + len(came)) * own.shape[0] // 2, own.shape[1])
    return in_vmem(pack_kernel, "pack_visual", [(half, BF16)] * 2, own, *came)


def turn_kernel(near_ref, far_ref, out_ref):
    out_ref[...] = jnp.concatenate([near_ref[...], far_ref[...]], axis=0).T


def turn(near, far):
    shape = (near.shape[1], 2 * near.shape[0])
    return in_vmem(turn_kernel, "turn_visual", [(shape, BF16)], near, far)[0]


def weight_kernel(order, core_ref, visual_ref, value_ref, *refs):
    pieces = len(order)
    kg_refs = [refs[order.index(m)] for m in range(pieces)]
    keep_ref, send_ref, near_ref, far_ref = refs[pieces:]
    rows = near_ref.shape[0]
    product = dot(visual_ref[...], jnp.concatenate([r[:rows, :] for r in kg_refs], axis=0))
    count, share, _ = keep_ref.shape
    core = core_ref[0] == 0
    for n in range(count):
        even = product[2 * n * share : (2 * n + 1) * share]
        odd = product[(2 * n + 1) * share : (2 * n + 2) * share]
        keep_ref[n] = jnp.where(core, even, odd)
        send_ref[n] = jnp.where(core, odd, even).astype(BF16)
    for side, ref in enumerate((near_ref, far_ref)):
        total = value_ref[side * rows : (side + 1) * rows, :]
        for kg_ref in kg_refs[1 : pieces // 2]:
            total += kg_ref[(1 + side) * rows : (2 + side) * rows, :].astype(F32)
        ref[...] = total.astype(ref.dtype)


def weight_terms(samples, core, visual, value_own, key_grads):
    rows, width = key_grads[0].shape
    half = (samples // 2, visual.shape[0] // samples, width)
    middle = len(key_grads) // 2
    order = [0, *range(middle - 1, 0, -1), *range(middle + 1, 2 * middle), middle]
    return pl.pallas_call(
        functools.partial(weight_kernel, order),
        in_specs=[pl.BlockSpec(memory_space=pltpu.SMEM)] + [VMEM] * (2 + len(key_grads)),
        out_specs=[VMEM] * 4,
        out_shape=[
            jax.ShapeDtypeStruct(half, F32),
            jax.ShapeDtypeStruct(half, BF16),
            jax.ShapeDtypeStruct((rows, width), F32),
            jax.ShapeDtypeStruct((rows, width), BF16),
        ],
        compiler_params=pltpu.CompilerParams(vmem_limit_bytes=32 * MIB),
        name="weight_terms",
    )(core, visual, value_own, *[key_grads[m] for m in order])


def halve_kernel(bit_ref, kept_ref, came_ref, keep_ref, send_ref):
    low = bit_ref[0] == 0
    for n in range(keep_ref.shape[0]):
        even = kept_ref[2 * n] + came_ref[2 * n].astype(F32)
        odd = kept_ref[2 * n + 1] + came_ref[2 * n + 1].astype(F32)
        keep_ref[n] = jnp.where(low, even, odd)
        send_ref[n] = jnp.where(low, odd, even).astype(BF16)


def halve(bit, kept, came):
    half = (kept.shape[0] // 2, *kept.shape[1:])
    return pl.pallas_call(
        halve_kernel,
        in_specs=[pl.BlockSpec(memory_space=pltpu.SMEM), VMEM, VMEM],
        out_specs=[VMEM] * 2,
        out_shape=[jax.ShapeDtypeStruct(half, F32), jax.ShapeDtypeStruct(half, BF16)],
        compiler_params=pltpu.CompilerParams(vmem_limit_bytes=32 * MIB),
        name="halve",
    )(bit, kept, came)


def local(visual_rows, value_matrix, key_weight, queries, output_gradient, visual_len, frame_end):
    tie = lax.optimization_barrier
    blocks, samples = lax.axis_size("blk"), lax.axis_size("dp")
    sample = lax.axis_index("dp").astype(jnp.int32)
    visual, half = visual_rows[0], blocks // 2

    own, visual_own, near = project(blocks, visual, key_weight, value_matrix[0])
    keys_values = gather(own, near)
    keys_values[half + 1], visual_own = tie((keys_values[half + 1], visual_own))
    visual_near, visual_far = pack(visual_own, keys_values[1:half])
    visual_far = swap(visual_far, "blk", half)
    attention = Attention(queries[0], blocks, visual.shape[0])
    inner, key_own, key_near = attention.scores(
        visual_len, frame_end, queries[0], output_gradient[0], keys_values
    )
    weights, again, dscores, keys, values = inner
    key_near, visual_far = tie((key_near, visual_far))

    key_near = near_exchange(key_near)
    value_own, value_near = attention.values(output_gradient[0], weights)
    key_own, value_own = tie((key_own, value_own))
    key_sum, key_far = near_sums(key_own, key_near, "key_sums")
    key_far = swap(key_far, "blk", half)
    key_grad, key_again, near = add_far(key_sum, key_far, value_near)
    key_grads = gather(key_grad, near)
    key_grads[0] = key_again
    visual_columns = turn(visual_near, visual_far)
    attn_out = attention.over_rows(again, values, "output")
    visual_columns, attn_out, dscores = tie((visual_columns, attn_out, dscores))
    kept, sent, value_sum, value_far = weight_terms(
        samples, (sample % 2)[None], visual_columns, value_own, key_grads
    )
    value_far = swap(value_far, "blk", half)
    query_grad = attention.over_rows(dscores, keys, "query_grad")
    came, bit = swap(sent, "dp", 1), 1
    while kept.shape[0] > 1:
        kept, sent = halve(((sample >> bit) % 2)[None], kept, came)
        came, bit = swap(sent, "dp", 1 << bit), bit + 1
    value_far, query_grad = tie((value_far, query_grad))
    shape = [(value_far.shape, BF16)]
    value_grad = in_vmem(add_value_kernel, "value_grad", shape, value_sum, value_far)[0]
    came, query_grad, value_grad = tie((came, query_grad, value_grad))
    weight_grad = kept[0] + came[0].astype(F32)
    return attn_out[None], query_grad[None], value_grad[None], weight_grad


def solution(mesh):
    return jax.shard_map(
        local,
        mesh=mesh,
        in_specs=(
            P("dp", "blk", None),
            P("dp", "blk", None),
            P(),
            P("dp", "blk", None),
            P("dp", "blk", None),
            P("dp"),
            P("dp", None),
        ),
        out_specs=(
            P("dp", "blk", None),
            P("dp", "blk", None),
            P("dp", "blk", None),
            P(("blk", "dp"), None),
        ),
        check_vma=False,
    )
```

```python
import functools

import jax
import jax.numpy as jnp
from jax import lax
from jax.experimental import pallas as pl
from jax.experimental.pallas import tpu as pltpu
from jax.sharding import PartitionSpec as P

KEY_HEADS = 4
HEAD_SIZE = 128
TILE = 128
HEADS_PER_KEY = 8
LOG2_E = 1.4426950408889634
NEGATIVE_FILLER = -1e30
F32 = jnp.float32
BF16 = jnp.bfloat16
MIB = 1024 * 1024
VMEM = pl.BlockSpec(memory_space=pltpu.VMEM)


def dot(a, b, contract=((1,), (0,))):
    return lax.dot_general(a, b, (contract, ((), ())), preferred_element_type=F32)


def swap(x, axis, mask):
    size = lax.axis_size(axis)
    return lax.ppermute(x, axis, [(i, i ^ mask) for i in range(size)])


def in_hbm(x):
    return pltpu.with_memory_space_constraint(x, pltpu.HBM)


def gather(own, near=None, onward=None):
    blocks = lax.axis_size("blk")
    half = blocks // 2
    masks = range(half - 1, 0, -1)
    far = swap(own, "blk", half)
    pieces = {0: own, half: far}
    pieces.update({m: swap(near[m - 1] if near else own, "blk", m) for m in masks})
    sent = onward(far) if onward else [far] * (half - 1)
    pieces.update({m + half: swap(sent[m - 1], "blk", m) for m in masks})
    return [pieces[m] for m in range(blocks)]


def near_exchange(pieces):
    return [swap(piece, "blk", m) for m, piece in enumerate(pieces, 1)]


def project_kernel(streams, visual_ref, *refs):
    weight_refs, value_ref = refs[:streams], refs[streams]
    out_ref, near_ref, far_ref, acc_ref = refs[streams + 1 :]
    step = pl.program_id(0)
    slab = weight_refs[0].shape[0]
    part = 0.0
    for p in range(streams):
        start = pl.multiple_of((step * streams + p) * slab, HEAD_SIZE)
        part += dot(visual_ref[:, pl.ds(start, slab)], weight_refs[p][...])

    @pl.when(step == 0)
    def _():
        acc_ref[...] = part
        block = lax.axis_index("blk")
        rows, width = visual_ref.shape[0], near_ref.shape[1]
        half = near_ref.shape[0] // rows
        for side, ref in enumerate((near_ref, far_ref)):
            for m in range(half):
                start = pl.multiple_of((block ^ (m + side * half)) * width, HEAD_SIZE)
                ref[m * rows : (m + 1) * rows, :] = visual_ref[:, pl.ds(start, width)]

    @pl.when(step > 0)
    def _():
        acc_ref[...] += part

    @pl.when(step == pl.num_programs(0) - 1)
    def _():
        columns = acc_ref.shape[1]
        out_ref[:, :columns] = acc_ref[...].astype(BF16)
        out_ref[:, columns:] = value_ref[...]


def project(blocks, visual, key_weight, value):
    rows, features = visual.shape
    columns = key_weight.shape[1]
    steps, streams = 2, 4
    slab = features // (steps * streams)
    out = (rows, columns + value.shape[1])
    half = (blocks // 2 * rows, features // blocks)

    def whole(shape):
        return pl.BlockSpec(shape, lambda k: (0, 0))

    out = pl.pallas_call(
        functools.partial(project_kernel, streams),
        grid=(steps,),
        in_specs=[whole(visual.shape)]
        + [
            pl.BlockSpec((slab, columns), lambda k, p=p: (k * streams + p, 0))
            for p in range(streams)
        ]
        + [whole(value.shape)],
        out_specs=[whole(out)] + [whole(half)] * 2,
        out_shape=[jax.ShapeDtypeStruct(out, BF16)] + [jax.ShapeDtypeStruct(half, BF16)] * 2,
        scratch_shapes=[pltpu.VMEM((rows, columns), F32)],
        cost_estimate=pl.CostEstimate(
            flops=2 * rows * features * columns,
            bytes_accessed=2 * features * columns,
            transcendentals=0,
        ),
        compiler_params=pltpu.CompilerParams(vmem_limit_bytes=32 * MIB),
        name="project",
    )(in_hbm(visual), *[in_hbm(key_weight)] * streams, in_hbm(value))
    return out


def head_pair(ref, rows, start):
    first = pl.ds(pl.multiple_of(start, HEAD_SIZE), HEAD_SIZE)
    second = pl.ds(pl.multiple_of(start + HEAD_SIZE, HEAD_SIZE), HEAD_SIZE)
    return jnp.concatenate([ref[rows, first], ref[rows, second]], axis=0)


def store_sides(own_ref, near_refs, terms, columns):
    half = len(near_refs) + 1
    rows = own_ref.shape[0] // 2
    for m, ref in enumerate((own_ref, *near_refs)):
        for side in range(2):
            first = (m + side * half) * rows
            part = terms[first : first + rows, :].astype(ref.dtype)
            ref[side * rows : (side + 1) * rows, columns] = part


def scores_kernel(pieces, length_ref, frame_ref, q_ref, g_ref, *refs):
    kv_refs, (w_ref, again_ref, ds_ref, k_ref, v_ref) = refs[:pieces], refs[pieces : pieces + 5]
    own_ref, near_refs, (kg_acc, bias_ref) = refs[pieces + 5], refs[pieces + 6 : -2], refs[-2:]
    block = lax.axis_index("blk")
    tiles = q_ref.shape[0] // TILE
    rows = kv_refs[0].shape[0]
    width = KEY_HEADS * HEAD_SIZE
    pair = 2 * TILE
    pairs = HEADS_PER_KEY // 2
    span = HEADS_PER_KEY * HEAD_SIZE
    scale = HEAD_SIZE**-0.5
    for m in range(pieces):
        part = slice(m * rows, (m + 1) * rows)
        k_ref[part, :] = kv_refs[m][:, :width]
        v_ref[part, :] = kv_refs[m][:, width:]
    row = lax.broadcasted_iota(jnp.int32, (rows, pair), 0)
    for i in range(tiles):
        text = slice(i * TILE, (i + 1) * TILE)
        limit = jnp.minimum(length_ref[0], TILE * frame_ref[0, block * tiles + i])
        for m in range(pieces):
            live = row + (block ^ m) * rows < limit
            bias_ref[m * rows : (m + 1) * rows, :] = jnp.where(live, 0.0, NEGATIVE_FILLER)

        @pl.loop(0, KEY_HEADS)
        def _(j, i=i, text=text):
            head = pl.ds(pl.multiple_of(j * HEAD_SIZE, HEAD_SIZE), HEAD_SIZE)
            keys, values = k_ref[:, head], v_ref[:, head]
            q_stack, raw, dprobs = [], {}, {}

            def products(p):
                start = j * span + p * pair
                q_stack.append(head_pair(q_ref, text, start))
                raw[p] = dot(keys, q_stack[p], ((1,), (1,)))
                dprobs[p] = dot(values, head_pair(g_ref, text, start), ((1,), (1,)))

            products(0)
            ds_stack = []
            for p in range(pairs):
                if p + 1 < pairs:
                    products(p + 1)
                scores = raw.pop(p) + bias_ref[...]
                peak = jnp.max(scores, axis=0, keepdims=True)
                shifted = jnp.exp2((scores - peak) * (scale * LOG2_E))
                terms = shifted * dprobs.pop(p)
                inverse = 1.0 / jnp.sum(shifted, axis=0, keepdims=True)
                slope = inverse * scale
                offset = jnp.sum(terms, axis=0, keepdims=True) * inverse * slope
                start = (i * KEY_HEADS + j) * span + p * pair
                both = pl.ds(pl.multiple_of(start, HEAD_SIZE), pair)
                weights = (shifted * inverse).astype(BF16)
                w_ref[:, both] = weights
                again_ref[:, both] = weights
                ds_stack.append((terms * slope - shifted * offset).astype(BF16))
                ds_ref[:, both] = ds_stack[p]
            kg = dot(jnp.concatenate(ds_stack, axis=1), jnp.concatenate(q_stack, axis=0))
            if i == 0:
                kg_acc[:, head] = kg
            else:
                kg_acc[:, head] += kg

    store_sides(own_ref, near_refs, kg_acc, slice(None))


def values_kernel(pieces, g_ref, w_ref, own_ref, *refs):
    near_refs, vg_acc = refs[:-1], refs[-1]
    j, i = pl.program_id(0), pl.program_id(1)
    head = pl.ds(pl.multiple_of(j * HEAD_SIZE, HEAD_SIZE), HEAD_SIZE)
    stack = [g_ref[:, h * HEAD_SIZE : (h + 1) * HEAD_SIZE] for h in range(HEADS_PER_KEY)]
    vg = dot(w_ref[...], jnp.concatenate(stack, axis=0))

    @pl.when(i == 0)
    def _():
        vg_acc[...] = vg

    @pl.when(i > 0)
    def _():
        vg_acc[...] += vg

    @pl.when(i == pl.num_programs(1) - 1)
    def _():
        store_sides(own_ref, near_refs, vg_acc, head)


def store_rows(out_ref, left, inner_ref):
    pair = 2 * TILE
    for p in range(HEADS_PER_KEY // 2):
        out = dot(left, inner_ref[:, p * pair : (p + 1) * pair]).T.astype(BF16)
        out_ref[:, p * pair : p * pair + HEAD_SIZE] = out[:TILE]
        out_ref[:, p * pair + HEAD_SIZE : (p + 1) * pair] = out[TILE:]


def rows_kernel(pieces, inner_ref, head_ref, out_ref):
    store_rows(out_ref, head_ref[...].T, inner_ref)


class Attention:
    def __init__(self, queries, pieces, rows):
        self.pieces, self.rows = pieces, rows
        self.text, self.wide = queries.shape
        self.tiles = self.text // TILE
        self.all_rows = pieces * rows
        self.width = KEY_HEADS * HEAD_SIZE
        span = HEADS_PER_KEY * HEAD_SIZE
        self.text_block = pl.BlockSpec((TILE, span), lambda j, i: (i, j))
        self.inner_block = pl.BlockSpec((self.all_rows, span), lambda j, i: (0, i * KEY_HEADS + j))
        self.head_block = pl.BlockSpec((self.all_rows, HEAD_SIZE), lambda j, i: (0, j))
        self.inner = jax.ShapeDtypeStruct((self.all_rows, self.tiles * self.wide), BF16)
        self.sides = (2 * rows, self.width)
        self.terms = [jax.ShapeDtypeStruct(self.sides, F32)]
        self.terms += [jax.ShapeDtypeStruct(self.sides, BF16)] * (pieces // 2 - 1)

    def call(self, kernel, share, name, **specs):
        return pl.pallas_call(
            functools.partial(kernel, self.pieces),
            cost_estimate=pl.CostEstimate(
                flops=int(share * 12 * self.text * self.all_rows * self.wide),
                bytes_accessed=int(share * 8 * self.text * self.wide),
                transcendentals=0,
            ),
            compiler_params=pltpu.CompilerParams(vmem_limit_bytes=32 * MIB),
            name=name,
            **specs,
        )

    def scores(self, length, frames, queries, gradients, keys_values):
        smem = pl.BlockSpec(memory_space=pltpu.SMEM)
        heads = jax.ShapeDtypeStruct((self.all_rows, self.width), BF16)
        out = self.call(
            scores_kernel,
            1.0,
            "scores",
            in_specs=[smem, smem, VMEM, VMEM] + [VMEM] * self.pieces,
            out_specs=[VMEM] * (5 + len(self.terms)),
            out_shape=[self.inner] * 3 + [heads] * 2 + self.terms,
            scratch_shapes=[
                pltpu.VMEM((self.all_rows, self.width), F32),
                pltpu.VMEM((self.all_rows, 2 * TILE), F32),
            ],
        )(length, frames, queries, gradients, *keys_values)
        return out[:5], out[5], out[6:]

    def values(self, gradients, weights):
        out = self.call(
            values_kernel,
            0.1,
            "values",
            grid=(KEY_HEADS, self.tiles),
            in_specs=[self.text_block, self.inner_block],
            out_specs=[pl.BlockSpec(self.sides, lambda j, i: (0, 0))] * len(self.terms),
            out_shape=self.terms,
            scratch_shapes=[pltpu.VMEM((self.all_rows, HEAD_SIZE), F32)],
        )(in_hbm(gradients), weights)
        return out[0], out[1:]

    def over_rows(self, inner, heads, name):
        return self.call(
            rows_kernel,
            0.1,
            name,
            grid=(KEY_HEADS, self.tiles),
            in_specs=[self.inner_block, self.head_block],
            out_specs=self.text_block,
            out_shape=jax.ShapeDtypeStruct((self.text, self.wide), BF16),
        )(inner, heads)


def in_vmem(kernel, name, out_shape, *arrays):
    return pl.pallas_call(
        kernel,
        in_specs=[VMEM] * len(arrays),
        out_specs=[VMEM] * len(out_shape),
        out_shape=[jax.ShapeDtypeStruct(*shape) for shape in out_shape],
        compiler_params=pltpu.CompilerParams(vmem_limit_bytes=32 * MIB),
        name=name,
    )(*arrays)


def sum_kernel(own_ref, *refs):
    came_refs, (near_ref, far_ref) = refs[:-2], refs[-2:]
    rows = near_ref.shape[0]
    for ref, part in ((near_ref, slice(0, rows)), (far_ref, slice(rows, 2 * rows))):
        total = own_ref[part, :]
        for came_ref in came_refs:
            total += came_ref[part, :].astype(F32)
        ref[...] = total.astype(ref.dtype)


def near_sums(own, came, name):
    half = (own.shape[0] // 2, own.shape[1])
    return in_vmem(sum_kernel, name, [(half, F32), (half, BF16)], own, *came)


def add_kernel(near_ref, far_ref, visual_ref, came_ref, own_ref, again_ref, sides_ref, *near_refs):
    rows, columns = own_ref.shape
    width = visual_ref.shape[1]
    total = (near_ref[...] + far_ref[...].astype(F32)).astype(BF16)
    own_ref[...] = total
    again_ref[...] = total
    sides_ref[:rows, :] = visual_ref[:rows, :]
    sides_ref[rows:, :] = came_ref[:rows, :]
    for m, ref in enumerate(near_refs, 1):
        part = slice(m * rows, (m + 1) * rows)
        ref[:, :columns] = total
        ref[:, columns : columns + width] = visual_ref[part, :]
        ref[:, columns + width :] = came_ref[part, :]


def add_far(near, far, visual_near, visual_came):
    rows, columns = far.shape
    width = visual_near.shape[1]
    shapes = [(far.shape, BF16)] * 2 + [((2 * rows, width), BF16)]
    shapes += [((rows, columns + 2 * width), BF16)] * (visual_near.shape[0] // rows - 1)
    out = in_vmem(add_kernel, "key_grad", shapes, near, far, visual_near, visual_came)
    return out[0], out[1], out[2], out[3:]


def onward_kernel(far_ref, *refs):
    value_refs, out_refs = refs[: len(refs) // 2], refs[len(refs) // 2 :]
    rows, columns = far_ref.shape
    for value_ref, ref in zip(value_refs, out_refs):
        ref[:, :columns] = far_ref[...]
        ref[:, columns : 2 * columns] = value_ref[:rows, :]
        ref[:, 2 * columns :] = value_ref[rows:, :]


def onward(far, values):
    shape = (far.shape[0], 3 * far.shape[1])
    return in_vmem(onward_kernel, "onward", [(shape, BF16)] * len(values), far, *values)


def add_value_kernel(near_ref, far_ref, out_ref):
    out_ref[...] = (near_ref[...] + far_ref[...].astype(F32)).astype(BF16)


def turn_kernel(columns, own_ref, *refs):
    came_refs, out_ref = refs[:-1], refs[-1]
    rows, width = own_ref.shape[0] // 2, own_ref.shape[1]
    parts = []
    for side in range(2):
        parts.append(own_ref[side * rows : (side + 1) * rows, :])
        first = columns + side * width
        parts += [ref[:, first : first + width] for ref in came_refs]
    out_ref[...] = jnp.concatenate(parts, axis=0).T


def turn(columns, own, came):
    rows, width = own.shape
    shape = (width, (1 + len(came)) * rows)
    kernel = functools.partial(turn_kernel, columns)
    return in_vmem(kernel, "turn_visual", [(shape, BF16)], own, *came)[0]


def weight_kernel(order, visual_ref, value_ref, *refs):
    pieces = len(order)
    kg_refs = [refs[order.index(m)] for m in range(pieces)]
    keep_ref, send_ref, near_ref, far_ref = refs[pieces:]
    rows, width = near_ref.shape
    product = dot(visual_ref[...], jnp.concatenate([r[:, :width] for r in kg_refs], axis=0))
    count, share, _ = keep_ref.shape
    core = lax.axis_index("dp") % 2 == 0
    for n in range(count):
        even = product[2 * n * share : (2 * n + 1) * share]
        odd = product[(2 * n + 1) * share : (2 * n + 2) * share]
        keep_ref[n] = jnp.where(core, even, odd)
        send_ref[n] = jnp.where(core, odd, even).astype(BF16)
    for side, ref in enumerate((near_ref, far_ref)):
        total = value_ref[side * rows : (side + 1) * rows, :]
        for kg_ref in kg_refs[pieces // 2 + 1 :]:
            total += kg_ref[:, (1 + side) * width : (2 + side) * width].astype(F32)
        ref[...] = total.astype(ref.dtype)


def weight_terms(samples, visual, value_own, key_grads):
    rows, width = key_grads[0].shape
    middle = len(key_grads) // 2
    order = [0, *range(middle + 1, 2 * middle), *range(middle - 1, 0, -1), middle]
    half = ((samples // 2, visual.shape[0] // samples, width), F32)
    shapes = [half, (half[0], BF16), ((rows, width), F32), ((rows, width), BF16)]
    kernel = functools.partial(weight_kernel, order)
    ordered = [key_grads[m] for m in order]
    return in_vmem(kernel, "weight_terms", shapes, visual, value_own, *ordered)


def halve_kernel(bit, kept_ref, came_ref, keep_ref, send_ref):
    low = (lax.axis_index("dp") >> bit) % 2 == 0
    for n in range(keep_ref.shape[0]):
        even = kept_ref[2 * n] + came_ref[2 * n].astype(F32)
        odd = kept_ref[2 * n + 1] + came_ref[2 * n + 1].astype(F32)
        keep_ref[n] = jnp.where(low, even, odd)
        send_ref[n] = jnp.where(low, odd, even).astype(BF16)


def halve(bit, kept, came):
    half = (kept.shape[0] // 2, *kept.shape[1:])
    kernel = functools.partial(halve_kernel, bit)
    return in_vmem(kernel, "halve", [(half, F32), (half, BF16)], kept, came)


def local(visual_rows, value_matrix, key_weight, queries, output_gradient, visual_len, frame_end):
    tie = lax.optimization_barrier
    blocks, samples = lax.axis_size("blk"), lax.axis_size("dp")
    visual, half = visual_rows[0], blocks // 2

    own, visual_near, visual_far = project(blocks, visual, key_weight, value_matrix[0])
    keys_values = gather(own)
    visual_far = swap(visual_far, "blk", half)
    attention = Attention(queries[0], blocks, visual.shape[0])
    inner, key_own, key_near = attention.scores(
        visual_len, frame_end, queries[0], output_gradient[0], keys_values
    )
    weights, again, dscores, keys, values = inner
    key_near, visual_far = tie((key_near, visual_far))

    key_near = near_exchange(key_near)
    value_own, value_near = attention.values(output_gradient[0], weights)
    key_own, value_own = tie((key_own, value_own))
    key_sum, key_far = near_sums(key_own, key_near, "key_sums")
    key_sum, dscores = tie((key_sum, dscores))
    key_far = swap(key_far, "blk", half)
    query_grad = attention.over_rows(dscores, keys, "query_grad")
    key_sum, query_grad = tie((key_sum, query_grad))
    key_grad, key_again, visual_own, near = add_far(key_sum, key_far, visual_near, visual_far)

    key_grads = gather(key_grad, near, lambda far: onward(far, value_near))
    key_grads[0] = key_again
    attn_out = attention.over_rows(again, values, "output")
    visual_columns = turn(key_grad.shape[1], visual_own, key_grads[1:half])
    visual_columns, attn_out = tie((visual_columns, attn_out))
    kept, sent, value_sum, value_far = weight_terms(samples, visual_columns, value_own, key_grads)
    value_far = swap(value_far, "blk", half)
    came, bit = swap(sent, "dp", 1), 1
    while kept.shape[0] > 1:
        kept, sent = halve(bit, kept, came)
        came, bit = swap(sent, "dp", 1 << bit), bit + 1
    shape = [(value_far.shape, BF16)]
    value_grad = in_vmem(add_value_kernel, "value_grad", shape, value_sum, value_far)[0]
    came, value_grad = tie((came, value_grad))
    weight_grad = kept[0] + came[0].astype(F32)
    return attn_out[None], query_grad[None], value_grad[None], weight_grad


def solution(mesh):
    return jax.shard_map(
        local,
        mesh=mesh,
        in_specs=(
            P("dp", "blk", None),
            P("dp", "blk", None),
            P(),
            P("dp", "blk", None),
            P("dp", "blk", None),
            P("dp"),
            P("dp", None),
        ),
        out_specs=(
            P("dp", "blk", None),
            P("dp", "blk", None),
            P("dp", "blk", None),
            P(("blk", "dp"), None),
        ),
        check_vma=False,
    )
```

```python
import functools

import jax
import jax.numpy as jnp
from jax import lax
from jax.experimental import pallas as pl
from jax.experimental.pallas import tpu as pltpu
from jax.sharding import PartitionSpec as P

KEY_HEADS = 4
HEAD_SIZE = 128
TILE = 128
HEADS_PER_KEY = 8
LOG2_E = 1.4426950408889634
NEGATIVE_FILLER = -1e30
F32 = jnp.float32
BF16 = jnp.bfloat16
MIB = 1024 * 1024
VMEM = pl.BlockSpec(memory_space=pltpu.VMEM)


def dot(a, b, contract=((1,), (0,))):
    return lax.dot_general(a, b, (contract, ((), ())), preferred_element_type=F32)


def swap(x, axis, mask):
    size = lax.axis_size(axis)
    return lax.ppermute(x, axis, [(i, i ^ mask) for i in range(size)])


def in_hbm(x):
    return pltpu.with_memory_space_constraint(x, pltpu.HBM)


def gather(own, near=None, onward=None):
    blocks = lax.axis_size("blk")
    half = blocks // 2
    masks = range(half - 1, 0, -1)
    far = swap(own, "blk", half)
    pieces = {0: own, half: far}
    pieces.update({m: swap(near[m - 1] if near else own, "blk", m) for m in masks})
    kept, sent = onward(far) if onward else (None, [far] * (half - 1))
    pieces.update({m + half: swap(sent[m - 1], "blk", m) for m in masks})
    return [pieces[m] for m in range(blocks)], kept


def near_exchange(pieces):
    return [swap(piece, "blk", m) for m, piece in enumerate(pieces, 1)]


def project_kernel(streams, visual_ref, *refs):
    weight_refs, value_ref = refs[:streams], refs[streams]
    out_ref, near_ref, far_ref, acc_ref = refs[streams + 1 :]
    step = pl.program_id(0)
    slab = weight_refs[0].shape[0]
    part = 0.0
    for p in range(streams):
        start = pl.multiple_of((step * streams + p) * slab, HEAD_SIZE)
        part += dot(visual_ref[:, pl.ds(start, slab)], weight_refs[p][...])

    @pl.when(step == 0)
    def _():
        acc_ref[...] = part
        block = lax.axis_index("blk")
        rows, width = visual_ref.shape[0], near_ref.shape[1]
        half = near_ref.shape[0] // rows
        for side, ref in enumerate((near_ref, far_ref)):
            for m in range(half):
                start = pl.multiple_of((block ^ (m + side * half)) * width, HEAD_SIZE)
                ref[m * rows : (m + 1) * rows, :] = visual_ref[:, pl.ds(start, width)]

    @pl.when(step > 0)
    def _():
        acc_ref[...] += part

    @pl.when(step == pl.num_programs(0) - 1)
    def _():
        columns = acc_ref.shape[1]
        out_ref[:, :columns] = acc_ref[...].astype(BF16)
        out_ref[:, columns:] = value_ref[...]


def project(blocks, visual, key_weight, value):
    rows, features = visual.shape
    columns = key_weight.shape[1]
    steps, streams = 4, 4
    slab = features // (steps * streams)
    out = (rows, columns + value.shape[1])
    half = (blocks // 2 * rows, features // blocks)

    def whole(shape):
        return pl.BlockSpec(shape, lambda k: (0, 0))

    out = pl.pallas_call(
        functools.partial(project_kernel, streams),
        grid=(steps,),
        in_specs=[whole(visual.shape)]
        + [
            pl.BlockSpec((slab, columns), lambda k, p=p: (k * streams + p, 0))
            for p in range(streams)
        ]
        + [whole(value.shape)],
        out_specs=[whole(out)] + [whole(half)] * 2,
        out_shape=[jax.ShapeDtypeStruct(out, BF16)] + [jax.ShapeDtypeStruct(half, BF16)] * 2,
        scratch_shapes=[pltpu.VMEM((rows, columns), F32)],
        cost_estimate=pl.CostEstimate(
            flops=2 * rows * features * columns,
            bytes_accessed=2 * features * columns,
            transcendentals=0,
        ),
        compiler_params=pltpu.CompilerParams(vmem_limit_bytes=32 * MIB),
        name="project",
    )(in_hbm(visual), *[in_hbm(key_weight)] * streams, in_hbm(value))
    return out


def head_pair(ref, rows, start):
    first = pl.ds(pl.multiple_of(start, HEAD_SIZE), HEAD_SIZE)
    second = pl.ds(pl.multiple_of(start + HEAD_SIZE, HEAD_SIZE), HEAD_SIZE)
    return jnp.concatenate([ref[rows, first], ref[rows, second]], axis=0)


def store_sides(own_ref, near_refs, terms, columns):
    half = len(near_refs) + 1
    rows = own_ref.shape[0] // 2
    for m, ref in enumerate((own_ref, *near_refs)):
        for side in range(2):
            first = (m + side * half) * rows
            part = terms[first : first + rows, :].astype(ref.dtype)
            ref[side * rows : (side + 1) * rows, columns] = part


def scores_kernel(pieces, length_ref, frame_ref, q_ref, g_ref, *refs):
    kv_refs, (w_ref, ds_ref, k_ref, v_ref) = refs[:pieces], refs[pieces : pieces + 4]
    own_ref, near_refs, (kg_acc, bias_ref) = refs[pieces + 4], refs[pieces + 5 : -2], refs[-2:]
    block = lax.axis_index("blk")
    tiles = q_ref.shape[0] // TILE
    rows = kv_refs[0].shape[0]
    width = KEY_HEADS * HEAD_SIZE
    pair = 2 * TILE
    pairs = HEADS_PER_KEY // 2
    span = HEADS_PER_KEY * HEAD_SIZE
    scale = HEAD_SIZE**-0.5
    for m in range(pieces):
        part = slice(m * rows, (m + 1) * rows)
        k_ref[part, :] = kv_refs[m][:, :width]
        v_ref[part, :] = kv_refs[m][:, width:]
    row = lax.broadcasted_iota(jnp.int32, (rows, TILE), 0)
    for i in range(tiles):
        text = slice(i * TILE, (i + 1) * TILE)
        limit = jnp.minimum(length_ref[0], TILE * frame_ref[0, block * tiles + i])
        for m in range(pieces):
            live = row + (block ^ m) * rows < limit
            bias_ref[m * rows : (m + 1) * rows, :] = jnp.where(live, 0.0, NEGATIVE_FILLER)

        @pl.loop(0, KEY_HEADS)
        def _(j, i=i, text=text):
            head = pl.ds(pl.multiple_of(j * HEAD_SIZE, HEAD_SIZE), HEAD_SIZE)
            keys, values = k_ref[:, head], v_ref[:, head]
            q_stack, raw, dprobs = [], {}, {}

            def products(p):
                start = j * span + p * pair
                q_stack.append(head_pair(q_ref, text, start))
                raw[p] = dot(keys, q_stack[p], ((1,), (1,)))
                dprobs[p] = dot(values, head_pair(g_ref, text, start), ((1,), (1,)))

            products(0)
            ds_stack = []
            for p in range(pairs):
                if p + 1 < pairs:
                    products(p + 1)
                for h in range(2):
                    one = slice(h * TILE, (h + 1) * TILE)
                    scores = raw[p][:, one] + bias_ref[...]
                    peak = jnp.max(scores, axis=0, keepdims=True)
                    shifted = jnp.exp2((scores - peak) * (scale * LOG2_E))
                    terms = shifted * dprobs[p][:, one]
                    inverse = 1.0 / jnp.sum(shifted, axis=0, keepdims=True)
                    slope = inverse * scale
                    offset = jnp.sum(terms, axis=0, keepdims=True) * inverse * slope
                    start = (i * KEY_HEADS + j) * span + p * pair + h * TILE
                    columns = pl.ds(pl.multiple_of(start, HEAD_SIZE), TILE)
                    w_ref[:, columns] = (shifted * inverse).astype(BF16)
                    ds_stack.append((terms * slope - shifted * offset).astype(BF16))
                    ds_ref[:, columns] = ds_stack[-1]
            kg = dot(jnp.concatenate(ds_stack, axis=1), jnp.concatenate(q_stack, axis=0))
            if i == 0:
                kg_acc[:, head] = kg
            else:
                kg_acc[:, head] += kg

    store_sides(own_ref, near_refs, kg_acc, slice(None))


def values_kernel(pieces, g_ref, w_ref, near_ref, far_ref, vg_acc):
    j, i = pl.program_id(0), pl.program_id(1)
    head = pl.ds(pl.multiple_of(j * HEAD_SIZE, HEAD_SIZE), HEAD_SIZE)
    half = near_ref.shape[0]
    stack = [g_ref[:, h * HEAD_SIZE : (h + 1) * HEAD_SIZE] for h in range(HEADS_PER_KEY)]
    vg = dot(w_ref[...], jnp.concatenate(stack, axis=0))

    @pl.when(i == 0)
    def _():
        vg_acc[...] = vg

    @pl.when(i > 0)
    def _():
        vg_acc[...] += vg

    @pl.when(i == pl.num_programs(1) - 1)
    def _():
        near_ref[:, head] = vg_acc[:half, :]
        far_ref[:, head] = vg_acc[half:, :].astype(BF16)


def store_rows(out_ref, left, inner_ref):
    pair = 2 * TILE
    for p in range(HEADS_PER_KEY // 2):
        out = dot(left, inner_ref[:, p * pair : (p + 1) * pair]).T.astype(BF16)
        out_ref[:, p * pair : p * pair + HEAD_SIZE] = out[:TILE]
        out_ref[:, p * pair + HEAD_SIZE : (p + 1) * pair] = out[TILE:]


def rows_kernel(pieces, inner_ref, head_ref, out_ref):
    store_rows(out_ref, head_ref[...].T, inner_ref)


class Attention:
    def __init__(self, queries, pieces, rows):
        self.pieces, self.rows = pieces, rows
        self.text, self.wide = queries.shape
        self.tiles = self.text // TILE
        self.all_rows = pieces * rows
        self.width = KEY_HEADS * HEAD_SIZE
        span = HEADS_PER_KEY * HEAD_SIZE
        self.text_block = pl.BlockSpec((TILE, span), lambda j, i: (i, j))
        self.inner_block = pl.BlockSpec((self.all_rows, span), lambda j, i: (0, i * KEY_HEADS + j))
        self.head_block = pl.BlockSpec((self.all_rows, HEAD_SIZE), lambda j, i: (0, j))
        self.inner = jax.ShapeDtypeStruct((self.all_rows, self.tiles * self.wide), BF16)
        self.sides = (2 * rows, self.width)
        self.terms = [jax.ShapeDtypeStruct(self.sides, F32)]
        self.terms += [jax.ShapeDtypeStruct(self.sides, BF16)] * (pieces // 2 - 1)

    def call(self, kernel, share, name, **specs):
        return pl.pallas_call(
            functools.partial(kernel, self.pieces),
            cost_estimate=pl.CostEstimate(
                flops=int(share * 12 * self.text * self.all_rows * self.wide),
                bytes_accessed=int(share * 8 * self.text * self.wide),
                transcendentals=0,
            ),
            compiler_params=pltpu.CompilerParams(vmem_limit_bytes=32 * MIB),
            name=name,
            **specs,
        )

    def scores(self, length, frames, queries, gradients, keys_values):
        smem = pl.BlockSpec(memory_space=pltpu.SMEM)
        heads = jax.ShapeDtypeStruct((self.all_rows, self.width), BF16)
        out = self.call(
            scores_kernel,
            1.0,
            "scores",
            in_specs=[smem, smem, VMEM, VMEM] + [VMEM] * self.pieces,
            out_specs=[VMEM] * (4 + len(self.terms)),
            out_shape=[self.inner] * 2 + [heads] * 2 + self.terms,
            scratch_shapes=[
                pltpu.VMEM((self.all_rows, self.width), F32),
                pltpu.VMEM((self.all_rows, TILE), F32),
            ],
        )(length, frames, queries, gradients, *keys_values)
        return out[:4], out[4], out[5:]

    def values(self, gradients, weights):
        half = (self.all_rows // 2, self.width)
        return self.call(
            values_kernel,
            0.1,
            "values",
            grid=(KEY_HEADS, self.tiles),
            in_specs=[self.text_block, self.inner_block],
            out_specs=[pl.BlockSpec(half, lambda j, i: (0, 0))] * 2,
            out_shape=[jax.ShapeDtypeStruct(half, F32), jax.ShapeDtypeStruct(half, BF16)],
            scratch_shapes=[pltpu.VMEM((self.all_rows, HEAD_SIZE), F32)],
        )(in_hbm(gradients), weights)

    def over_rows(self, inner, heads, name):
        return self.call(
            rows_kernel,
            0.1,
            name,
            grid=(KEY_HEADS, self.tiles),
            in_specs=[self.inner_block, self.head_block],
            out_specs=self.text_block,
            out_shape=jax.ShapeDtypeStruct((self.text, self.wide), BF16),
        )(inner, heads)


def in_vmem(kernel, name, out_shape, *arrays):
    return pl.pallas_call(
        kernel,
        in_specs=[VMEM] * len(arrays),
        out_specs=[VMEM] * len(out_shape),
        out_shape=[jax.ShapeDtypeStruct(*shape) for shape in out_shape],
        compiler_params=pltpu.CompilerParams(vmem_limit_bytes=32 * MIB),
        name=name,
    )(*arrays)


def sum_kernel(own_ref, *refs):
    came_refs, (near_ref, far_ref) = refs[:-2], refs[-2:]
    rows = near_ref.shape[0]
    for ref, part in ((near_ref, slice(0, rows)), (far_ref, slice(rows, 2 * rows))):
        total = own_ref[part, :]
        for came_ref in came_refs:
            total += came_ref[part, :].astype(F32)
        ref[...] = total.astype(ref.dtype)


def near_sums(own, came, name):
    half = (own.shape[0] // 2, own.shape[1])
    return in_vmem(sum_kernel, name, [(half, F32), (half, BF16)], own, *came)


def add_kernel(near_ref, far_ref, visual_ref, came_ref, own_ref, again_ref, sides_ref, *near_refs):
    rows, columns = own_ref.shape
    width = visual_ref.shape[1]
    total = (near_ref[...] + far_ref[...].astype(F32)).astype(BF16)
    own_ref[...] = total
    again_ref[...] = total
    sides_ref[:rows, :] = visual_ref[:rows, :]
    sides_ref[rows:, :] = came_ref[:rows, :]
    for m, ref in enumerate(near_refs, 1):
        part = slice(m * rows, (m + 1) * rows)
        ref[:, :columns] = total
        ref[:, columns : columns + width] = visual_ref[part, :]
        ref[:, columns + width :] = came_ref[part, :]


def add_far(near, far, visual_near, visual_came):
    rows, columns = far.shape
    width = visual_near.shape[1]
    shapes = [(far.shape, BF16)] * 2 + [((2 * rows, width), BF16)]
    shapes += [((rows, columns + 2 * width), BF16)] * (visual_near.shape[0] // rows - 1)
    out = in_vmem(add_kernel, "key_grad", shapes, near, far, visual_near, visual_came)
    return out[0], out[1], out[2], out[3:]


def onward_kernel(far_ref, value_ref, came_ref, own_ref, *refs):
    rows, columns = far_ref.shape
    for m, ref in enumerate((own_ref, *refs)):
        part = slice(m * rows, (m + 1) * rows)
        total = value_ref[part, :] + came_ref[part, :].astype(F32)
        if m == 0:
            ref[...] = total
        else:
            ref[:, :columns] = far_ref[...]
            ref[:, columns:] = total.astype(BF16)


def onward(far, values, came):
    rows, columns = far.shape
    shapes = [((rows, columns), F32)]
    shapes += [((rows, 2 * columns), BF16)] * (values.shape[0] // rows - 1)
    out = in_vmem(onward_kernel, "onward", shapes, far, values, came)
    return out[0], out[1:]


def turn_kernel(columns, own_ref, *refs):
    came_refs, out_ref = refs[:-1], refs[-1]
    rows, width = own_ref.shape[0] // 2, own_ref.shape[1]
    parts = []
    for side in range(2):
        parts.append(own_ref[side * rows : (side + 1) * rows, :])
        first = columns + side * width
        parts += [ref[:, first : first + width] for ref in came_refs]
    out_ref[...] = jnp.concatenate(parts, axis=0).T


def turn(columns, own, came):
    rows, width = own.shape
    shape = (width, (1 + len(came)) * rows)
    kernel = functools.partial(turn_kernel, columns)
    return in_vmem(kernel, "turn_visual", [(shape, BF16)], own, *came)[0]


def weight_kernel(visual_ref, value_ref, *refs):
    kg_refs, (keep_ref, send_ref, grad_ref) = refs[:-3], refs[-3:]
    width = grad_ref.shape[1]
    product = dot(visual_ref[...], jnp.concatenate([r[:, :width] for r in kg_refs], axis=0))
    count, share, _ = keep_ref.shape
    core = lax.axis_index("dp") % 2 == 0
    for n in range(count):
        even = product[2 * n * share : (2 * n + 1) * share]
        odd = product[(2 * n + 1) * share : (2 * n + 2) * share]
        keep_ref[n] = jnp.where(core, even, odd)
        send_ref[n] = jnp.where(core, odd, even).astype(BF16)
    total = value_ref[...]
    for ref in kg_refs[len(kg_refs) // 2 + 1 :]:
        total += ref[:, width:].astype(F32)
    grad_ref[...] = total.astype(BF16)


def weight_terms(samples, visual, value_own, key_grads):
    rows, width = key_grads[0].shape
    half = ((samples // 2, visual.shape[0] // samples, width), F32)
    shapes = [half, (half[0], BF16), ((rows, width), BF16)]
    return in_vmem(weight_kernel, "weight_terms", shapes, visual, value_own, *key_grads)


def halve_kernel(bit, kept_ref, came_ref, keep_ref, send_ref):
    low = (lax.axis_index("dp") >> bit) % 2 == 0
    for n in range(keep_ref.shape[0]):
        even = kept_ref[2 * n] + came_ref[2 * n].astype(F32)
        odd = kept_ref[2 * n + 1] + came_ref[2 * n + 1].astype(F32)
        keep_ref[n] = jnp.where(low, even, odd)
        send_ref[n] = jnp.where(low, odd, even).astype(BF16)


def halve(bit, kept, came):
    half = (kept.shape[0] // 2, *kept.shape[1:])
    kernel = functools.partial(halve_kernel, bit)
    return in_vmem(kernel, "halve", [(half, F32), (half, BF16)], kept, came)


def local(visual_rows, value_matrix, key_weight, queries, output_gradient, visual_len, frame_end):
    tie = lax.optimization_barrier
    blocks, samples = lax.axis_size("blk"), lax.axis_size("dp")
    visual, half = visual_rows[0], blocks // 2

    own, visual_near, visual_far = project(blocks, visual, key_weight, value_matrix[0])
    keys_values, _ = gather(own)
    visual_far = swap(visual_far, "blk", half)
    attention = Attention(queries[0], blocks, visual.shape[0])
    inner, key_own, key_near = attention.scores(
        visual_len, frame_end, queries[0], output_gradient[0], keys_values
    )
    weights, dscores, keys, values = inner
    key_near, visual_far = tie((key_near, visual_far))

    key_near = near_exchange(key_near)
    value_near, value_far = attention.values(output_gradient[0], weights)
    value_far = swap(value_far, "blk", half)
    key_own, value_near = tie((key_own, value_near))
    key_sum, key_far = near_sums(key_own, key_near, "key_sums")
    key_sum, dscores = tie((key_sum, dscores))
    key_far = swap(key_far, "blk", half)
    query_grad = attention.over_rows(dscores, keys, "query_grad")
    key_sum, query_grad = tie((key_sum, query_grad))
    key_grad, key_again, visual_own, near = add_far(key_sum, key_far, visual_near, visual_far)

    key_grads, value_own = gather(key_grad, near, lambda far: onward(far, value_near, value_far))
    key_grads[0] = key_again
    attn_out = attention.over_rows(weights, values, "output")
    visual_columns = turn(key_grad.shape[1], visual_own, key_grads[1:half])
    visual_columns, attn_out = tie((visual_columns, attn_out))
    kept, sent, value_grad = weight_terms(samples, visual_columns, value_own, key_grads)
    came, bit = swap(sent, "dp", 1), 1
    while kept.shape[0] > 1:
        kept, sent = halve(bit, kept, came)
        came, bit = swap(sent, "dp", 1 << bit), bit + 1
    weight_grad = kept[0] + came[0].astype(F32)
    return attn_out[None], query_grad[None], value_grad[None], weight_grad


def solution(mesh):
    return jax.shard_map(
        local,
        mesh=mesh,
        in_specs=(
            P("dp", "blk", None),
            P("dp", "blk", None),
            P(),
            P("dp", "blk", None),
            P("dp", "blk", None),
            P("dp"),
            P("dp", None),
        ),
        out_specs=(
            P("dp", "blk", None),
            P("dp", "blk", None),
            P("dp", "blk", None),
            P(("blk", "dp"), None),
        ),
        check_vma=False,
    )
```

```python
import functools

import jax
import jax.numpy as jnp
from jax import lax
from jax.experimental import pallas as pl
from jax.experimental.pallas import tpu as pltpu
from jax.sharding import PartitionSpec as P

KEY_HEADS = 4
HEAD_SIZE = 128
TILE = 128
HEADS_PER_KEY = 8
LOG2_E = 1.4426950408889634
NEGATIVE_FILLER = -1e30
F32 = jnp.float32
BF16 = jnp.bfloat16
MIB = 1024 * 1024
VMEM = pl.BlockSpec(memory_space=pltpu.VMEM)


def dot(a, b, contract=((1,), (0,))):
    return lax.dot_general(a, b, (contract, ((), ())), preferred_element_type=F32)


def swap(x, axis, mask):
    size = lax.axis_size(axis)
    return lax.ppermute(x, axis, [(i, i ^ mask) for i in range(size)])


def in_hbm(x):
    return pltpu.with_memory_space_constraint(x, pltpu.HBM)


def gather(own, near=None, onward=None):
    blocks = lax.axis_size("blk")
    half = blocks // 2
    masks = range(half - 1, 0, -1)
    far = swap(own, "blk", half)
    pieces = {0: own, half: far}
    pieces.update({m: swap(near[m - 1] if near else own, "blk", m) for m in masks})
    sent = onward(far) if onward else [far] * (half - 1)
    pieces.update({m + half: swap(sent[m - 1], "blk", m) for m in masks})
    return [pieces[m] for m in range(blocks)]


def near_exchange(pieces):
    return [swap(piece, "blk", m) for m, piece in enumerate(pieces, 1)]


def project_kernel(streams, visual_ref, *refs):
    weight_refs, value_ref = refs[:streams], refs[streams]
    out_ref, near_ref, far_ref, acc_ref = refs[streams + 1 :]
    step = pl.program_id(0)
    slab = weight_refs[0].shape[0]
    part = 0.0
    for p in range(streams):
        start = pl.multiple_of((step * streams + p) * slab, HEAD_SIZE)
        part += dot(visual_ref[:, pl.ds(start, slab)], weight_refs[p][...])

    @pl.when(step == 0)
    def _():
        acc_ref[...] = part
        block = lax.axis_index("blk")
        rows, width = visual_ref.shape[0], near_ref.shape[1]
        half = near_ref.shape[0] // rows
        for side, ref in enumerate((near_ref, far_ref)):
            for m in range(half):
                start = pl.multiple_of((block ^ (m + side * half)) * width, HEAD_SIZE)
                ref[m * rows : (m + 1) * rows, :] = visual_ref[:, pl.ds(start, width)]

    @pl.when(step > 0)
    def _():
        acc_ref[...] += part

    @pl.when(step == pl.num_programs(0) - 1)
    def _():
        columns = acc_ref.shape[1]
        out_ref[:, :columns] = acc_ref[...].astype(BF16)
        out_ref[:, columns:] = value_ref[...]


def project(blocks, visual, key_weight, value):
    rows, features = visual.shape
    columns = key_weight.shape[1]
    steps, streams = 2, 4
    slab = features // (steps * streams)
    out = (rows, columns + value.shape[1])
    half = (blocks // 2 * rows, features // blocks)

    def whole(shape):
        return pl.BlockSpec(shape, lambda k: (0, 0))

    out = pl.pallas_call(
        functools.partial(project_kernel, streams),
        grid=(steps,),
        in_specs=[whole(visual.shape)]
        + [
            pl.BlockSpec((slab, columns), lambda k, p=p: (k * streams + p, 0))
            for p in range(streams)
        ]
        + [whole(value.shape)],
        out_specs=[whole(out)] + [whole(half)] * 2,
        out_shape=[jax.ShapeDtypeStruct(out, BF16)] + [jax.ShapeDtypeStruct(half, BF16)] * 2,
        scratch_shapes=[pltpu.VMEM((rows, columns), F32)],
        cost_estimate=pl.CostEstimate(
            flops=2 * rows * features * columns,
            bytes_accessed=2 * features * columns,
            transcendentals=0,
        ),
        compiler_params=pltpu.CompilerParams(vmem_limit_bytes=32 * MIB),
        name="project",
    )(in_hbm(visual), *[in_hbm(key_weight)] * streams, in_hbm(value))
    return out


def head_pair(ref, rows, start):
    first = pl.ds(pl.multiple_of(start, HEAD_SIZE), HEAD_SIZE)
    second = pl.ds(pl.multiple_of(start + HEAD_SIZE, HEAD_SIZE), HEAD_SIZE)
    return jnp.concatenate([ref[rows, first], ref[rows, second]], axis=0)


def store_sides(own_ref, near_refs, terms, columns):
    half = len(near_refs) + 1
    rows = own_ref.shape[0] // 2
    for m, ref in enumerate((own_ref, *near_refs)):
        for side in range(2):
            first = (m + side * half) * rows
            part = terms[first : first + rows, :].astype(ref.dtype)
            ref[side * rows : (side + 1) * rows, columns] = part


def scores_kernel(pieces, length_ref, frame_ref, q_ref, g_ref, *refs):
    kv_refs, (w_ref, ds_ref, k_ref, v_ref) = refs[:pieces], refs[pieces : pieces + 4]
    kv_refs = (kv_refs[0], *kv_refs[:0:-1])
    own_ref, near_refs, (kg_acc, bias_ref) = refs[pieces + 4], refs[pieces + 5 : -2], refs[-2:]
    block = lax.axis_index("blk")
    tiles = q_ref.shape[0] // TILE
    rows = kv_refs[0].shape[0]
    width = KEY_HEADS * HEAD_SIZE
    pair = 2 * TILE
    pairs = HEADS_PER_KEY // 2
    span = HEADS_PER_KEY * HEAD_SIZE
    scale = HEAD_SIZE**-0.5
    for m in range(pieces):
        part = slice(m * rows, (m + 1) * rows)
        k_ref[part, :] = kv_refs[m][:, :width]
        v_ref[part, :] = kv_refs[m][:, width:]
    row = lax.broadcasted_iota(jnp.int32, (rows, pair), 0)
    for i in range(tiles):
        text = slice(i * TILE, (i + 1) * TILE)
        limit = jnp.minimum(length_ref[0], TILE * frame_ref[0, block * tiles + i])
        for m in range(pieces):
            live = row + (block ^ m) * rows < limit
            bias_ref[m * rows : (m + 1) * rows, :] = jnp.where(live, 0.0, NEGATIVE_FILLER)

        @pl.loop(0, KEY_HEADS)
        def _(j, i=i, text=text):
            head = pl.ds(pl.multiple_of(j * HEAD_SIZE, HEAD_SIZE), HEAD_SIZE)
            keys, values = k_ref[:, head], v_ref[:, head]
            q_stack, raw, dprobs = [], {}, {}

            def products(p):
                start = j * span + p * pair
                q_stack.append(head_pair(q_ref, text, start))
                raw[p] = dot(keys, q_stack[p], ((1,), (1,)))
                dprobs[p] = dot(values, head_pair(g_ref, text, start), ((1,), (1,)))

            products(0)
            ds_stack = []
            for p in range(pairs):
                if p + 1 < pairs:
                    products(p + 1)
                scores = raw.pop(p) + bias_ref[...]
                peak = jnp.max(scores, axis=0, keepdims=True)
                shifted = jnp.exp2((scores - peak) * (scale * LOG2_E))
                terms = shifted * dprobs.pop(p)
                inverse = 1.0 / jnp.sum(shifted, axis=0, keepdims=True)
                slope = inverse * scale
                offset = jnp.sum(terms, axis=0, keepdims=True) * inverse * slope
                start = (i * KEY_HEADS + j) * span + p * pair
                both = pl.ds(pl.multiple_of(start, HEAD_SIZE), pair)
                w_ref[:, both] = (shifted * inverse).astype(BF16)
                ds_stack.append((terms * slope - shifted * offset).astype(BF16))
                ds_ref[:, both] = ds_stack[p]
            kg = dot(jnp.concatenate(ds_stack, axis=1), jnp.concatenate(q_stack, axis=0))
            if i == 0:
                kg_acc[:, head] = kg
            else:
                kg_acc[:, head] += kg

    store_sides(own_ref, near_refs, kg_acc, slice(None))


def values_kernel(pieces, g_ref, w_ref, own_ref, *refs):
    near_refs, vg_acc = refs[:-1], refs[-1]
    j, i = pl.program_id(0), pl.program_id(1)
    head = pl.ds(pl.multiple_of(j * HEAD_SIZE, HEAD_SIZE), HEAD_SIZE)
    stack = [g_ref[:, h * HEAD_SIZE : (h + 1) * HEAD_SIZE] for h in range(HEADS_PER_KEY)]
    vg = dot(w_ref[...], jnp.concatenate(stack, axis=0))

    @pl.when(i == 0)
    def _():
        vg_acc[...] = vg

    @pl.when(i > 0)
    def _():
        vg_acc[...] += vg

    @pl.when(i == pl.num_programs(1) - 1)
    def _():
        store_sides(own_ref, near_refs, vg_acc, head)


def store_rows(out_ref, left, inner_ref):
    pair = 2 * TILE
    for p in range(HEADS_PER_KEY // 2):
        out = dot(left, inner_ref[:, p * pair : (p + 1) * pair]).T.astype(BF16)
        out_ref[:, p * pair : p * pair + HEAD_SIZE] = out[:TILE]
        out_ref[:, p * pair + HEAD_SIZE : (p + 1) * pair] = out[TILE:]


def rows_kernel(pieces, inner_ref, head_ref, out_ref):
    store_rows(out_ref, head_ref[...].T, inner_ref)


class Attention:
    def __init__(self, queries, pieces, rows):
        self.pieces, self.rows = pieces, rows
        self.text, self.wide = queries.shape
        self.tiles = self.text // TILE
        self.all_rows = pieces * rows
        self.width = KEY_HEADS * HEAD_SIZE
        span = HEADS_PER_KEY * HEAD_SIZE
        self.text_block = pl.BlockSpec((TILE, span), lambda j, i: (i, j))
        self.inner_block = pl.BlockSpec((self.all_rows, span), lambda j, i: (0, i * KEY_HEADS + j))
        self.head_block = pl.BlockSpec((self.all_rows, HEAD_SIZE), lambda j, i: (0, j))
        self.inner = jax.ShapeDtypeStruct((self.all_rows, self.tiles * self.wide), BF16)
        self.sides = (2 * rows, self.width)
        self.terms = [jax.ShapeDtypeStruct(self.sides, F32)]
        self.terms += [jax.ShapeDtypeStruct(self.sides, BF16)] * (pieces // 2 - 1)

    def call(self, kernel, share, name, **specs):
        return pl.pallas_call(
            functools.partial(kernel, self.pieces),
            cost_estimate=pl.CostEstimate(
                flops=int(share * 12 * self.text * self.all_rows * self.wide),
                bytes_accessed=int(share * 8 * self.text * self.wide),
                transcendentals=0,
            ),
            compiler_params=pltpu.CompilerParams(vmem_limit_bytes=32 * MIB),
            name=name,
            **specs,
        )

    def scores(self, length, frames, queries, gradients, keys_values):
        smem = pl.BlockSpec(memory_space=pltpu.SMEM)
        heads = jax.ShapeDtypeStruct((self.all_rows, self.width), BF16)
        out = self.call(
            scores_kernel,
            1.0,
            "scores",
            in_specs=[smem, smem, VMEM, VMEM] + [VMEM] * self.pieces,
            out_specs=[VMEM] * (4 + len(self.terms)),
            out_shape=[self.inner] * 2 + [heads] * 2 + self.terms,
            scratch_shapes=[
                pltpu.VMEM((self.all_rows, self.width), F32),
                pltpu.VMEM((self.all_rows, 2 * TILE), F32),
            ],
        )(length, frames, queries, gradients, keys_values[0], *keys_values[:0:-1])
        return out[:4], out[4], out[5:]

    def values(self, gradients, weights):
        out = self.call(
            values_kernel,
            0.1,
            "values",
            grid=(KEY_HEADS, self.tiles),
            in_specs=[self.text_block, self.inner_block],
            out_specs=[pl.BlockSpec(self.sides, lambda j, i: (0, 0))] * len(self.terms),
            out_shape=self.terms,
            scratch_shapes=[pltpu.VMEM((self.all_rows, HEAD_SIZE), F32)],
        )(in_hbm(gradients), weights)
        return out[0], out[1:]

    def over_rows(self, inner, heads, name):
        return self.call(
            rows_kernel,
            0.1,
            name,
            grid=(KEY_HEADS, self.tiles),
            in_specs=[self.inner_block, self.head_block],
            out_specs=self.text_block,
            out_shape=jax.ShapeDtypeStruct((self.text, self.wide), BF16),
        )(inner, heads)


def in_vmem(kernel, name, out_shape, *arrays, cost=None):
    return pl.pallas_call(
        kernel,
        cost_estimate=cost,
        in_specs=[VMEM] * len(arrays),
        out_specs=[VMEM] * len(out_shape),
        out_shape=[jax.ShapeDtypeStruct(*shape) for shape in out_shape],
        compiler_params=pltpu.CompilerParams(vmem_limit_bytes=32 * MIB),
        name=name,
    )(*arrays)


def sum_kernel(own_ref, *refs):
    came_refs, (near_ref, far_ref) = refs[:-2], refs[-2:]
    rows = near_ref.shape[0]
    for ref, part in ((near_ref, slice(0, rows)), (far_ref, slice(rows, 2 * rows))):
        total = own_ref[part, :]
        for came_ref in came_refs:
            total += came_ref[part, :].astype(F32)
        ref[...] = total.astype(ref.dtype)


def near_sums(own, came, name):
    half = (own.shape[0] // 2, own.shape[1])
    return in_vmem(sum_kernel, name, [(half, F32), (half, BF16)], own, *came)


def add_kernel(near_ref, far_ref, visual_ref, came_ref, own_ref, again_ref, sides_ref, *near_refs):
    rows, columns = own_ref.shape
    width = visual_ref.shape[1]
    total = (near_ref[...] + far_ref[...].astype(F32)).astype(BF16)
    own_ref[...] = total
    again_ref[...] = total
    sides_ref[:rows, :] = visual_ref[:rows, :]
    sides_ref[rows:, :] = came_ref[:rows, :]
    for m, ref in enumerate(near_refs, 1):
        part = slice(m * rows, (m + 1) * rows)
        ref[:, :columns] = total
        ref[:, columns : columns + width] = visual_ref[part, :]
        ref[:, columns + width :] = came_ref[part, :]


def add_far(near, far, visual_near, visual_came):
    rows, columns = far.shape
    width = visual_near.shape[1]
    shapes = [(far.shape, BF16)] * 2 + [((2 * rows, width), BF16)]
    shapes += [((rows, columns + 2 * width), BF16)] * (visual_near.shape[0] // rows - 1)
    out = in_vmem(add_kernel, "key_grad", shapes, near, far, visual_near, visual_came)
    return out[0], out[1], out[2], out[3:]


def onward_kernel(far_ref, *refs):
    value_refs, out_refs = refs[: len(refs) // 2], refs[len(refs) // 2 :]
    rows, columns = far_ref.shape
    for value_ref, ref in zip(value_refs, out_refs):
        ref[:, :columns] = far_ref[...]
        ref[:, columns : 2 * columns] = value_ref[:rows, :]
        ref[:, 2 * columns :] = value_ref[rows:, :]


def onward(far, values):
    shape = (far.shape[0], 3 * far.shape[1])
    return in_vmem(onward_kernel, "onward", [(shape, BF16)] * len(values), far, *values)


def add_value_kernel(near_ref, far_ref, out_ref):
    out_ref[...] = (near_ref[...] + far_ref[...].astype(F32)).astype(BF16)


def turn_kernel(columns, own_ref, *refs):
    came_refs, out_ref = refs[:-1], refs[-1]
    rows, width = own_ref.shape[0] // 2, own_ref.shape[1]
    parts = []
    for side in range(2):
        parts.append(own_ref[side * rows : (side + 1) * rows, :])
        first = columns + side * width
        parts += [ref[:, first : first + width] for ref in came_refs]
    out_ref[...] = jnp.concatenate(parts, axis=0).T


def turn(columns, own, came):
    rows, width = own.shape
    shape = (width, (1 + len(came)) * rows)
    kernel = functools.partial(turn_kernel, columns)
    return in_vmem(kernel, "turn_visual", [(shape, BF16)], own, *came)[0]


def weight_kernel(order, visual_ref, value_ref, *refs):
    pieces = len(order)
    kg_refs = [refs[order.index(m)] for m in range(pieces)]
    keep_ref, send_ref, near_ref, far_ref = refs[pieces:]
    rows, width = near_ref.shape
    product = dot(visual_ref[...], jnp.concatenate([r[:, :width] for r in kg_refs], axis=0))
    count, share, _ = keep_ref.shape
    core = lax.axis_index("dp") % 2 == 0
    for n in range(count):
        even = product[2 * n * share : (2 * n + 1) * share]
        odd = product[(2 * n + 1) * share : (2 * n + 2) * share]
        keep_ref[n] = jnp.where(core, even, odd)
        send_ref[n] = jnp.where(core, odd, even).astype(BF16)
    for side, ref in enumerate((near_ref, far_ref)):
        total = value_ref[side * rows : (side + 1) * rows, :]
        for kg_ref in kg_refs[pieces // 2 + 1 :]:
            total += kg_ref[:, (1 + side) * width : (2 + side) * width].astype(F32)
        ref[...] = total.astype(ref.dtype)


def weight_terms(samples, visual, value_own, key_grads):
    rows, width = key_grads[0].shape
    middle = len(key_grads) // 2
    order = [0, *range(2 * middle - 1, middle, -1), *range(middle - 1, 0, -1), middle]
    half = ((samples // 2, visual.shape[0] // samples, width), F32)
    shapes = [half, (half[0], BF16), ((rows, width), F32), ((rows, width), BF16)]
    kernel = functools.partial(weight_kernel, order)
    ordered = [key_grads[m] for m in order]
    return in_vmem(kernel, "weight_terms", shapes, visual, value_own, *ordered)


def halve_kernel(bit, kept_ref, came_ref, keep_ref, send_ref):
    low = (lax.axis_index("dp") >> bit) % 2 == 0
    for n in range(keep_ref.shape[0]):
        even = kept_ref[2 * n] + came_ref[2 * n].astype(F32)
        odd = kept_ref[2 * n + 1] + came_ref[2 * n + 1].astype(F32)
        keep_ref[n] = jnp.where(low, even, odd)
        send_ref[n] = jnp.where(low, odd, even).astype(BF16)


def halve(bit, kept, came):
    half = (kept.shape[0] // 2, *kept.shape[1:])
    kernel = functools.partial(halve_kernel, bit)
    return in_vmem(kernel, "halve", [(half, F32), (half, BF16)], kept, came)


def local(visual_rows, value_matrix, key_weight, queries, output_gradient, visual_len, frame_end):
    tie = lax.optimization_barrier
    blocks, samples = lax.axis_size("blk"), lax.axis_size("dp")
    visual, half = visual_rows[0], blocks // 2

    own, visual_near, visual_far = project(blocks, visual, key_weight, value_matrix[0])
    keys_values = gather(own)
    visual_far = swap(visual_far, "blk", half)
    attention = Attention(queries[0], blocks, visual.shape[0])
    inner, key_own, key_near = attention.scores(
        visual_len, frame_end, queries[0], output_gradient[0], keys_values
    )
    weights, dscores, keys, values = inner
    key_near, visual_far = tie((key_near, visual_far))

    key_near = near_exchange(key_near)
    value_own, value_near = attention.values(output_gradient[0], weights)
    key_own, value_own = tie((key_own, value_own))
    key_sum, key_far = near_sums(key_own, key_near[::-1], "key_sums")
    key_sum, dscores = tie((key_sum, dscores))
    key_far = swap(key_far, "blk", half)
    query_grad = attention.over_rows(dscores, keys, "query_grad")
    key_sum, query_grad = tie((key_sum, query_grad))
    key_grad, key_again, visual_own, near = add_far(key_sum, key_far, visual_near, visual_far)

    key_grads = gather(key_grad, near, lambda far: onward(far, value_near))
    key_grads[0] = key_again
    attn_out = attention.over_rows(weights, values, "output")
    visual_columns = turn(key_grad.shape[1], visual_own, key_grads[1:half])
    visual_columns, attn_out = tie((visual_columns, attn_out))
    kept, sent, value_sum, value_far = weight_terms(samples, visual_columns, value_own, key_grads)
    value_far = swap(value_far, "blk", half)
    came, bit = swap(sent, "dp", 1), 1
    while kept.shape[0] > 1:
        kept, sent = halve(bit, kept, came)
        came, bit = swap(sent, "dp", 1 << bit), bit + 1
    shape = [(value_far.shape, BF16)]
    cost = pl.CostEstimate(flops=4 * 10**9, bytes_accessed=2**24, transcendentals=0)
    value_grad = in_vmem(
        add_value_kernel, "value_grad", shape, value_sum, value_far, cost=cost
    )[0]
    came, value_grad = tie((came, value_grad))
    weight_grad = kept[0] + came[0].astype(F32)
    return attn_out[None], query_grad[None], value_grad[None], weight_grad


def solution(mesh):
    return jax.shard_map(
        local,
        mesh=mesh,
        in_specs=(
            P("dp", "blk", None),
            P("dp", "blk", None),
            P(),
            P("dp", "blk", None),
            P("dp", "blk", None),
            P("dp"),
            P("dp", None),
        ),
        out_specs=(
            P("dp", "blk", None),
            P("dp", "blk", None),
            P("dp", "blk", None),
            P(("blk", "dp"), None),
        ),
        check_vma=False,
    )
```

```python
import functools

import jax
import jax.numpy as jnp
from jax import lax
from jax.experimental import pallas as pl
from jax.experimental.pallas import tpu as pltpu
from jax.sharding import PartitionSpec as P

KEY_HEADS = 4
HEAD_SIZE = 128
TILE = 128
HEADS_PER_KEY = 8
LOG2_E = 1.4426950408889634
NEGATIVE_FILLER = -1e30
F32 = jnp.float32
BF16 = jnp.bfloat16
MIB = 1024 * 1024
VMEM = pl.BlockSpec(memory_space=pltpu.VMEM)


def dot(a, b, contract=((1,), (0,))):
    return lax.dot_general(a, b, (contract, ((), ())), preferred_element_type=F32)


def swap(x, axis, mask):
    size = lax.axis_size(axis)
    return lax.ppermute(x, axis, [(i, i ^ mask) for i in range(size)])


def in_hbm(x):
    return pltpu.with_memory_space_constraint(x, pltpu.HBM)


def gather(own, near=None, onward=None):
    blocks = lax.axis_size("blk")
    half = blocks // 2
    masks = range(half - 1, 0, -1)
    far = swap(own, "blk", half)
    pieces = {0: own, half: far}
    pieces.update({m: swap(near[m - 1] if near else own, "blk", m) for m in masks})
    sent = onward(far) if onward else [far] * (half - 1)
    pieces.update({m + half: swap(sent[m - 1], "blk", m) for m in masks})
    return [pieces[m] for m in range(blocks)]


def near_exchange(pieces):
    return [swap(piece, "blk", m) for m, piece in enumerate(pieces, 1)]


def project_kernel(chunks, weight_hbm, visual_hbm, value_hbm, *refs):
    out_ref, near_ref, far_ref, weight, visual_ref, value_ref, sems = refs
    slab = weight.shape[0] // chunks
    copies = [
        pltpu.make_async_copy(visual_hbm, visual_ref, sems.at[chunks]),
        pltpu.make_async_copy(value_hbm, value_ref, sems.at[chunks + 1]),
    ]
    for c in range(chunks):
        part = pl.ds(c * slab, slab)
        copies.append(pltpu.make_async_copy(weight_hbm.at[part], weight.at[part], sems.at[c]))
    for copy in copies:
        copy.start()
    copies[0].wait()
    copies[1].wait()
    block = lax.axis_index("blk")
    rows, width = visual_ref.shape[0], near_ref.shape[1]
    half = near_ref.shape[0] // rows
    for side, ref in enumerate((near_ref, far_ref)):
        for m in range(half):
            start = pl.multiple_of((block ^ (m + side * half)) * width, HEAD_SIZE)
            ref[m * rows : (m + 1) * rows, :] = visual_ref[:, pl.ds(start, width)]
    columns = weight.shape[1]
    out_ref[:, columns:] = value_ref[...]
    keys = jnp.zeros((rows, columns), F32)
    for c in range(chunks):
        copies[2 + c].wait()
        part = slice(c * slab, (c + 1) * slab)
        keys += dot(visual_ref[:, part], weight[part, :])
    out_ref[:, :columns] = keys.astype(BF16)


def project(blocks, visual, key_weight, value):
    rows, features = visual.shape
    columns = key_weight.shape[1]
    chunks = 4
    half = (blocks // 2 * rows, features // blocks)
    shapes = [(rows, columns + value.shape[1]), half, half]
    return pl.pallas_call(
        functools.partial(project_kernel, chunks),
        in_specs=[pl.BlockSpec(memory_space=pltpu.HBM)] * 3,
        out_specs=[VMEM] * 3,
        out_shape=[jax.ShapeDtypeStruct(shape, BF16) for shape in shapes],
        scratch_shapes=[
            pltpu.VMEM(key_weight.shape, BF16),
            pltpu.VMEM(visual.shape, BF16),
            pltpu.VMEM(value.shape, BF16),
            pltpu.SemaphoreType.DMA((chunks + 2,)),
        ],
        cost_estimate=pl.CostEstimate(
            flops=2 * rows * features * columns,
            bytes_accessed=2 * features * columns,
            transcendentals=0,
        ),
        compiler_params=pltpu.CompilerParams(vmem_limit_bytes=32 * MIB),
        name="project",
    )(in_hbm(key_weight), in_hbm(visual), in_hbm(value))


def head_pair(ref, rows, start):
    first = pl.ds(pl.multiple_of(start, HEAD_SIZE), HEAD_SIZE)
    second = pl.ds(pl.multiple_of(start + HEAD_SIZE, HEAD_SIZE), HEAD_SIZE)
    return jnp.concatenate([ref[rows, first], ref[rows, second]], axis=0)


def store_sides(own_ref, near_refs, terms, columns):
    half = len(near_refs) + 1
    rows = own_ref.shape[0] // 2
    for m, ref in enumerate((own_ref, *near_refs)):
        for side in range(2):
            first = (m + side * half) * rows
            part = terms[first : first + rows, :].astype(ref.dtype)
            ref[side * rows : (side + 1) * rows, columns] = part


def scores_kernel(pieces, length_ref, frame_ref, q_ref, g_ref, *refs):
    kv_refs, (w_ref, ds_ref, k_ref, v_ref) = refs[:pieces], refs[pieces : pieces + 4]
    kv_refs = (kv_refs[0], *kv_refs[:0:-1])
    own_ref, near_refs, (kg_acc, bias_ref) = refs[pieces + 4], refs[pieces + 5 : -2], refs[-2:]
    block = lax.axis_index("blk")
    tiles = q_ref.shape[0] // TILE
    rows = kv_refs[0].shape[0]
    width = KEY_HEADS * HEAD_SIZE
    pair = 2 * TILE
    pairs = HEADS_PER_KEY // 2
    span = HEADS_PER_KEY * HEAD_SIZE
    scale = HEAD_SIZE**-0.5
    for m in range(pieces):
        part = slice(m * rows, (m + 1) * rows)
        k_ref[part, :] = kv_refs[m][:, :width]
        v_ref[part, :] = kv_refs[m][:, width:]
    row = lax.broadcasted_iota(jnp.int32, (rows, pair), 0)
    for i in range(tiles):
        text = slice(i * TILE, (i + 1) * TILE)
        limit = jnp.minimum(length_ref[0], TILE * frame_ref[0, block * tiles + i])
        for m in range(pieces):
            live = row + (block ^ m) * rows < limit
            bias_ref[m * rows : (m + 1) * rows, :] = jnp.where(live, 0.0, NEGATIVE_FILLER)

        @pl.loop(0, KEY_HEADS, unroll=True)
        def _(j, i=i, text=text):
            head = pl.ds(pl.multiple_of(j * HEAD_SIZE, HEAD_SIZE), HEAD_SIZE)
            keys, values = k_ref[:, head], v_ref[:, head]
            q_stack, raw, dprobs = [], {}, {}

            def products(p):
                start = j * span + p * pair
                q_stack.append(head_pair(q_ref, text, start))
                raw[p] = dot(keys, q_stack[p], ((1,), (1,)))
                dprobs[p] = dot(values, head_pair(g_ref, text, start), ((1,), (1,)))

            products(0)
            ds_stack = []
            for p in range(pairs):
                if p + 1 < pairs:
                    products(p + 1)
                scores = raw.pop(p) + bias_ref[...]
                peak = jnp.max(scores, axis=0, keepdims=True)
                shifted = jnp.exp2((scores - peak) * (scale * LOG2_E))
                terms = shifted * dprobs.pop(p)
                inverse = 1.0 / jnp.sum(shifted, axis=0, keepdims=True)
                slope = inverse * scale
                offset = jnp.sum(terms, axis=0, keepdims=True) * inverse * slope
                start = (i * KEY_HEADS + j) * span + p * pair
                both = pl.ds(pl.multiple_of(start, HEAD_SIZE), pair)
                w_ref[:, both] = (shifted * inverse).astype(BF16)
                ds_stack.append((terms * slope - shifted * offset).astype(BF16))
                ds_ref[:, both] = ds_stack[p]
            kg = dot(jnp.concatenate(ds_stack, axis=1), jnp.concatenate(q_stack, axis=0))
            if i == 0:
                kg_acc[:, head] = kg
            else:
                kg_acc[:, head] += kg

    store_sides(own_ref, near_refs, kg_acc, slice(None))


def values_kernel(pieces, g_ref, w_ref, own_ref, *refs):
    near_refs, vg_acc = refs[:-1], refs[-1]
    j, i = pl.program_id(0), pl.program_id(1)
    head = pl.ds(pl.multiple_of(j * HEAD_SIZE, HEAD_SIZE), HEAD_SIZE)
    stack = [g_ref[:, h * HEAD_SIZE : (h + 1) * HEAD_SIZE] for h in range(HEADS_PER_KEY)]
    vg = dot(w_ref[...], jnp.concatenate(stack, axis=0))

    @pl.when(i == 0)
    def _():
        vg_acc[...] = vg

    @pl.when(i > 0)
    def _():
        vg_acc[...] += vg

    @pl.when(i == pl.num_programs(1) - 1)
    def _():
        store_sides(own_ref, near_refs, vg_acc, head)


def store_rows(out_ref, left, inner_ref):
    pair = 2 * TILE
    for p in range(HEADS_PER_KEY // 2):
        out = dot(left, inner_ref[:, p * pair : (p + 1) * pair]).T.astype(BF16)
        out_ref[:, p * pair : p * pair + HEAD_SIZE] = out[:TILE]
        out_ref[:, p * pair + HEAD_SIZE : (p + 1) * pair] = out[TILE:]


def rows_kernel(pieces, inner_ref, head_ref, out_ref):
    store_rows(out_ref, head_ref[...].T, inner_ref)


class Attention:
    def __init__(self, queries, pieces, rows):
        self.pieces, self.rows = pieces, rows
        self.text, self.wide = queries.shape
        self.tiles = self.text // TILE
        self.all_rows = pieces * rows
        self.width = KEY_HEADS * HEAD_SIZE
        span = HEADS_PER_KEY * HEAD_SIZE
        self.text_block = pl.BlockSpec((TILE, span), lambda j, i: (i, j))
        self.inner_block = pl.BlockSpec((self.all_rows, span), lambda j, i: (0, i * KEY_HEADS + j))
        self.head_block = pl.BlockSpec((self.all_rows, HEAD_SIZE), lambda j, i: (0, j))
        self.inner = jax.ShapeDtypeStruct((self.all_rows, self.tiles * self.wide), BF16)
        self.sides = (2 * rows, self.width)
        self.terms = [jax.ShapeDtypeStruct(self.sides, F32)]
        self.terms += [jax.ShapeDtypeStruct(self.sides, BF16)] * (pieces // 2 - 1)

    def call(self, kernel, share, name, **specs):
        return pl.pallas_call(
            functools.partial(kernel, self.pieces),
            cost_estimate=pl.CostEstimate(
                flops=int(share * 12 * self.text * self.all_rows * self.wide),
                bytes_accessed=int(share * 8 * self.text * self.wide),
                transcendentals=0,
            ),
            compiler_params=pltpu.CompilerParams(vmem_limit_bytes=32 * MIB),
            name=name,
            **specs,
        )

    def scores(self, length, frames, queries, gradients, keys_values):
        smem = pl.BlockSpec(memory_space=pltpu.SMEM)
        heads = jax.ShapeDtypeStruct((self.all_rows, self.width), BF16)
        out = self.call(
            scores_kernel,
            1.0,
            "scores",
            in_specs=[smem, smem, VMEM, VMEM] + [VMEM] * self.pieces,
            out_specs=[VMEM] * (4 + len(self.terms)),
            out_shape=[self.inner] * 2 + [heads] * 2 + self.terms,
            scratch_shapes=[
                pltpu.VMEM((self.all_rows, self.width), F32),
                pltpu.VMEM((self.all_rows, 2 * TILE), F32),
            ],
        )(length, frames, queries, gradients, keys_values[0], *keys_values[:0:-1])
        return out[:4], out[4], out[5:]

    def values(self, gradients, weights):
        out = self.call(
            values_kernel,
            0.1,
            "values",
            grid=(KEY_HEADS, self.tiles),
            in_specs=[self.text_block, self.inner_block],
            out_specs=[pl.BlockSpec(self.sides, lambda j, i: (0, 0))] * len(self.terms),
            out_shape=self.terms,
            scratch_shapes=[pltpu.VMEM((self.all_rows, HEAD_SIZE), F32)],
        )(in_hbm(gradients), weights)
        return out[0], out[1:]

    def over_rows(self, inner, heads, name):
        return self.call(
            rows_kernel,
            0.1,
            name,
            grid=(KEY_HEADS, self.tiles),
            in_specs=[self.inner_block, self.head_block],
            out_specs=self.text_block,
            out_shape=jax.ShapeDtypeStruct((self.text, self.wide), BF16),
        )(inner, heads)


def in_vmem(kernel, name, out_shape, *arrays, cost=None):
    return pl.pallas_call(
        kernel,
        cost_estimate=cost,
        in_specs=[VMEM] * len(arrays),
        out_specs=[VMEM] * len(out_shape),
        out_shape=[jax.ShapeDtypeStruct(*shape) for shape in out_shape],
        compiler_params=pltpu.CompilerParams(vmem_limit_bytes=32 * MIB),
        name=name,
    )(*arrays)


def sum_kernel(own_ref, *refs):
    came_refs, (near_ref, far_ref) = refs[:-2], refs[-2:]
    rows = near_ref.shape[0]
    for ref, part in ((near_ref, slice(0, rows)), (far_ref, slice(rows, 2 * rows))):
        total = own_ref[part, :]
        for came_ref in came_refs:
            total += came_ref[part, :].astype(F32)
        ref[...] = total.astype(ref.dtype)


def near_sums(own, came, name):
    half = (own.shape[0] // 2, own.shape[1])
    return in_vmem(sum_kernel, name, [(half, F32), (half, BF16)], own, *came)


def add_kernel(near_ref, far_ref, visual_ref, came_ref, own_ref, again_ref, sides_ref, *near_refs):
    rows, columns = own_ref.shape
    width = visual_ref.shape[1]
    total = (near_ref[...] + far_ref[...].astype(F32)).astype(BF16)
    own_ref[...] = total
    again_ref[...] = total
    sides_ref[:rows, :] = visual_ref[:rows, :]
    sides_ref[rows:, :] = came_ref[:rows, :]
    for m, ref in enumerate(near_refs, 1):
        part = slice(m * rows, (m + 1) * rows)
        ref[:, :columns] = total
        ref[:, columns : columns + width] = visual_ref[part, :]
        ref[:, columns + width :] = came_ref[part, :]


def add_far(near, far, visual_near, visual_came):
    rows, columns = far.shape
    width = visual_near.shape[1]
    shapes = [(far.shape, BF16)] * 2 + [((2 * rows, width), BF16)]
    shapes += [((rows, columns + 2 * width), BF16)] * (visual_near.shape[0] // rows - 1)
    out = in_vmem(add_kernel, "key_grad", shapes, near, far, visual_near, visual_came)
    return out[0], out[1], out[2], out[3:]


def onward_kernel(far_ref, *refs):
    value_refs, out_refs = refs[: len(refs) // 2], refs[len(refs) // 2 :]
    rows, columns = far_ref.shape
    for value_ref, ref in zip(value_refs, out_refs):
        ref[:, :columns] = far_ref[...]
        ref[:, columns : 2 * columns] = value_ref[:rows, :]
        ref[:, 2 * columns :] = value_ref[rows:, :]


def onward(far, values):
    shape = (far.shape[0], 3 * far.shape[1])
    return in_vmem(onward_kernel, "onward", [(shape, BF16)] * len(values), far, *values)


def add_value_kernel(near_ref, far_ref, out_ref):
    out_ref[...] = (near_ref[...] + far_ref[...].astype(F32)).astype(BF16)


def turn_kernel(columns, own_ref, *refs):
    came_refs, out_ref = refs[:-1], refs[-1]
    rows, width = own_ref.shape[0] // 2, own_ref.shape[1]
    parts = []
    for side in range(2):
        parts.append(own_ref[side * rows : (side + 1) * rows, :])
        first = columns + side * width
        parts += [ref[:, first : first + width] for ref in came_refs]
    out_ref[...] = jnp.concatenate(parts, axis=0).T


def turn(columns, own, came):
    rows, width = own.shape
    shape = (width, (1 + len(came)) * rows)
    kernel = functools.partial(turn_kernel, columns)
    return in_vmem(kernel, "turn_visual", [(shape, BF16)], own, *came)[0]


def weight_kernel(order, visual_ref, value_ref, *refs):
    pieces = len(order)
    kg_refs = [refs[order.index(m)] for m in range(pieces)]
    keep_ref, send_ref, near_ref, far_ref = refs[pieces:]
    rows, width = near_ref.shape
    product = dot(visual_ref[...], jnp.concatenate([r[:, :width] for r in kg_refs], axis=0))
    count, share, _ = keep_ref.shape
    core = lax.axis_index("dp") % 2 == 0
    for n in range(count):
        even = product[2 * n * share : (2 * n + 1) * share]
        odd = product[(2 * n + 1) * share : (2 * n + 2) * share]
        keep_ref[n] = jnp.where(core, even, odd)
        send_ref[n] = jnp.where(core, odd, even).astype(BF16)
    for side, ref in enumerate((near_ref, far_ref)):
        total = value_ref[side * rows : (side + 1) * rows, :]
        for kg_ref in kg_refs[pieces // 2 + 1 :]:
            total += kg_ref[:, (1 + side) * width : (2 + side) * width].astype(F32)
        ref[...] = total.astype(ref.dtype)


def weight_terms(samples, visual, value_own, key_grads):
    rows, width = key_grads[0].shape
    middle = len(key_grads) // 2
    order = [0, *range(2 * middle - 1, middle, -1), *range(middle - 1, 0, -1), middle]
    half = ((samples // 2, visual.shape[0] // samples, width), F32)
    shapes = [half, (half[0], BF16), ((rows, width), F32), ((rows, width), BF16)]
    kernel = functools.partial(weight_kernel, order)
    ordered = [key_grads[m] for m in order]
    return in_vmem(kernel, "weight_terms", shapes, visual, value_own, *ordered)


def halve_kernel(bit, kept_ref, came_ref, keep_ref, send_ref):
    low = (lax.axis_index("dp") >> bit) % 2 == 0
    for n in range(keep_ref.shape[0]):
        even = kept_ref[2 * n] + came_ref[2 * n].astype(F32)
        odd = kept_ref[2 * n + 1] + came_ref[2 * n + 1].astype(F32)
        keep_ref[n] = jnp.where(low, even, odd)
        send_ref[n] = jnp.where(low, odd, even).astype(BF16)


def halve(bit, kept, came):
    half = (kept.shape[0] // 2, *kept.shape[1:])
    kernel = functools.partial(halve_kernel, bit)
    return in_vmem(kernel, "halve", [(half, F32), (half, BF16)], kept, came)


def local(visual_rows, value_matrix, key_weight, queries, output_gradient, visual_len, frame_end):
    tie = lax.optimization_barrier
    blocks, samples = lax.axis_size("blk"), lax.axis_size("dp")
    visual, half = visual_rows[0], blocks // 2

    own, visual_near, visual_far = project(blocks, visual, key_weight, value_matrix[0])
    keys_values = gather(own)
    visual_far = swap(visual_far, "blk", half)
    attention = Attention(queries[0], blocks, visual.shape[0])
    inner, key_own, key_near = attention.scores(
        visual_len, frame_end, queries[0], output_gradient[0], keys_values
    )
    weights, dscores, keys, values = inner
    key_near, visual_far = tie((key_near, visual_far))

    key_near = near_exchange(key_near)
    value_own, value_near = attention.values(output_gradient[0], weights)
    key_own, value_own = tie((key_own, value_own))
    key_sum, key_far = near_sums(key_own, key_near[::-1], "key_sums")
    key_sum, dscores = tie((key_sum, dscores))
    key_far = swap(key_far, "blk", half)
    query_grad = attention.over_rows(dscores, keys, "query_grad")
    key_sum, query_grad = tie((key_sum, query_grad))
    key_grad, key_again, visual_own, near = add_far(key_sum, key_far, visual_near, visual_far)

    key_grads = gather(key_grad, near, lambda far: onward(far, value_near))
    key_grads[0] = key_again
    attn_out = attention.over_rows(weights, values, "output")
    visual_columns = turn(key_grad.shape[1], visual_own, key_grads[1:half])
    visual_columns, attn_out = tie((visual_columns, attn_out))
    kept, sent, value_sum, value_far = weight_terms(samples, visual_columns, value_own, key_grads)
    value_far = swap(value_far, "blk", half)
    came, bit = swap(sent, "dp", 1), 1
    while kept.shape[0] > 1:
        kept, sent = halve(bit, kept, came)
        came, bit = swap(sent, "dp", 1 << bit), bit + 1
    shape = [(value_far.shape, BF16)]
    cost = pl.CostEstimate(flops=4 * 10**9, bytes_accessed=2**24, transcendentals=0)
    value_grad = in_vmem(
        add_value_kernel, "value_grad", shape, value_sum, value_far, cost=cost
    )[0]
    came, value_grad = tie((came, value_grad))
    weight_grad = kept[0] + came[0].astype(F32)
    return attn_out[None], query_grad[None], value_grad[None], weight_grad


def solution(mesh):
    return jax.shard_map(
        local,
        mesh=mesh,
        in_specs=(
            P("dp", "blk", None),
            P("dp", "blk", None),
            P(),
            P("dp", "blk", None),
            P("dp", "blk", None),
            P("dp"),
            P("dp", None),
        ),
        out_specs=(
            P("dp", "blk", None),
            P("dp", "blk", None),
            P("dp", "blk", None),
            P(("blk", "dp"), None),
        ),
        check_vma=False,
    )
```

```python
import functools

import jax
import jax.numpy as jnp
from jax import lax
from jax.experimental import pallas as pl
from jax.experimental.pallas import tpu as pltpu
from jax.sharding import PartitionSpec as P

KEY_HEADS = 4
HEAD_SIZE = 128
TILE = 128
HEADS_PER_KEY = 8
LOG2_E = 1.4426950408889634
NEGATIVE_FILLER = -1e30
F32 = jnp.float32
BF16 = jnp.bfloat16
MIB = 1024 * 1024
VMEM = pl.BlockSpec(memory_space=pltpu.VMEM)


def dot(a, b, contract=((1,), (0,))):
    return lax.dot_general(a, b, (contract, ((), ())), preferred_element_type=F32)


def swap(x, axis, mask):
    size = lax.axis_size(axis)
    return lax.ppermute(x, axis, [(i, i ^ mask) for i in range(size)])


def in_hbm(x):
    return pltpu.with_memory_space_constraint(x, pltpu.HBM)


def gather(own, near=None, onward=None):
    blocks = lax.axis_size("blk")
    half = blocks // 2
    masks = range(half - 1, 0, -1)
    far = swap(own, "blk", half)
    pieces = {0: own, half: far}
    pieces.update({m: swap(near[m - 1] if near else own, "blk", m) for m in masks})
    sent = onward(far) if onward else [far] * (half - 1)
    pieces.update({m + half: swap(sent[m - 1], "blk", m) for m in masks})
    return [pieces[m] for m in range(blocks)]


def near_exchange(pieces):
    return [swap(piece, "blk", m) for m, piece in enumerate(pieces, 1)]


def project_kernel(chunks, weight_hbm, visual_hbm, value_hbm, *refs):
    out_ref, near_ref, far_ref, weight, visual_ref, value_ref, sems = refs
    slab = weight.shape[0] // chunks
    copies = [
        pltpu.make_async_copy(visual_hbm, visual_ref, sems.at[chunks]),
        pltpu.make_async_copy(value_hbm, value_ref, sems.at[chunks + 1]),
    ]
    for c in range(chunks):
        part = pl.ds(c * slab, slab)
        copies.append(pltpu.make_async_copy(weight_hbm.at[part], weight.at[part], sems.at[c]))
    for copy in copies:
        copy.start()
    copies[0].wait()
    copies[1].wait()
    block = lax.axis_index("blk")
    rows, width = visual_ref.shape[0], near_ref.shape[1]
    half = near_ref.shape[0] // rows
    for side, ref in enumerate((near_ref, far_ref)):
        for m in range(half):
            start = pl.multiple_of((block ^ (m + side * half)) * width, HEAD_SIZE)
            ref[m * rows : (m + 1) * rows, :] = visual_ref[:, pl.ds(start, width)]
    columns = weight.shape[1]
    out_ref[:, columns:] = value_ref[...]
    keys = jnp.zeros((rows, columns), F32)
    for c in range(chunks):
        copies[2 + c].wait()
        part = slice(c * slab, (c + 1) * slab)
        keys += dot(visual_ref[:, part], weight[part, :])
    out_ref[:, :columns] = keys.astype(BF16)


def project(blocks, visual, key_weight, value):
    rows, features = visual.shape
    columns = key_weight.shape[1]
    chunks = 4
    half = (blocks // 2 * rows, features // blocks)
    shapes = [(rows, columns + value.shape[1]), half, half]
    return pl.pallas_call(
        functools.partial(project_kernel, chunks),
        in_specs=[pl.BlockSpec(memory_space=pltpu.HBM)] * 3,
        out_specs=[VMEM] * 3,
        out_shape=[jax.ShapeDtypeStruct(shape, BF16) for shape in shapes],
        scratch_shapes=[
            pltpu.VMEM(key_weight.shape, BF16),
            pltpu.VMEM(visual.shape, BF16),
            pltpu.VMEM(value.shape, BF16),
            pltpu.SemaphoreType.DMA((chunks + 2,)),
        ],
        cost_estimate=pl.CostEstimate(
            flops=2 * rows * features * columns,
            bytes_accessed=2 * features * columns,
            transcendentals=0,
        ),
        compiler_params=pltpu.CompilerParams(vmem_limit_bytes=32 * MIB),
        name="project",
    )(in_hbm(key_weight), in_hbm(visual), in_hbm(value))


def head_pair(ref, rows, start):
    first = pl.ds(pl.multiple_of(start, HEAD_SIZE), HEAD_SIZE)
    second = pl.ds(pl.multiple_of(start + HEAD_SIZE, HEAD_SIZE), HEAD_SIZE)
    return jnp.concatenate([ref[rows, first], ref[rows, second]], axis=0)


def store_sides(own_ref, near_refs, terms, columns):
    half = len(near_refs) + 1
    rows = own_ref.shape[0] // 2
    for m, ref in enumerate((own_ref, *near_refs)):
        for side in range(2):
            first = (m + side * half) * rows
            part = terms[first : first + rows, :].astype(ref.dtype)
            ref[side * rows : (side + 1) * rows, columns] = part


def scores_kernel(pieces, length_ref, frame_ref, q_ref, g_ref, *refs):
    kv_refs, (w_ref, ds_ref, k_ref, v_ref) = refs[:pieces], refs[pieces : pieces + 4]
    kv_refs = (kv_refs[0], *kv_refs[:0:-1])
    own_ref, near_refs, (kg_acc, bias_ref) = refs[pieces + 4], refs[pieces + 5 : -2], refs[-2:]
    block = lax.axis_index("blk")
    tiles = q_ref.shape[0] // TILE
    rows = kv_refs[0].shape[0]
    width = KEY_HEADS * HEAD_SIZE
    pair = 2 * TILE
    pairs = HEADS_PER_KEY // 2
    span = HEADS_PER_KEY * HEAD_SIZE
    scale = HEAD_SIZE**-0.5
    for m in range(pieces):
        part = slice(m * rows, (m + 1) * rows)
        k_ref[part, :] = kv_refs[m][:, :width]
        v_ref[part, :] = kv_refs[m][:, width:]
    row = lax.broadcasted_iota(jnp.int32, (rows, pair), 0)
    for i in range(tiles):
        text = slice(i * TILE, (i + 1) * TILE)
        limit = jnp.minimum(length_ref[0], TILE * frame_ref[0, block * tiles + i])
        for m in range(pieces):
            live = row + (block ^ m) * rows < limit
            bias_ref[m * rows : (m + 1) * rows, :] = jnp.where(live, 0.0, NEGATIVE_FILLER)

        @pl.loop(0, KEY_HEADS, unroll=True)
        def _(j, i=i, text=text):
            head = pl.ds(pl.multiple_of(j * HEAD_SIZE, HEAD_SIZE), HEAD_SIZE)
            keys, values = k_ref[:, head], v_ref[:, head]
            q_stack, raw, dprobs = [], {}, {}

            def products(p):
                start = j * span + p * pair
                q_stack.append(head_pair(q_ref, text, start))
                raw[p] = dot(keys, q_stack[p], ((1,), (1,)))
                dprobs[p] = dot(values, head_pair(g_ref, text, start), ((1,), (1,)))

            products(0)
            ds_stack = []
            for p in range(pairs):
                if p + 1 < pairs:
                    products(p + 1)
                scores = raw.pop(p) + bias_ref[...]
                peak = jnp.max(scores, axis=0, keepdims=True)
                shifted = jnp.exp2((scores - peak) * (scale * LOG2_E))
                inverse = 1.0 / jnp.sum(shifted, axis=0, keepdims=True)
                change = dprobs.pop(p)
                delta = jnp.sum(shifted * change, axis=0, keepdims=True) * inverse
                probs = shifted * inverse
                start = (i * KEY_HEADS + j) * span + p * pair
                both = pl.ds(pl.multiple_of(start, HEAD_SIZE), pair)
                w_ref[:, both] = probs.astype(BF16)
                ds_stack.append((probs * (change - delta)).astype(BF16))
                ds_ref[:, both] = ds_stack[p]
            kg = dot(jnp.concatenate(ds_stack, axis=1), jnp.concatenate(q_stack, axis=0)) * scale
            if i == 0:
                kg_acc[:, head] = kg
            else:
                kg_acc[:, head] += kg

    store_sides(own_ref, near_refs, kg_acc, slice(None))


def values_kernel(pieces, g_ref, w_ref, own_ref, *near_refs):
    span = HEADS_PER_KEY * HEAD_SIZE
    for j in range(KEY_HEADS):
        total = 0.0
        for i in range(g_ref.shape[0] // TILE):
            text = slice(i * TILE, (i + 1) * TILE)
            starts = range(j * span, (j + 1) * span, HEAD_SIZE)
            stack = [g_ref[text, start : start + HEAD_SIZE] for start in starts]
            first = (i * KEY_HEADS + j) * span
            total += dot(w_ref[:, first : first + span], jnp.concatenate(stack, axis=0))
        store_sides(own_ref, near_refs, total, slice(j * HEAD_SIZE, (j + 1) * HEAD_SIZE))


def rows_kernel(factor, pieces, inner_ref, head_ref, out_ref):
    left = head_ref[...].T
    pair = 2 * TILE
    for p in range(HEADS_PER_KEY // 2):
        out = dot(left, inner_ref[:, p * pair : (p + 1) * pair])
        if factor is not None:
            out *= factor
        out = out.T.astype(BF16)
        out_ref[:, p * pair : p * pair + HEAD_SIZE] = out[:TILE]
        out_ref[:, p * pair + HEAD_SIZE : (p + 1) * pair] = out[TILE:]


class Attention:
    def __init__(self, queries, pieces, rows):
        self.pieces, self.rows = pieces, rows
        self.text, self.wide = queries.shape
        self.tiles = self.text // TILE
        self.all_rows = pieces * rows
        self.width = KEY_HEADS * HEAD_SIZE
        span = HEADS_PER_KEY * HEAD_SIZE
        self.text_block = pl.BlockSpec((TILE, span), lambda j, i: (i, j))
        self.inner_block = pl.BlockSpec((self.all_rows, span), lambda j, i: (0, i * KEY_HEADS + j))
        self.head_block = pl.BlockSpec((self.all_rows, HEAD_SIZE), lambda j, i: (0, j))
        self.inner = jax.ShapeDtypeStruct((self.all_rows, self.tiles * self.wide), BF16)
        self.sides = (2 * rows, self.width)
        self.terms = [jax.ShapeDtypeStruct(self.sides, F32)]
        self.terms += [jax.ShapeDtypeStruct(self.sides, BF16)] * (pieces // 2 - 1)

    def call(self, kernel, share, name, **specs):
        return pl.pallas_call(
            functools.partial(kernel, self.pieces),
            cost_estimate=pl.CostEstimate(
                flops=int(share * 12 * self.text * self.all_rows * self.wide),
                bytes_accessed=int(share * 8 * self.text * self.wide),
                transcendentals=0,
            ),
            compiler_params=pltpu.CompilerParams(vmem_limit_bytes=32 * MIB),
            name=name,
            **specs,
        )

    def scores(self, length, frames, queries, gradients, keys_values):
        smem = pl.BlockSpec(memory_space=pltpu.SMEM)
        heads = jax.ShapeDtypeStruct((self.all_rows, self.width), BF16)
        out = self.call(
            scores_kernel,
            1.0,
            "scores",
            in_specs=[smem, smem, VMEM, VMEM] + [VMEM] * self.pieces,
            out_specs=[VMEM] * (4 + len(self.terms)),
            out_shape=[self.inner] * 2 + [heads] * 2 + self.terms,
            scratch_shapes=[
                pltpu.VMEM((self.all_rows, self.width), F32),
                pltpu.VMEM((self.all_rows, 2 * TILE), F32),
            ],
        )(length, frames, queries, gradients, keys_values[0], *keys_values[:0:-1])
        return out[:4], out[4], out[5:]

    def values(self, gradients, weights):
        out = self.call(
            values_kernel,
            0.1,
            "values",
            in_specs=[VMEM] * 2,
            out_specs=[VMEM] * len(self.terms),
            out_shape=self.terms,
        )(gradients, weights)
        return out[0], out[1:]

    def over_rows(self, inner, heads, name, factor=None):
        return self.call(
            functools.partial(rows_kernel, factor),
            0.1,
            name,
            grid=(KEY_HEADS, self.tiles),
            in_specs=[self.inner_block, self.head_block],
            out_specs=self.text_block,
            out_shape=jax.ShapeDtypeStruct((self.text, self.wide), BF16),
        )(inner, heads)


def in_vmem(kernel, name, out_shape, *arrays, cost=None):
    return pl.pallas_call(
        kernel,
        cost_estimate=cost,
        in_specs=[VMEM] * len(arrays),
        out_specs=[VMEM] * len(out_shape),
        out_shape=[jax.ShapeDtypeStruct(*shape) for shape in out_shape],
        compiler_params=pltpu.CompilerParams(vmem_limit_bytes=32 * MIB),
        name=name,
    )(*arrays)


def sum_kernel(own_ref, *refs):
    came_refs, (near_ref, far_ref) = refs[:-2], refs[-2:]
    rows = near_ref.shape[0]
    for ref, part in ((near_ref, slice(0, rows)), (far_ref, slice(rows, 2 * rows))):
        total = own_ref[part, :]
        for came_ref in came_refs:
            total += came_ref[part, :].astype(F32)
        ref[...] = total.astype(ref.dtype)


def near_sums(own, came, name):
    half = (own.shape[0] // 2, own.shape[1])
    return in_vmem(sum_kernel, name, [(half, F32), (half, BF16)], own, *came)


def add_kernel(near_ref, far_ref, visual_ref, came_ref, own_ref, again_ref, sides_ref, *near_refs):
    rows, columns = own_ref.shape
    width = visual_ref.shape[1]
    total = (near_ref[...] + far_ref[...].astype(F32)).astype(BF16)
    own_ref[...] = total
    again_ref[...] = total
    sides_ref[:rows, :] = visual_ref[:rows, :]
    sides_ref[rows:, :] = came_ref[:rows, :]
    for m, ref in enumerate(near_refs, 1):
        part = slice(m * rows, (m + 1) * rows)
        ref[:, :columns] = total
        ref[:, columns : columns + width] = visual_ref[part, :]
        ref[:, columns + width :] = came_ref[part, :]


def add_far(near, far, visual_near, visual_came):
    rows, columns = far.shape
    width = visual_near.shape[1]
    shapes = [(far.shape, BF16)] * 2 + [((2 * rows, width), BF16)]
    shapes += [((rows, columns + 2 * width), BF16)] * (visual_near.shape[0] // rows - 1)
    out = in_vmem(add_kernel, "key_grad", shapes, near, far, visual_near, visual_came)
    return out[0], out[1], out[2], out[3:]


def onward_kernel(far_ref, *refs):
    value_refs, out_refs = refs[: len(refs) // 2], refs[len(refs) // 2 :]
    rows, columns = far_ref.shape
    for value_ref, ref in zip(value_refs, out_refs):
        ref[:, :columns] = far_ref[...]
        ref[:, columns : 2 * columns] = value_ref[:rows, :]
        ref[:, 2 * columns :] = value_ref[rows:, :]


def onward(far, values):
    shape = (far.shape[0], 3 * far.shape[1])
    return in_vmem(onward_kernel, "onward", [(shape, BF16)] * len(values), far, *values)


def add_value_kernel(near_ref, far_ref, out_ref):
    out_ref[...] = (near_ref[...] + far_ref[...].astype(F32)).astype(BF16)


def turn_kernel(columns, own_ref, *refs):
    came_refs, out_ref = refs[:-1], refs[-1]
    rows, width = own_ref.shape[0] // 2, own_ref.shape[1]
    parts = []
    for side in range(2):
        parts.append(own_ref[side * rows : (side + 1) * rows, :])
        first = columns + side * width
        parts += [ref[:, first : first + width] for ref in came_refs]
    out_ref[...] = jnp.concatenate(parts, axis=0).T


def turn(columns, own, came):
    rows, width = own.shape
    shape = (width, (1 + len(came)) * rows)
    kernel = functools.partial(turn_kernel, columns)
    return in_vmem(kernel, "turn_visual", [(shape, BF16)], own, *came)[0]


def weight_kernel(order, visual_ref, value_ref, *refs):
    pieces = len(order)
    kg_refs = [refs[order.index(m)] for m in range(pieces)]
    keep_ref, send_ref, near_ref, far_ref = refs[pieces:]
    rows, width = near_ref.shape
    product = dot(visual_ref[...], jnp.concatenate([r[:, :width] for r in kg_refs], axis=0))
    count, share, _ = keep_ref.shape
    core = lax.axis_index("dp") % 2 == 0
    for n in range(count):
        even = product[2 * n * share : (2 * n + 1) * share]
        odd = product[(2 * n + 1) * share : (2 * n + 2) * share]
        keep_ref[n] = jnp.where(core, even, odd)
        send_ref[n] = jnp.where(core, odd, even).astype(BF16)
    for side, ref in enumerate((near_ref, far_ref)):
        total = value_ref[side * rows : (side + 1) * rows, :]
        for kg_ref in kg_refs[pieces // 2 + 1 :]:
            total += kg_ref[:, (1 + side) * width : (2 + side) * width].astype(F32)
        ref[...] = total.astype(ref.dtype)


def weight_terms(samples, visual, value_own, key_grads):
    rows, width = key_grads[0].shape
    middle = len(key_grads) // 2
    order = [0, *range(2 * middle - 1, middle, -1), *range(middle - 1, 0, -1), middle]
    half = ((samples // 2, visual.shape[0] // samples, width), F32)
    shapes = [half, (half[0], BF16), ((rows, width), F32), ((rows, width), BF16)]
    kernel = functools.partial(weight_kernel, order)
    ordered = [key_grads[m] for m in order]
    return in_vmem(kernel, "weight_terms", shapes, visual, value_own, *ordered)


def halve_kernel(bit, kept_ref, came_ref, keep_ref, send_ref):
    low = (lax.axis_index("dp") >> bit) % 2 == 0
    for n in range(keep_ref.shape[0]):
        even = kept_ref[2 * n] + came_ref[2 * n].astype(F32)
        odd = kept_ref[2 * n + 1] + came_ref[2 * n + 1].astype(F32)
        keep_ref[n] = jnp.where(low, even, odd)
        send_ref[n] = jnp.where(low, odd, even).astype(BF16)


def halve(bit, kept, came):
    half = (kept.shape[0] // 2, *kept.shape[1:])
    kernel = functools.partial(halve_kernel, bit)
    return in_vmem(kernel, "halve", [(half, F32), (half, BF16)], kept, came)


def local(visual_rows, value_matrix, key_weight, queries, output_gradient, visual_len, frame_end):
    tie = lax.optimization_barrier
    blocks, samples = lax.axis_size("blk"), lax.axis_size("dp")
    visual, half = visual_rows[0], blocks // 2

    own, visual_near, visual_far = project(blocks, visual, key_weight, value_matrix[0])
    keys_values = gather(own)
    visual_far = swap(visual_far, "blk", half)
    attention = Attention(queries[0], blocks, visual.shape[0])
    inner, key_own, key_near = attention.scores(
        visual_len, frame_end, queries[0], output_gradient[0], keys_values
    )
    weights, dscores, keys, values = inner
    key_near, visual_far = tie((key_near, visual_far))

    key_near = near_exchange(key_near)
    value_own, value_near = attention.values(output_gradient[0], weights)
    key_own, value_own = tie((key_own, value_own))
    key_sum, key_far = near_sums(key_own, key_near[::-1], "key_sums")
    key_sum, dscores = tie((key_sum, dscores))
    key_far = swap(key_far, "blk", half)
    query_grad = attention.over_rows(dscores, keys, "query_grad", HEAD_SIZE**-0.5)
    key_sum, query_grad = tie((key_sum, query_grad))
    key_grad, key_again, visual_own, near = add_far(key_sum, key_far, visual_near, visual_far)

    key_grads = gather(key_grad, near, lambda far: onward(far, value_near))
    key_grads[0] = key_again
    attn_out = attention.over_rows(weights, values, "output")
    visual_columns = turn(key_grad.shape[1], visual_own, key_grads[1:half])
    visual_columns, attn_out = tie((visual_columns, attn_out))
    kept, sent, value_sum, value_far = weight_terms(samples, visual_columns, value_own, key_grads)
    value_far = swap(value_far, "blk", half)
    came, bit = swap(sent, "dp", 1), 1
    while kept.shape[0] > 1:
        kept, sent = halve(bit, kept, came)
        came, bit = swap(sent, "dp", 1 << bit), bit + 1
    shape = [(value_far.shape, BF16)]
    cost = pl.CostEstimate(flops=4 * 10**9, bytes_accessed=2**24, transcendentals=0)
    value_grad = in_vmem(
        add_value_kernel, "value_grad", shape, value_sum, value_far, cost=cost
    )[0]
    came, value_grad = tie((came, value_grad))
    weight_grad = kept[0] + came[0].astype(F32)
    return attn_out[None], query_grad[None], value_grad[None], weight_grad


def solution(mesh):
    return jax.shard_map(
        local,
        mesh=mesh,
        in_specs=(
            P("dp", "blk", None),
            P("dp", "blk", None),
            P(),
            P("dp", "blk", None),
            P("dp", "blk", None),
            P("dp"),
            P("dp", None),
        ),
        out_specs=(
            P("dp", "blk", None),
            P("dp", "blk", None),
            P("dp", "blk", None),
            P(("blk", "dp"), None),
        ),
        check_vma=False,
    )
```

```python
import functools

import jax
import jax.numpy as jnp
from jax import lax
from jax.experimental import pallas as pl
from jax.experimental.pallas import tpu as pltpu
from jax.sharding import PartitionSpec as P

KEY_HEADS = 4
HEAD_SIZE = 128
TILE = 128
HEADS_PER_KEY = 8
LOG2_E = 1.4426950408889634
NEGATIVE_FILLER = -1e30
F32 = jnp.float32
BF16 = jnp.bfloat16
MIB = 1024 * 1024
VMEM = pl.BlockSpec(memory_space=pltpu.VMEM)


def dot(a, b, contract=((1,), (0,))):
    return lax.dot_general(a, b, (contract, ((), ())), preferred_element_type=F32)


def swap(x, axis, mask):
    size = lax.axis_size(axis)
    return lax.ppermute(x, axis, [(i, i ^ mask) for i in range(size)])


def in_hbm(x):
    return pltpu.with_memory_space_constraint(x, pltpu.HBM)


def gather(own, near=None, onward=None):
    blocks = lax.axis_size("blk")
    half = blocks // 2
    masks = range(half - 1, 0, -1)
    far = swap(own, "blk", half)
    pieces = {0: own, half: far}
    pieces.update({m: swap(near[m - 1] if near else own, "blk", m) for m in masks})
    sent = onward(far) if onward else [far] * (half - 1)
    pieces.update({m + half: swap(sent[m - 1], "blk", m) for m in masks})
    return [pieces[m] for m in range(blocks)]


def near_exchange(pieces):
    return [swap(piece, "blk", m) for m, piece in enumerate(pieces, 1)]


def project_kernel(chunks, weight_hbm, visual_hbm, value_hbm, *refs):
    out_ref, near_ref, far_ref, weight, visual_ref, value_ref, sems = refs
    slab = weight.shape[0] // chunks
    copies = [
        pltpu.make_async_copy(visual_hbm, visual_ref, sems.at[chunks]),
        pltpu.make_async_copy(value_hbm, value_ref, sems.at[chunks + 1]),
    ]
    for c in range(chunks):
        part = pl.ds(c * slab, slab)
        copies.append(pltpu.make_async_copy(weight_hbm.at[part], weight.at[part], sems.at[c]))
    for copy in copies:
        copy.start()
    copies[0].wait()
    copies[1].wait()
    block = lax.axis_index("blk")
    rows, width = visual_ref.shape[0], near_ref.shape[1]
    half = near_ref.shape[0] // rows
    for side, ref in enumerate((near_ref, far_ref)):
        for m in range(half):
            start = pl.multiple_of((block ^ (m + side * half)) * width, HEAD_SIZE)
            ref[m * rows : (m + 1) * rows, :] = visual_ref[:, pl.ds(start, width)]
    columns = weight.shape[1]
    out_ref[:, columns:] = value_ref[...]
    keys = jnp.zeros((rows, columns), F32)
    for c in range(chunks):
        copies[2 + c].wait()
        part = slice(c * slab, (c + 1) * slab)
        keys += dot(visual_ref[:, part], weight[part, :])
    out_ref[:, :columns] = keys.astype(BF16)


def project(blocks, visual, key_weight, value):
    rows, features = visual.shape
    columns = key_weight.shape[1]
    chunks = 4
    half = (blocks // 2 * rows, features // blocks)
    shapes = [(rows, columns + value.shape[1]), half, half]
    return pl.pallas_call(
        functools.partial(project_kernel, chunks),
        in_specs=[pl.BlockSpec(memory_space=pltpu.HBM)] * 3,
        out_specs=[VMEM] * 3,
        out_shape=[jax.ShapeDtypeStruct(shape, BF16) for shape in shapes],
        scratch_shapes=[
            pltpu.VMEM(key_weight.shape, BF16),
            pltpu.VMEM(visual.shape, BF16),
            pltpu.VMEM(value.shape, BF16),
            pltpu.SemaphoreType.DMA((chunks + 2,)),
        ],
        cost_estimate=pl.CostEstimate(
            flops=2 * rows * features * columns,
            bytes_accessed=2 * features * columns,
            transcendentals=0,
        ),
        compiler_params=pltpu.CompilerParams(vmem_limit_bytes=32 * MIB),
        name="project",
    )(in_hbm(key_weight), in_hbm(visual), in_hbm(value))


def head_pair(ref, rows, start):
    first = pl.ds(pl.multiple_of(start, HEAD_SIZE), HEAD_SIZE)
    second = pl.ds(pl.multiple_of(start + HEAD_SIZE, HEAD_SIZE), HEAD_SIZE)
    return jnp.concatenate([ref[rows, first], ref[rows, second]], axis=0)


def store_sides(own_ref, near_refs, terms, columns):
    half = len(near_refs) + 1
    rows = own_ref.shape[0] // 2
    for m, ref in enumerate((own_ref, *near_refs)):
        for side in range(2):
            first = (m + side * half) * rows
            part = terms[first : first + rows, :].astype(ref.dtype)
            ref[side * rows : (side + 1) * rows, columns] = part


def scores_kernel(pieces, length_ref, frame_ref, q_ref, g_ref, *refs):
    kv_refs, (w_ref, ds_ref, k_ref, v_ref) = refs[:pieces], refs[pieces : pieces + 4]
    kv_refs = (kv_refs[0], *kv_refs[:0:-1])
    own_ref, near_refs, (kg_acc, bias_ref) = refs[pieces + 4], refs[pieces + 5 : -2], refs[-2:]
    block = lax.axis_index("blk")
    tiles = q_ref.shape[0] // TILE
    rows = kv_refs[0].shape[0]
    width = KEY_HEADS * HEAD_SIZE
    pair = 2 * TILE
    pairs = HEADS_PER_KEY // 2
    span = HEADS_PER_KEY * HEAD_SIZE
    scale = HEAD_SIZE**-0.5
    for m in range(pieces):
        part = slice(m * rows, (m + 1) * rows)
        k_ref[part, :] = kv_refs[m][:, :width]
        v_ref[part, :] = kv_refs[m][:, width:]
    row = lax.broadcasted_iota(jnp.int32, (rows, pair), 0)
    for i in range(tiles):
        text = slice(i * TILE, (i + 1) * TILE)
        limit = jnp.minimum(length_ref[0], TILE * frame_ref[0, block * tiles + i])
        for m in range(pieces):
            live = row + (block ^ m) * rows < limit
            bias_ref[m * rows : (m + 1) * rows, :] = jnp.where(live, 0.0, NEGATIVE_FILLER)

        @pl.loop(0, KEY_HEADS, unroll=True)
        def _(j, i=i, text=text):
            head = pl.ds(pl.multiple_of(j * HEAD_SIZE, HEAD_SIZE), HEAD_SIZE)
            keys, values = k_ref[:, head], v_ref[:, head]
            q_stack, raw, dprobs = [], {}, {}

            def products(p):
                start = j * span + p * pair
                q_stack.append(head_pair(q_ref, text, start))
                raw[p] = dot(keys, q_stack[p], ((1,), (1,)))
                dprobs[p] = dot(values, head_pair(g_ref, text, start), ((1,), (1,)))

            products(0)
            ds_stack = []
            for p in range(pairs):
                if p + 1 < pairs:
                    products(p + 1)
                scores = raw.pop(p) + bias_ref[...]
                peak = jnp.max(scores, axis=0, keepdims=True)
                shifted = jnp.exp2((scores - peak) * (scale * LOG2_E))
                inverse = 1.0 / jnp.sum(shifted, axis=0, keepdims=True)
                change = dprobs.pop(p)
                delta = jnp.sum(shifted * change, axis=0, keepdims=True) * inverse
                probs = shifted * inverse
                start = (i * KEY_HEADS + j) * span + p * pair
                both = pl.ds(pl.multiple_of(start, HEAD_SIZE), pair)
                w_ref[:, both] = probs.astype(BF16)
                ds_stack.append((probs * (change - delta)).astype(BF16))
                ds_ref[:, both] = ds_stack[p]
            kg = dot(jnp.concatenate(ds_stack, axis=1), jnp.concatenate(q_stack, axis=0)) * scale
            if i == 0:
                kg_acc[:, head] = kg
            else:
                kg_acc[:, head] += kg

    store_sides(own_ref, near_refs, kg_acc, slice(None))


def values_kernel(pieces, g_ref, w_ref, own_ref, *near_refs):
    span = HEADS_PER_KEY * HEAD_SIZE
    for j in range(KEY_HEADS):
        total = 0.0
        for i in range(g_ref.shape[0] // TILE):
            text = slice(i * TILE, (i + 1) * TILE)
            starts = range(j * span, (j + 1) * span, HEAD_SIZE)
            stack = [g_ref[text, start : start + HEAD_SIZE] for start in starts]
            first = (i * KEY_HEADS + j) * span
            total += dot(w_ref[:, first : first + span], jnp.concatenate(stack, axis=0))
        store_sides(own_ref, near_refs, total, slice(j * HEAD_SIZE, (j + 1) * HEAD_SIZE))


def rows_kernel(factor, pieces, inner_ref, head_ref, out_ref):
    left = head_ref[...].T
    pair = 2 * TILE
    for p in range(HEADS_PER_KEY // 2):
        out = dot(left, inner_ref[:, p * pair : (p + 1) * pair])
        if factor is not None:
            out *= factor
        out = out.T.astype(BF16)
        out_ref[:, p * pair : p * pair + HEAD_SIZE] = out[:TILE]
        out_ref[:, p * pair + HEAD_SIZE : (p + 1) * pair] = out[TILE:]


class Attention:
    def __init__(self, queries, pieces, rows):
        self.pieces, self.rows = pieces, rows
        self.text, self.wide = queries.shape
        self.tiles = self.text // TILE
        self.all_rows = pieces * rows
        self.width = KEY_HEADS * HEAD_SIZE
        span = HEADS_PER_KEY * HEAD_SIZE
        self.text_block = pl.BlockSpec((TILE, span), lambda j, i: (i, j))
        self.inner_block = pl.BlockSpec((self.all_rows, span), lambda j, i: (0, i * KEY_HEADS + j))
        self.head_block = pl.BlockSpec((self.all_rows, HEAD_SIZE), lambda j, i: (0, j))
        self.inner = jax.ShapeDtypeStruct((self.all_rows, self.tiles * self.wide), BF16)
        self.sides = (2 * rows, self.width)
        self.terms = [jax.ShapeDtypeStruct(self.sides, F32)]
        self.terms += [jax.ShapeDtypeStruct(self.sides, BF16)] * (pieces // 2 - 1)

    def call(self, kernel, share, name, **specs):
        return pl.pallas_call(
            functools.partial(kernel, self.pieces),
            cost_estimate=pl.CostEstimate(
                flops=int(share * 12 * self.text * self.all_rows * self.wide),
                bytes_accessed=int(share * 8 * self.text * self.wide),
                transcendentals=0,
            ),
            compiler_params=pltpu.CompilerParams(vmem_limit_bytes=32 * MIB),
            name=name,
            **specs,
        )

    def scores(self, length, frames, queries, gradients, keys_values):
        smem = pl.BlockSpec(memory_space=pltpu.SMEM)
        heads = jax.ShapeDtypeStruct((self.all_rows, self.width), BF16)
        out = self.call(
            scores_kernel,
            1.0,
            "scores",
            in_specs=[smem, smem, VMEM, VMEM] + [VMEM] * self.pieces,
            out_specs=[VMEM] * (4 + len(self.terms)),
            out_shape=[self.inner] * 2 + [heads] * 2 + self.terms,
            scratch_shapes=[
                pltpu.VMEM((self.all_rows, self.width), F32),
                pltpu.VMEM((self.all_rows, 2 * TILE), F32),
            ],
        )(length, frames, queries, gradients, keys_values[0], *keys_values[:0:-1])
        return out[:4], out[4], out[5:]

    def values(self, gradients, weights):
        out = self.call(
            values_kernel,
            0.1,
            "values",
            in_specs=[VMEM] * 2,
            out_specs=[VMEM] * len(self.terms),
            out_shape=self.terms,
        )(gradients, weights)
        return out[0], out[1:]

    def over_rows(self, inner, heads, name, factor=None):
        return self.call(
            functools.partial(rows_kernel, factor),
            0.1,
            name,
            grid=(KEY_HEADS, self.tiles),
            in_specs=[self.inner_block, self.head_block],
            out_specs=self.text_block,
            out_shape=jax.ShapeDtypeStruct((self.text, self.wide), BF16),
        )(inner, heads)


def in_vmem(kernel, name, out_shape, *arrays, cost=None):
    return pl.pallas_call(
        kernel,
        cost_estimate=cost,
        in_specs=[VMEM] * len(arrays),
        out_specs=[VMEM] * len(out_shape),
        out_shape=[jax.ShapeDtypeStruct(*shape) for shape in out_shape],
        compiler_params=pltpu.CompilerParams(vmem_limit_bytes=32 * MIB),
        name=name,
    )(*arrays)


def sum_kernel(own_ref, *refs):
    came_refs, (near_ref, far_ref) = refs[:-2], refs[-2:]
    rows = near_ref.shape[0]
    for ref, part in ((near_ref, slice(0, rows)), (far_ref, slice(rows, 2 * rows))):
        total = own_ref[part, :]
        for came_ref in came_refs:
            total += came_ref[part, :].astype(F32)
        ref[...] = total.astype(ref.dtype)


def near_sums(own, came, name):
    half = (own.shape[0] // 2, own.shape[1])
    return in_vmem(sum_kernel, name, [(half, F32), (half, BF16)], own, *came)


def add_kernel(near_ref, far_ref, visual_ref, came_ref, own_ref, again_ref, sides_ref, *near_refs):
    rows, columns = own_ref.shape
    width = visual_ref.shape[1]
    total = (near_ref[...] + far_ref[...].astype(F32)).astype(BF16)
    own_ref[...] = total
    again_ref[...] = total
    sides_ref[:rows, :] = visual_ref[:rows, :]
    sides_ref[rows:, :] = came_ref[:rows, :]
    for m, ref in enumerate(near_refs, 1):
        part = slice(m * rows, (m + 1) * rows)
        ref[:, :columns] = total
        ref[:, columns : columns + width] = visual_ref[part, :]
        ref[:, columns + width :] = came_ref[part, :]


def add_far(near, far, visual_near, visual_came):
    rows, columns = far.shape
    width = visual_near.shape[1]
    shapes = [(far.shape, BF16)] * 2 + [((2 * rows, width), BF16)]
    shapes += [((rows, columns + 2 * width), BF16)] * (visual_near.shape[0] // rows - 1)
    out = in_vmem(add_kernel, "key_grad", shapes, near, far, visual_near, visual_came)
    return out[0], out[1], out[2], out[3:]


def onward_kernel(far_ref, *refs):
    value_refs, out_refs = refs[: len(refs) // 2], refs[len(refs) // 2 :]
    rows, columns = far_ref.shape
    for value_ref, ref in zip(value_refs, out_refs):
        ref[:, :columns] = far_ref[...]
        ref[:, columns : 2 * columns] = value_ref[:rows, :]
        ref[:, 2 * columns :] = value_ref[rows:, :]


def onward(far, values):
    shape = (far.shape[0], 3 * far.shape[1])
    return in_vmem(onward_kernel, "onward", [(shape, BF16)] * len(values), far, *values)


def add_value_kernel(near_ref, far_ref, out_ref):
    out_ref[...] = (near_ref[...] + far_ref[...].astype(F32)).astype(BF16)


def turn_kernel(columns, own_ref, *refs):
    came_refs, out_ref = refs[:-1], refs[-1]
    rows, width = own_ref.shape[0] // 2, own_ref.shape[1]
    parts = []
    for side in range(2):
        parts.append(own_ref[side * rows : (side + 1) * rows, :])
        first = columns + side * width
        parts += [ref[:, first : first + width] for ref in came_refs]
    out_ref[...] = jnp.concatenate(parts, axis=0).T


def turn(columns, own, came):
    rows, width = own.shape
    shape = (width, (1 + len(came)) * rows)
    kernel = functools.partial(turn_kernel, columns)
    return in_vmem(kernel, "turn_visual", [(shape, BF16)], own, *came)[0]


def weight_kernel(order, visual_ref, value_ref, *refs):
    pieces = len(order)
    kg_refs = [refs[order.index(m)] for m in range(pieces)]
    keep_ref, send_ref, near_ref, far_ref = refs[pieces:]
    rows, width = near_ref.shape
    product = dot(visual_ref[...], jnp.concatenate([r[:, :width] for r in kg_refs], axis=0))
    count, share, _ = keep_ref.shape
    core = lax.axis_index("dp") % 2 == 0
    for n in range(count):
        even = product[2 * n * share : (2 * n + 1) * share]
        odd = product[(2 * n + 1) * share : (2 * n + 2) * share]
        keep_ref[n] = jnp.where(core, even, odd)
        send_ref[n] = jnp.where(core, odd, even).astype(BF16)
    for side, ref in enumerate((near_ref, far_ref)):
        total = value_ref[side * rows : (side + 1) * rows, :]
        for kg_ref in kg_refs[pieces // 2 + 1 :]:
            total += kg_ref[:, (1 + side) * width : (2 + side) * width].astype(F32)
        ref[...] = total.astype(ref.dtype)


def weight_terms(samples, visual, value_own, key_grads):
    rows, width = key_grads[0].shape
    middle = len(key_grads) // 2
    order = [0, *range(2 * middle - 1, middle, -1), *range(middle - 1, 0, -1), middle]
    half = ((samples // 2, visual.shape[0] // samples, width), F32)
    shapes = [half, (half[0], BF16), ((rows, width), F32), ((rows, width), BF16)]
    kernel = functools.partial(weight_kernel, order)
    ordered = [key_grads[m] for m in order]
    return in_vmem(kernel, "weight_terms", shapes, visual, value_own, *ordered)


def halve_kernel(bit, kept_ref, came_ref, keep_ref, send_ref):
    low = (lax.axis_index("dp") >> bit) % 2 == 0
    for n in range(keep_ref.shape[0]):
        even = kept_ref[2 * n] + came_ref[2 * n].astype(F32)
        odd = kept_ref[2 * n + 1] + came_ref[2 * n + 1].astype(F32)
        keep_ref[n] = jnp.where(low, even, odd)
        send_ref[n] = jnp.where(low, odd, even).astype(BF16)


def halve(bit, kept, came):
    half = (kept.shape[0] // 2, *kept.shape[1:])
    kernel = functools.partial(halve_kernel, bit)
    return in_vmem(kernel, "halve", [(half, F32), (half, BF16)], kept, came)


def local(visual_rows, value_matrix, key_weight, queries, output_gradient, visual_len, frame_end):
    tie = lax.optimization_barrier
    blocks, samples = lax.axis_size("blk"), lax.axis_size("dp")
    visual, half = visual_rows[0], blocks // 2

    own, visual_near, visual_far = project(blocks, visual, key_weight, value_matrix[0])
    keys_values = gather(own)
    visual_far = swap(visual_far, "blk", half)
    attention = Attention(queries[0], blocks, visual.shape[0])
    inner, key_own, key_near = attention.scores(
        visual_len, frame_end, queries[0], output_gradient[0], keys_values
    )
    weights, dscores, keys, values = inner

    key_near = near_exchange(key_near)
    value_own, value_near = attention.values(output_gradient[0], weights)
    key_own, value_own, visual_far = tie((key_own, value_own, visual_far))
    key_sum, key_far = near_sums(key_own, key_near[::-1], "key_sums")
    key_sum, dscores = tie((key_sum, dscores))
    key_far = swap(key_far, "blk", half)
    query_grad = attention.over_rows(dscores, keys, "query_grad", HEAD_SIZE**-0.5)
    key_sum, query_grad = tie((key_sum, query_grad))
    key_grad, key_again, visual_own, near = add_far(key_sum, key_far, visual_near, visual_far)

    key_grads = gather(key_grad, near, lambda far: onward(far, value_near))
    key_grads[0] = key_again
    attn_out = attention.over_rows(weights, values, "output")
    visual_columns = turn(key_grad.shape[1], visual_own, key_grads[1:half])
    visual_columns, attn_out = tie((visual_columns, attn_out))
    kept, sent, value_sum, value_far = weight_terms(samples, visual_columns, value_own, key_grads)
    value_far = swap(value_far, "blk", half)
    came, bit = swap(sent, "dp", 1), 1
    while kept.shape[0] > 1:
        kept, sent = halve(bit, kept, came)
        came, bit = swap(sent, "dp", 1 << bit), bit + 1
    shape = [(value_far.shape, BF16)]
    cost = pl.CostEstimate(flops=4 * 10**9, bytes_accessed=2**24, transcendentals=0)
    value_grad = in_vmem(
        add_value_kernel, "value_grad", shape, value_sum, value_far, cost=cost
    )[0]
    came, value_grad = tie((came, value_grad))
    weight_grad = kept[0] + came[0].astype(F32)
    return attn_out[None], query_grad[None], value_grad[None], weight_grad


def solution(mesh):
    return jax.shard_map(
        local,
        mesh=mesh,
        in_specs=(
            P("dp", "blk", None),
            P("dp", "blk", None),
            P(),
            P("dp", "blk", None),
            P("dp", "blk", None),
            P("dp"),
            P("dp", None),
        ),
        out_specs=(
            P("dp", "blk", None),
            P("dp", "blk", None),
            P("dp", "blk", None),
            P(("blk", "dp"), None),
        ),
        check_vma=False,
    )
```

```python
import functools

import jax
import jax.numpy as jnp
from jax import lax
from jax.experimental import pallas as pl
from jax.experimental.pallas import tpu as pltpu
from jax.sharding import PartitionSpec as P

KEY_HEADS = 4
HEAD_SIZE = 128
TILE = 128
HEADS_PER_KEY = 8
LOG2_E = 1.4426950408889634
NEGATIVE_FILLER = -1e30
F32 = jnp.float32
BF16 = jnp.bfloat16
MIB = 1024 * 1024
VMEM = pl.BlockSpec(memory_space=pltpu.VMEM)


def dot(a, b, contract=((1,), (0,))):
    return lax.dot_general(a, b, (contract, ((), ())), preferred_element_type=F32)


def swap(x, axis, mask):
    size = lax.axis_size(axis)
    return lax.ppermute(x, axis, [(i, i ^ mask) for i in range(size)])


def in_hbm(x):
    return pltpu.with_memory_space_constraint(x, pltpu.HBM)


def gather(own, near=None, onward=None):
    blocks = lax.axis_size("blk")
    half = blocks // 2
    masks = range(half - 1, 0, -1)
    far = swap(own, "blk", half)
    pieces = {0: own, half: far}
    pieces.update({m: swap(near[m - 1] if near else own, "blk", m) for m in masks})
    sent = onward(far) if onward else [far] * (half - 1)
    pieces.update({m + half: swap(sent[m - 1], "blk", m) for m in masks})
    return [pieces[m] for m in range(blocks)]


def near_exchange(pieces):
    return [swap(piece, "blk", m) for m, piece in enumerate(pieces, 1)]


def project_kernel(chunks, weight_hbm, visual_hbm, value_hbm, *refs):
    out_ref, near_ref, far_ref, weight, visual_ref, value_ref, sems = refs
    slab = weight.shape[0] // chunks
    copies = [
        pltpu.make_async_copy(visual_hbm, visual_ref, sems.at[chunks]),
        pltpu.make_async_copy(value_hbm, value_ref, sems.at[chunks + 1]),
    ]
    for c in range(chunks):
        part = pl.ds(c * slab, slab)
        copies.append(pltpu.make_async_copy(weight_hbm.at[part], weight.at[part], sems.at[c]))
    for copy in copies:
        copy.start()
    copies[0].wait()
    copies[1].wait()
    block = lax.axis_index("blk")
    rows, width = visual_ref.shape[0], near_ref.shape[1]
    half = near_ref.shape[0] // rows
    for side, ref in enumerate((near_ref, far_ref)):
        for m in range(half):
            start = pl.multiple_of((block ^ (m + side * half)) * width, HEAD_SIZE)
            ref[m * rows : (m + 1) * rows, :] = visual_ref[:, pl.ds(start, width)]
    columns = weight.shape[1]
    out_ref[:, columns:] = value_ref[...]
    keys = jnp.zeros((rows, columns), F32)
    for c in range(chunks):
        copies[2 + c].wait()
        part = slice(c * slab, (c + 1) * slab)
        keys += dot(visual_ref[:, part], weight[part, :])
    out_ref[:, :columns] = keys.astype(BF16)


def project(blocks, visual, key_weight, value):
    rows, features = visual.shape
    columns = key_weight.shape[1]
    chunks = 4
    half = (blocks // 2 * rows, features // blocks)
    shapes = [(rows, columns + value.shape[1]), half, half]
    return pl.pallas_call(
        functools.partial(project_kernel, chunks),
        in_specs=[pl.BlockSpec(memory_space=pltpu.HBM)] * 3,
        out_specs=[VMEM] * 3,
        out_shape=[jax.ShapeDtypeStruct(shape, BF16) for shape in shapes],
        scratch_shapes=[
            pltpu.VMEM(key_weight.shape, BF16),
            pltpu.VMEM(visual.shape, BF16),
            pltpu.VMEM(value.shape, BF16),
            pltpu.SemaphoreType.DMA((chunks + 2,)),
        ],
        cost_estimate=pl.CostEstimate(
            flops=2 * rows * features * columns,
            bytes_accessed=2 * features * columns,
            transcendentals=0,
        ),
        compiler_params=pltpu.CompilerParams(vmem_limit_bytes=32 * MIB),
        name="project",
    )(in_hbm(key_weight), in_hbm(visual), in_hbm(value))


def head_pair(ref, rows, start):
    first = pl.ds(pl.multiple_of(start, HEAD_SIZE), HEAD_SIZE)
    second = pl.ds(pl.multiple_of(start + HEAD_SIZE, HEAD_SIZE), HEAD_SIZE)
    return jnp.concatenate([ref[rows, first], ref[rows, second]], axis=0)


def store_sides(own_ref, near_refs, terms, columns):
    half = len(near_refs) + 1
    rows = own_ref.shape[0] // 2
    for m, ref in enumerate((own_ref, *near_refs)):
        for side in range(2):
            first = (m + side * half) * rows
            part = terms[first : first + rows, :].astype(ref.dtype)
            ref[side * rows : (side + 1) * rows, columns] = part


def scores_kernel(pieces, length_ref, frame_ref, q_ref, g_ref, *refs):
    kv_refs, (w_ref, ds_ref, k_ref, v_ref) = refs[:pieces], refs[pieces : pieces + 4]
    kv_refs = (kv_refs[0], *kv_refs[:0:-1])
    own_ref, near_refs, (kg_acc, bias_ref) = refs[pieces + 4], refs[pieces + 5 : -2], refs[-2:]
    block = lax.axis_index("blk")
    tiles = q_ref.shape[0] // TILE
    rows = kv_refs[0].shape[0]
    width = KEY_HEADS * HEAD_SIZE
    pair = 2 * TILE
    pairs = HEADS_PER_KEY // 2
    span = HEADS_PER_KEY * HEAD_SIZE
    scale = HEAD_SIZE**-0.5
    for m in range(pieces):
        part = slice(m * rows, (m + 1) * rows)
        k_ref[part, :] = kv_refs[m][:, :width]
        v_ref[part, :] = kv_refs[m][:, width:]
    row = lax.broadcasted_iota(jnp.int32, (rows, pair), 0)
    for i in range(tiles):
        text = slice(i * TILE, (i + 1) * TILE)
        limit = jnp.minimum(length_ref[0], TILE * frame_ref[0, block * tiles + i])
        for m in range(pieces):
            live = row + (block ^ m) * rows < limit
            bias_ref[m * rows : (m + 1) * rows, :] = jnp.where(live, 0.0, NEGATIVE_FILLER)

        @pl.loop(0, KEY_HEADS, unroll=True)
        def _(j, i=i, text=text):
            head = pl.ds(pl.multiple_of(j * HEAD_SIZE, HEAD_SIZE), HEAD_SIZE)
            keys, values = k_ref[:, head], v_ref[:, head]
            q_stack, raw, dprobs = [], {}, {}

            def products(p):
                start = j * span + p * pair
                q_stack.append(head_pair(q_ref, text, start))
                raw[p] = dot(keys, q_stack[p], ((1,), (1,)))
                dprobs[p] = dot(values, head_pair(g_ref, text, start), ((1,), (1,)))

            products(0)
            products(1)
            ds_stack = []
            for p in range(pairs):
                if p + 2 < pairs:
                    products(p + 2)
                scores = raw.pop(p) + bias_ref[...]
                peak = jnp.max(scores, axis=0, keepdims=True)
                shifted = jnp.exp2((scores - peak) * (scale * LOG2_E))
                inverse = 1.0 / jnp.sum(shifted, axis=0, keepdims=True)
                change = dprobs.pop(p)
                delta = jnp.sum(shifted * change, axis=0, keepdims=True) * inverse
                probs = shifted * inverse
                start = (i * KEY_HEADS + j) * span + p * pair
                both = pl.ds(pl.multiple_of(start, HEAD_SIZE), pair)
                w_ref[:, both] = probs.astype(BF16)
                ds_stack.append((probs * (change - delta)).astype(BF16))
                ds_ref[:, both] = ds_stack[p]
            kg = dot(jnp.concatenate(ds_stack, axis=1), jnp.concatenate(q_stack, axis=0)) * scale
            if i == 0:
                kg_acc[:, head] = kg
            else:
                kg_acc[:, head] += kg

    store_sides(own_ref, near_refs, kg_acc, slice(None))


def values_kernel(pieces, g_ref, w_ref, own_ref, *near_refs):
    span = HEADS_PER_KEY * HEAD_SIZE
    for j in range(KEY_HEADS):
        total = 0.0
        for i in range(g_ref.shape[0] // TILE):
            text = slice(i * TILE, (i + 1) * TILE)
            starts = range(j * span, (j + 1) * span, HEAD_SIZE)
            stack = [g_ref[text, start : start + HEAD_SIZE] for start in starts]
            first = (i * KEY_HEADS + j) * span
            total += dot(w_ref[:, first : first + span], jnp.concatenate(stack, axis=0))
        store_sides(own_ref, near_refs, total, slice(j * HEAD_SIZE, (j + 1) * HEAD_SIZE))


def rows_kernel(factor, pieces, inner_ref, head_ref, out_ref):
    left = head_ref[...].T
    pair = 2 * TILE
    for p in range(HEADS_PER_KEY // 2):
        out = dot(left, inner_ref[:, p * pair : (p + 1) * pair])
        if factor is not None:
            out *= factor
        out = out.T.astype(BF16)
        out_ref[:, p * pair : p * pair + HEAD_SIZE] = out[:TILE]
        out_ref[:, p * pair + HEAD_SIZE : (p + 1) * pair] = out[TILE:]


class Attention:
    def __init__(self, queries, pieces, rows):
        self.pieces, self.rows = pieces, rows
        self.text, self.wide = queries.shape
        self.tiles = self.text // TILE
        self.all_rows = pieces * rows
        self.width = KEY_HEADS * HEAD_SIZE
        span = HEADS_PER_KEY * HEAD_SIZE
        self.text_block = pl.BlockSpec((TILE, span), lambda j, i: (i, j))
        self.inner_block = pl.BlockSpec((self.all_rows, span), lambda j, i: (0, i * KEY_HEADS + j))
        self.head_block = pl.BlockSpec((self.all_rows, HEAD_SIZE), lambda j, i: (0, j))
        self.inner = jax.ShapeDtypeStruct((self.all_rows, self.tiles * self.wide), BF16)
        self.sides = (2 * rows, self.width)
        self.terms = [jax.ShapeDtypeStruct(self.sides, F32)]
        self.terms += [jax.ShapeDtypeStruct(self.sides, BF16)] * (pieces // 2 - 1)

    def call(self, kernel, share, name, **specs):
        return pl.pallas_call(
            functools.partial(kernel, self.pieces),
            cost_estimate=pl.CostEstimate(
                flops=int(share * 12 * self.text * self.all_rows * self.wide),
                bytes_accessed=int(share * 8 * self.text * self.wide),
                transcendentals=0,
            ),
            compiler_params=pltpu.CompilerParams(vmem_limit_bytes=32 * MIB),
            name=name,
            **specs,
        )

    def scores(self, length, frames, queries, gradients, keys_values):
        smem = pl.BlockSpec(memory_space=pltpu.SMEM)
        heads = jax.ShapeDtypeStruct((self.all_rows, self.width), BF16)
        out = self.call(
            scores_kernel,
            1.0,
            "scores",
            in_specs=[smem, smem, VMEM, VMEM] + [VMEM] * self.pieces,
            out_specs=[VMEM] * (4 + len(self.terms)),
            out_shape=[self.inner] * 2 + [heads] * 2 + self.terms,
            scratch_shapes=[
                pltpu.VMEM((self.all_rows, self.width), F32),
                pltpu.VMEM((self.all_rows, 2 * TILE), F32),
            ],
        )(length, frames, queries, gradients, keys_values[0], *keys_values[:0:-1])
        return out[:4], out[4], out[5:]

    def values(self, gradients, weights):
        out = self.call(
            values_kernel,
            0.1,
            "values",
            in_specs=[VMEM] * 2,
            out_specs=[VMEM] * len(self.terms),
            out_shape=self.terms,
        )(gradients, weights)
        return out[0], out[1:]

    def over_rows(self, inner, heads, name, factor=None):
        return self.call(
            functools.partial(rows_kernel, factor),
            0.1,
            name,
            grid=(KEY_HEADS, self.tiles),
            in_specs=[self.inner_block, self.head_block],
            out_specs=self.text_block,
            out_shape=jax.ShapeDtypeStruct((self.text, self.wide), BF16),
        )(inner, heads)


def in_vmem(kernel, name, out_shape, *arrays, cost=None):
    return pl.pallas_call(
        kernel,
        cost_estimate=cost,
        in_specs=[VMEM] * len(arrays),
        out_specs=[VMEM] * len(out_shape),
        out_shape=[jax.ShapeDtypeStruct(*shape) for shape in out_shape],
        compiler_params=pltpu.CompilerParams(vmem_limit_bytes=32 * MIB),
        name=name,
    )(*arrays)


def sum_kernel(own_ref, *refs):
    came_refs, (near_ref, far_ref) = refs[:-2], refs[-2:]
    rows = near_ref.shape[0]
    for ref, part in ((near_ref, slice(0, rows)), (far_ref, slice(rows, 2 * rows))):
        total = own_ref[part, :]
        for came_ref in came_refs:
            total += came_ref[part, :].astype(F32)
        ref[...] = total.astype(ref.dtype)


def near_sums(own, came, name):
    half = (own.shape[0] // 2, own.shape[1])
    return in_vmem(sum_kernel, name, [(half, F32), (half, BF16)], own, *came)


def add_kernel(near_ref, far_ref, visual_ref, came_ref, own_ref, again_ref, sides_ref, *near_refs):
    rows, columns = own_ref.shape
    width = visual_ref.shape[1]
    total = (near_ref[...] + far_ref[...].astype(F32)).astype(BF16)
    own_ref[...] = total
    again_ref[...] = total
    sides_ref[:rows, :] = visual_ref[:rows, :]
    sides_ref[rows:, :] = came_ref[:rows, :]
    for m, ref in enumerate(near_refs, 1):
        part = slice(m * rows, (m + 1) * rows)
        ref[:, :columns] = total
        ref[:, columns : columns + width] = visual_ref[part, :]
        ref[:, columns + width :] = came_ref[part, :]


def add_far(near, far, visual_near, visual_came):
    rows, columns = far.shape
    width = visual_near.shape[1]
    shapes = [(far.shape, BF16)] * 2 + [((2 * rows, width), BF16)]
    shapes += [((rows, columns + 2 * width), BF16)] * (visual_near.shape[0] // rows - 1)
    out = in_vmem(add_kernel, "key_grad", shapes, near, far, visual_near, visual_came)
    return out[0], out[1], out[2], out[3:]


def onward_kernel(far_ref, *refs):
    value_refs, out_refs = refs[: len(refs) // 2], refs[len(refs) // 2 :]
    rows, columns = far_ref.shape
    for value_ref, ref in zip(value_refs, out_refs):
        ref[:, :columns] = far_ref[...]
        ref[:, columns : 2 * columns] = value_ref[:rows, :]
        ref[:, 2 * columns :] = value_ref[rows:, :]


def onward(far, values):
    shape = (far.shape[0], 3 * far.shape[1])
    return in_vmem(onward_kernel, "onward", [(shape, BF16)] * len(values), far, *values)


def add_value_kernel(near_ref, far_ref, out_ref):
    out_ref[...] = (near_ref[...] + far_ref[...].astype(F32)).astype(BF16)


def turn_kernel(columns, own_ref, *refs):
    came_refs, out_ref = refs[:-1], refs[-1]
    rows, width = own_ref.shape[0] // 2, own_ref.shape[1]
    parts = []
    for side in range(2):
        parts.append(own_ref[side * rows : (side + 1) * rows, :])
        first = columns + side * width
        parts += [ref[:, first : first + width] for ref in came_refs]
    out_ref[...] = jnp.concatenate(parts, axis=0).T


def turn(columns, own, came):
    rows, width = own.shape
    shape = (width, (1 + len(came)) * rows)
    kernel = functools.partial(turn_kernel, columns)
    return in_vmem(kernel, "turn_visual", [(shape, BF16)], own, *came)[0]


def weight_kernel(order, visual_ref, value_ref, *refs):
    pieces = len(order)
    kg_refs = [refs[order.index(m)] for m in range(pieces)]
    keep_ref, send_ref, near_ref, far_ref = refs[pieces:]
    rows, width = near_ref.shape
    product = dot(visual_ref[...], jnp.concatenate([r[:, :width] for r in kg_refs], axis=0))
    count, share, _ = keep_ref.shape
    core = lax.axis_index("dp") % 2 == 0
    for n in range(count):
        even = product[2 * n * share : (2 * n + 1) * share]
        odd = product[(2 * n + 1) * share : (2 * n + 2) * share]
        keep_ref[n] = jnp.where(core, even, odd)
        send_ref[n] = jnp.where(core, odd, even).astype(BF16)
    for side, ref in enumerate((near_ref, far_ref)):
        total = value_ref[side * rows : (side + 1) * rows, :]
        for kg_ref in kg_refs[pieces // 2 + 1 :]:
            total += kg_ref[:, (1 + side) * width : (2 + side) * width].astype(F32)
        ref[...] = total.astype(ref.dtype)


def weight_terms(samples, visual, value_own, key_grads):
    rows, width = key_grads[0].shape
    middle = len(key_grads) // 2
    order = [0, *range(2 * middle - 1, middle, -1), *range(middle - 1, 0, -1), middle]
    half = ((samples // 2, visual.shape[0] // samples, width), F32)
    shapes = [half, (half[0], BF16), ((rows, width), F32), ((rows, width), BF16)]
    kernel = functools.partial(weight_kernel, order)
    ordered = [key_grads[m] for m in order]
    return in_vmem(kernel, "weight_terms", shapes, visual, value_own, *ordered)


def halve_kernel(bit, kept_ref, came_ref, keep_ref, send_ref):
    low = (lax.axis_index("dp") >> bit) % 2 == 0
    for n in range(keep_ref.shape[0]):
        even = kept_ref[2 * n] + came_ref[2 * n].astype(F32)
        odd = kept_ref[2 * n + 1] + came_ref[2 * n + 1].astype(F32)
        keep_ref[n] = jnp.where(low, even, odd)
        send_ref[n] = jnp.where(low, odd, even).astype(BF16)


def halve(bit, kept, came):
    half = (kept.shape[0] // 2, *kept.shape[1:])
    kernel = functools.partial(halve_kernel, bit)
    return in_vmem(kernel, "halve", [(half, F32), (half, BF16)], kept, came)


def local(visual_rows, value_matrix, key_weight, queries, output_gradient, visual_len, frame_end):
    tie = lax.optimization_barrier
    blocks, samples = lax.axis_size("blk"), lax.axis_size("dp")
    visual, half = visual_rows[0], blocks // 2

    own, visual_near, visual_far = project(blocks, visual, key_weight, value_matrix[0])
    keys_values = gather(own)
    visual_far = swap(visual_far, "blk", half)
    attention = Attention(queries[0], blocks, visual.shape[0])
    inner, key_own, key_near = attention.scores(
        visual_len, frame_end, queries[0], output_gradient[0], keys_values
    )
    weights, dscores, keys, values = inner

    key_near = near_exchange(key_near)
    value_own, value_near = attention.values(output_gradient[0], weights)
    key_own, value_own, visual_far = tie((key_own, value_own, visual_far))
    key_sum, key_far = near_sums(key_own, key_near[::-1], "key_sums")
    key_sum, dscores = tie((key_sum, dscores))
    key_far = swap(key_far, "blk", half)
    query_grad = attention.over_rows(dscores, keys, "query_grad", HEAD_SIZE**-0.5)
    key_sum, query_grad = tie((key_sum, query_grad))
    key_grad, key_again, visual_own, near = add_far(key_sum, key_far, visual_near, visual_far)

    key_grads = gather(key_grad, near, lambda far: onward(far, value_near))
    key_grads[0] = key_again
    attn_out = attention.over_rows(weights, values, "output")
    visual_columns = turn(key_grad.shape[1], visual_own, key_grads[1:half])
    visual_columns, attn_out = tie((visual_columns, attn_out))
    kept, sent, value_sum, value_far = weight_terms(samples, visual_columns, value_own, key_grads)
    value_far = swap(value_far, "blk", half)
    came, bit = swap(sent, "dp", 1), 1
    while kept.shape[0] > 1:
        kept, sent = halve(bit, kept, came)
        came, bit = swap(sent, "dp", 1 << bit), bit + 1
    shape = [(value_far.shape, BF16)]
    cost = pl.CostEstimate(flops=4 * 10**9, bytes_accessed=2**24, transcendentals=0)
    value_grad = in_vmem(
        add_value_kernel, "value_grad", shape, value_sum, value_far, cost=cost
    )[0]
    came, value_grad = tie((came, value_grad))
    weight_grad = kept[0] + came[0].astype(F32)
    return attn_out[None], query_grad[None], value_grad[None], weight_grad


def solution(mesh):
    return jax.shard_map(
        local,
        mesh=mesh,
        in_specs=(
            P("dp", "blk", None),
            P("dp", "blk", None),
            P(),
            P("dp", "blk", None),
            P("dp", "blk", None),
            P("dp"),
            P("dp", None),
        ),
        out_specs=(
            P("dp", "blk", None),
            P("dp", "blk", None),
            P("dp", "blk", None),
            P(("blk", "dp"), None),
        ),
        check_vma=False,
    )
```
